128 devices in a mesh: ctx: 16 (over x, y_lo, core), enc: 8 (over z, y_hi).
Axes of the slice: x: 4, y: 4 (y_hi: 2, y_lo: 2; y = y_hi * 2 + y_lo), z: 4, core: 2. Of those that a mesh axis runs over, the one named last changes fastest.
Arguments:
- self_q: bfloat16 [4096, 4096], P('ctx', 'enc')
- self_k: bfloat16 [4096, 4096], P('ctx', 'enc')
- self_v: bfloat16 [4096, 4096], P('ctx', 'enc'), may hold values from -6 to 6
- cross_q: bfloat16 [4096, 4096], P('ctx', 'enc'), may hold values from -6 to 6
- cross_k_weight: bfloat16 [896, 4096], P(None, 'enc'), may hold values from -0.1875 to 0.1875
- cross_v_weight: bfloat16 [896, 4096], P(None, 'enc'), may hold values from -0.1875 to 0.1875
- span_ctx: bfloat16 [4096, 896], P('ctx'), may hold values from -6 to 6
- neighbours: bfloat16 [256, 128, 896], P(('ctx', 'enc')), may hold values from -6 to 6
- neighbour_ids: int32 [64, 2], P('ctx'), may hold values from 0 to 15, as said below
- enc_q: bfloat16 [896, 896], replicated, may hold values from -0.1875 to 0.1875
- enc_k: bfloat16 [896, 896], replicated, may hold values from -0.1875 to 0.1875
- enc_v: bfloat16 [896, 896], replicated, may hold values from -0.1875 to 0.1875
- enc_o: bfloat16 [896, 896], replicated, may hold values from -0.1875 to 0.1875
- mixed_grad: bfloat16 [4096, 4096], P('ctx', 'enc'), may hold values from -6 to 6
Outputs:
- mixed: bfloat16 [4096, 4096], P('ctx', 'enc')
- neighbour_grad: float32 [256, 128, 896], P(('ctx', 'enc'))
The draws below stay inside these ranges and needn't reach their ends.
Inputs may be any that keep to these rules, and one draw needn't show every extreme that they name: `neighbour_ids`: within the 4 spans of one ctx index the 8 values are distinct slots; slot g of that index is held by enc index g // 2; in every such group some enc index has all of its 2 slots named.
All inputs are finite; a program needn't handle non-finite values.
Results may differ from the reference program's by a relative error of at most 0.025.
Values may be sent and summed in bfloat16 or wider, within the bound.
No kernel may reach another device: no remote copies, remote signals or barrier semaphores. Data moves between devices by JAX's collectives and lax.ppermute only.
A program may use at most 128 MiB of HBM per device.

```python
import math
import jax
import jax.numpy as jnp
from jax import lax

HEADS = 32
HSIZE = 128
EW = 896
EHEADS = 4
CL = 64
NL = 128
TOKENS = 4096
CH_DEV = 4
SPANS = 64
BLK_DEV = 2
NBLOCKS = 256
N_CTX = 16
N_ENC = 8


def draw_self_q(key, part):
    key = jax.random.fold_in(key, 11)
    values = jax.random.normal(key, (TOKENS, HEADS * HSIZE), jnp.float32)
    values = jnp.clip(values, -6.0, 6.0)
    return values.astype(jnp.bfloat16)


def draw_self_k(key, part):
    key = jax.random.fold_in(key, 13)
    values = jax.random.normal(key, (TOKENS, HEADS * HSIZE), jnp.float32)
    values = jnp.clip(values, -6.0, 6.0)
    return values.astype(jnp.bfloat16)


def draw_neighbour_ids(key, part):
    key = jax.random.fold_in(key, 23)
    slots_row = N_ENC * BLK_DEV
    wanted = 2 * CH_DEV

    def one_row(row_key):
        owners_key, jitter_key, shuffle_key = jax.random.split(row_key, 3)
        owner_score = jax.random.randint(owners_key, (N_ENC,), 0, 1 << 20) * N_ENC + jnp.arange(N_ENC)
        owner_rank = jnp.argsort(jnp.argsort(owner_score))
        slot_rank = owner_rank[jnp.arange(slots_row) // BLK_DEV]
        jitter = jax.random.randint(jitter_key, (slots_row,), 0, 2 * N_ENC)
        scores = jnp.where(slot_rank == 0, -1, jitter + slot_rank)
        scores = scores * slots_row + jnp.arange(slots_row)
        chosen = jnp.argsort(scores)[:wanted]
        shuffle = jax.random.permutation(shuffle_key, wanted)
        return chosen[shuffle].reshape(CH_DEV, 2)
    row_keys = jax.random.split(key, N_CTX)
    return jax.vmap(one_row)(row_keys).reshape(SPANS, 2).astype(jnp.int32)


def steps_of(stream_key, dims, shards, low, largest):
    def one(axis_at, parts):
        heights = jax.random.uniform(jax.random.fold_in(jax.random.fold_in(stream_key, 6), axis_at), (parts,), jnp.float32, low / len(shards), largest / len(shards))
        return jnp.repeat(jnp.exp(heights), dims[axis_at] // parts).reshape((-1,) + (1,) * (len(dims) - axis_at - 1))

    level = one(*shards[0])
    for cut in shards[1:]:
        level = level * one(*cut)
    return level


def centred(own_key, dims, width, most, cuts=(), kind=jnp.bfloat16):
    factor_of = steps_of(own_key, dims, cuts, -0.22, 0.18) if cuts else 1.0
    result = jax.random.normal(own_key, dims, jnp.float32) * width * factor_of
    return jnp.minimum(jnp.maximum(result, -most), most).astype(kind)


def setup_inputs(seed: int = 0) -> dict:
    keys = jax.random.split(jax.random.key(seed), 15)
    return {
        "self_q": draw_self_q(jax.random.fold_in(keys[14], 71), 0),
        "self_k": draw_self_k(jax.random.fold_in(keys[14], 71), 0),
        "self_v": centred(keys[2], (TOKENS, HEADS * HSIZE), 1.0, 6.0, ((0, 16), (1, 8))),
        "cross_q": centred(keys[3], (TOKENS, HEADS * HSIZE), 1.0, 6.0, ((0, 16), (1, 8))),
        "cross_k_weight": centred(keys[4], (EW, HEADS * HSIZE), EW ** -0.5, 0.1875, ((1, 8),)),
        "cross_v_weight": centred(keys[5], (EW, HEADS * HSIZE), EW ** -0.5, 0.1875, ((1, 8),)),
        "span_ctx": centred(keys[6], (TOKENS, EW), 1.0, 6.0, ((0, 16),)),
        "neighbours": centred(keys[7], (NBLOCKS, NL, EW), 1.0, 6.0, ((0, 128),)),
        "neighbour_ids": draw_neighbour_ids(jax.random.fold_in(keys[14], 71), 0),
        "enc_q": centred(keys[9], (EW, EW), EW ** -0.5, 0.1875),
        "enc_k": centred(keys[10], (EW, EW), EW ** -0.5, 0.1875),
        "enc_v": centred(keys[11], (EW, EW), EW ** -0.5, 0.1875),
        "enc_o": centred(keys[12], (EW, EW), EW ** -0.5, 0.1875),
        "mixed_grad": centred(keys[13], (TOKENS, HEADS * HSIZE), 1.0, 6.0, ((0, 16), (1, 8))),
    }


def encode(inputs, context, enc_q, enc_k, enc_v, enc_o):
    rows_in = inputs.shape[0]
    width_enc = inputs.shape[1]
    head_width = width_enc // EHEADS
    as_half = inputs.astype(jnp.bfloat16)
    queries = jnp.dot(as_half, enc_q, preferred_element_type=jnp.float32).astype(jnp.bfloat16)
    keys_enc = jnp.dot(context, enc_k, preferred_element_type=jnp.float32).astype(jnp.bfloat16)
    values_enc = jnp.dot(context, enc_v, preferred_element_type=jnp.float32).astype(jnp.bfloat16)
    q_heads = queries.reshape(rows_in, EHEADS, head_width).astype(jnp.float32)
    k_heads = keys_enc.reshape(-1, EHEADS, head_width).astype(jnp.float32)
    v_heads = values_enc.reshape(-1, EHEADS, head_width).astype(jnp.float32)
    scores = jnp.einsum('qhd,khd->hqk', q_heads, k_heads) / math.sqrt(head_width)
    weights = jax.nn.softmax(scores, axis=-1).astype(jnp.bfloat16).astype(jnp.float32)
    mixed_heads = jnp.einsum('hqk,khd->qhd', weights, v_heads).reshape(rows_in, width_enc).astype(jnp.bfloat16)
    return inputs + jnp.dot(mixed_heads, enc_o, preferred_element_type=jnp.float32)

def self_head(tensors):
    q_head, k_head, v_head = tensors
    scores = jnp.dot(q_head, k_head.T, preferred_element_type=jnp.float32) / math.sqrt(HSIZE)
    places = jnp.arange(TOKENS)
    visible = places[None, :] <= places[:, None]
    scores = jnp.where(visible, scores, -1e+30)
    row_top = lax.optimization_barrier(jnp.max(scores, axis=-1, keepdims=True))
    weights = jnp.where(visible, jnp.exp(scores - row_top), 0.0)
    total = lax.optimization_barrier(jnp.sum(weights, axis=-1, keepdims=True))
    return jnp.dot(weights.astype(jnp.bfloat16), v_head, preferred_element_type=jnp.float32) / total

def heads_first(array):
    return array.reshape(TOKENS, HEADS, HSIZE).transpose(1, 0, 2)

def reference(self_q, self_k, self_v, cross_q, cross_k_weight, cross_v_weight, span_ctx, neighbours, neighbour_ids, enc_q, enc_k, enc_v, enc_o, mixed_grad):
    full_width = HEADS * HSIZE
    width_per_group = full_width // N_ENC
    self_out = lax.map(self_head, (heads_first(self_q), heads_first(self_k), heads_first(self_v)))
    self_out = self_out.transpose(1, 0, 2).reshape(TOKENS, full_width)
    row_base = jnp.arange(SPANS, dtype=jnp.int32) // CH_DEV * (N_ENC * BLK_DEV)
    global_slot = (neighbour_ids + row_base[:, None]).astype(jnp.int32)
    inputs = neighbours[global_slot.reshape(-1)].reshape(SPANS, 2, NL, EW).astype(jnp.float32)
    contexts = span_ctx.reshape(SPANS, CL, EW)

    def encode_all(values_in):

        def per_span(pair, context):
            return jax.vmap(lambda single: encode(single, context, enc_q, enc_k, enc_v, enc_o))(pair)
        return jax.vmap(per_span)(values_in, contexts)
    encoded_f, pullback = jax.vjp(encode_all, inputs)
    encoded = encoded_f.astype(jnp.bfloat16).reshape(SPANS * 2 * NL, EW)
    cross_keys = jnp.dot(encoded, cross_k_weight, preferred_element_type=jnp.float32).astype(jnp.bfloat16)
    cross_vals = jnp.dot(encoded, cross_v_weight, preferred_element_type=jnp.float32).astype(jnp.bfloat16)
    keys_f = cross_keys.reshape(SPANS, 2 * NL, HEADS, HSIZE).astype(jnp.float32)
    vals_f = cross_vals.reshape(SPANS, 2 * NL, HEADS, HSIZE).astype(jnp.float32)
    query_f = cross_q.reshape(SPANS, CL, HEADS, HSIZE).astype(jnp.float32)
    scores = jnp.einsum('cqhd,ckhd->chqk', query_f, keys_f) / math.sqrt(HSIZE)
    probs = jax.nn.softmax(scores, axis=-1)
    probs_half = probs.astype(jnp.bfloat16).astype(jnp.float32)
    cross_out = jnp.einsum('chqk,ckhd->cqhd', probs_half, vals_f).reshape(TOKENS, full_width)
    mixed = (self_out + cross_out).astype(jnp.bfloat16)
    grad_f = mixed_grad.astype(jnp.float32).reshape(SPANS, CL, HEADS, HSIZE)
    grad_probs = jnp.einsum('cqhd,ckhd->chqk', grad_f, vals_f, precision=lax.Precision.HIGHEST)
    grad_scores = probs * (grad_probs - lax.optimization_barrier(jnp.sum(probs * grad_probs, axis=-1, keepdims=True)))
    grad_keys = (jnp.einsum('chqk,cqhd->ckhd', grad_scores, query_f, precision=lax.Precision.HIGHEST) / math.sqrt(HSIZE)).astype(jnp.bfloat16)
    grad_vals = jnp.einsum('chqk,cqhd->ckhd', probs_half, grad_f, precision=lax.Precision.HIGHEST).astype(jnp.bfloat16)
    rows_all = SPANS * 2 * NL
    grad_keys = grad_keys.reshape(rows_all, N_ENC, width_per_group).transpose(1, 0, 2)
    grad_vals = grad_vals.reshape(rows_all, N_ENC, width_per_group).transpose(1, 0, 2)
    key_groups = cross_k_weight.reshape(EW, N_ENC, width_per_group).transpose(1, 0, 2)
    val_groups = cross_v_weight.reshape(EW, N_ENC, width_per_group).transpose(1, 0, 2)

    def add_group(total, items):
        dk_group, dv_group, kw_group, vw_group = items
        term = jnp.dot(dk_group, kw_group.T, preferred_element_type=jnp.float32) + jnp.dot(dv_group, vw_group.T, preferred_element_type=jnp.float32)
        rounded = lax.optimization_barrier(term.astype(jnp.bfloat16))
        return (total + rounded.astype(jnp.float32), None)
    grad_enc, _ = lax.scan(add_group, jnp.zeros((rows_all, EW), jnp.float32), (grad_keys, grad_vals, key_groups, val_groups))
    grad_inputs = pullback(grad_enc.reshape(SPANS, 2, NL, EW))[0]
    neighbour_grad = jnp.zeros((NBLOCKS, NL, EW), jnp.float32).at[global_slot.reshape(-1)].add(grad_inputs.reshape(SPANS * 2, NL, EW))
    return (mixed, neighbour_grad)
```

```python
import math

import jax
import jax.numpy as jnp
from jax import lax
from jax.experimental import pallas as pl
from jax.experimental.pallas import tpu as pltpu
from jax.sharding import Mesh
from jax.sharding import PartitionSpec as P

HSIZE = 128
EHEADS = 4
CL = 64
NL = 128
NX = 4
LOG2E = math.log2(math.e)
BF16 = jnp.bfloat16
F32 = jnp.float32

NT = (((1,), (1,)), ((), ()))
TN = (((0,), (0,)), ((), ()))


def mm(a, b):
    return jnp.dot(a, b, preferred_element_type=F32)


def mm_nt(a, b):
    return lax.dot_general(a, b, NT, preferred_element_type=F32)


def mm_tn(a, b):
    return lax.dot_general(a, b, TN, preferred_element_type=F32)


def call(kernel, mib=32, **kw):
    return pl.pallas_call(
        kernel,
        compiler_params=pltpu.CompilerParams(vmem_limit_bytes=mib * 1024 * 1024),
        **kw,
    )


def smem():
    return pl.BlockSpec(memory_space=pltpu.SMEM)


def vmem():
    return pl.BlockSpec(memory_space=pltpu.VMEM)


def hbm():
    return pl.BlockSpec(memory_space=pl.ANY)


def pack_kernel(q_ref, k_ref, v_ref, o0, o1, o2, o3, sems):
    x = lax.axis_index("x")
    copies = []
    for d, out in enumerate((o0, o1, o2, o3)):
        cols = pl.ds(pl.multiple_of(lax.rem(x + d, NX) * HSIZE, HSIZE), HSIZE)
        for i, src in enumerate((q_ref, k_ref, v_ref)):
            copies.append(pltpu.make_async_copy(src.at[:, cols], out.at[i], sems.at[d, i]))
    for c in copies:
        c.start()
    for c in copies:
        c.wait()


def attend_kernel(q0, q1, q2, q3, kv, o0, o1, o2, o3, acc, top, total):
    x = lax.axis_index("x")
    r = lax.axis_index("yl") * 2 + lax.axis_index("core")
    scale = LOG2E / math.sqrt(HSIZE)
    for d, (q_ref, o_ref) in enumerate(zip((q0, q1, q2, q3), (o0, o1, o2, o3))):
        xq = lax.rem(x - d + NX, NX)
        q = q_ref[0]
        rows = q.shape[0]
        acc[...] = jnp.zeros_like(acc)
        top[...] = jnp.full_like(top, -1e30)
        total[...] = jnp.zeros_like(total)

        def group(xk, masked):
            dk = lax.rem(x - xk + NX, NX)
            scores = [mm_nt(q, kv[i, dk, 0]) for i in range(4)]
            if masked:
                at = lax.broadcasted_iota(jnp.int32, (rows, rows), 1)
                upto = lax.broadcasted_iota(jnp.int32, (rows, rows), 0)
                scores = [
                    jnp.where(at + i * rows <= upto + r * rows, s, -1e30)
                    for i, s in enumerate(scores)
                ]
            best = jnp.maximum(
                jnp.maximum(scores[0], scores[1]), jnp.maximum(scores[2], scores[3])
            )
            old = top[...]
            new = jnp.maximum(old, jnp.max(best, axis=-1, keepdims=True))
            fade = jnp.exp2((old - new) * scale)
            weights = [jnp.exp2((s - new) * scale) for s in scores]
            added = (weights[0] + weights[1]) + (weights[2] + weights[3])
            total[...] = total[...] * fade + jnp.sum(added, axis=-1, keepdims=True)
            out = mm(weights[0].astype(BF16), kv[0, dk, 1])
            for i in range(1, 4):
                out = out + mm(weights[i].astype(BF16), kv[i, dk, 1])
            acc[...] = acc[...] * fade + out
            top[...] = new

        def step(xk, carry):
            group(xk, False)
            return carry

        lax.fori_loop(0, xq, step, 0)
        group(xq, True)
        o_ref[...] = (acc[...] / total[...]).astype(BF16)


def mix_kernel(s0, s1, s2, s3, cross, out):
    x = lax.axis_index("x")
    for d, piece in enumerate((s0, s1, s2, s3)):
        cols = pl.ds(pl.multiple_of(lax.rem(x + d, NX) * HSIZE, HSIZE), HSIZE)
        out[:, cols] = (piece[...].astype(F32) + cross[:, cols]).astype(BF16)


def head_rows(rows):
    width = rows.shape[1]
    each = width // EHEADS
    at = lax.broadcasted_iota(jnp.int32, (1, width), 1)
    parts = []
    for h in range(EHEADS):
        keep = jnp.where((at >= h * each) & (at < (h + 1) * each), 1.0, 0.0).astype(BF16)
        parts.append(rows * keep)
    return jnp.concatenate(parts, axis=0)


def encode_kernel(
    ids, nb, ctx, wq_h, wk_h, wv_h, wo_h, enc, wt, ek_out, ev_out, wq, wk, wv, wo, sems
):
    copies = [
        pltpu.make_async_copy(a, b, sems.at[i])
        for i, (a, b) in enumerate(((wq_h, wq), (wk_h, wk), (wv_h, wv), (wo_h, wo)))
    ]
    for c in copies:
        c.start()
    slots, rows, width = nb.shape
    each = width // EHEADS
    x = nb[...].reshape(slots * rows, width)
    contexts = []
    for t in range(slots):
        mine = (lax.axis_index("z") * 2 + lax.axis_index("yh")) * slots + t
        span = jnp.int32(0)
        for c in range(1, ids.shape[0]):
            span = jnp.where((ids[c, 0] == mine) | (ids[c, 1] == mine), c, span)
        contexts.append(ctx[pl.ds(pl.multiple_of(span * CL, CL), CL), :])
    m = jnp.concatenate(contexts, axis=0)
    copies[0].wait()
    eq = mm(x, wq[...]).astype(BF16)
    copies[1].wait()
    ek = mm(m, wk[...]).astype(BF16)
    copies[2].wait()
    ev = mm(m, wv[...]).astype(BF16)
    mixed = []
    for t in range(slots):
        ek_t = ek[t * CL : (t + 1) * CL]
        ev_t = ev[t * CL : (t + 1) * CL]
        ek_out[t] = ek_t
        ev_out[t] = ev_t
        s = mm_nt(head_rows(ek_t), eq[t * rows : (t + 1) * rows]) * (1.0 / math.sqrt(each))
        s = s.reshape(EHEADS, CL, rows)
        p = jnp.exp(s - jnp.max(s, axis=1, keepdims=True))
        w = (p / jnp.sum(p, axis=1, keepdims=True)).reshape(EHEADS * CL, rows)
        wt[t] = w
        mixed.append(mm_tn(w.astype(BF16), head_rows(ev_t)).astype(BF16))
    copies[3].wait()
    out = x.astype(F32) + mm(jnp.concatenate(mixed, axis=0), wo[...])
    enc[...] = out.astype(BF16).reshape(slots, rows, width)


def pullback_kernel(d0, d1, d2, d3, wt, ek, ev, wq_h, wo_h, out, wq, wo, sems):
    load_o = pltpu.make_async_copy(wo_h, wo, sems.at[0])
    load_q = pltpu.make_async_copy(wq_h, wq, sems.at[1])
    load_o.start()
    load_q.start()
    slots, rows, width = d0.shape
    each = width // EHEADS
    d = (d0[...].astype(F32) + d1[...].astype(F32)) + (d2[...].astype(F32) + d3[...].astype(F32))
    d = d.reshape(slots * rows, width)
    load_o.wait()
    de = mm(d.astype(BF16), wo[...]).astype(BF16)
    back = []
    for t in range(slots):
        w = wt[t]
        dw = mm_nt(head_rows(ev[t]), de[t * rows : (t + 1) * rows])
        dw = dw.astype(BF16).astype(F32).reshape(EHEADS, CL, rows)
        w = w.reshape(EHEADS, CL, rows)
        ds = w * (dw - jnp.sum(w * dw, axis=1, keepdims=True)) * (1.0 / math.sqrt(each))
        ds = ds.reshape(EHEADS * CL, rows).astype(BF16)
        back.append(mm_tn(ds, head_rows(ek[t])).astype(BF16))
    load_q.wait()
    out[...] = (d + mm(jnp.concatenate(back, axis=0), wq[...])).reshape(slots, rows, width)


def prep_kernel(kw, vw, wq, wo, q, g, kw_t, vw_t, wq_t, wo_t, qm_t, gm_t):
    kw_t[...] = kw[...].T
    vw_t[...] = vw[...].T
    wq_t[...] = wq[...].T
    wo_t[...] = wo[...].T
    for c in range(qm_t.shape[0]):
        qm_t[c] = head_blocks(q[c * CL : (c + 1) * CL]).T
        gm_t[c] = head_blocks(g[c * CL : (c + 1) * CL]).T


def head_blocks(rows):
    width = rows.shape[1]
    at = lax.broadcasted_iota(jnp.int32, (1, width), 1)
    parts = []
    for h in range(width // HSIZE):
        keep = jnp.where((at >= h * HSIZE) & (at < (h + 1) * HSIZE), 1.0, 0.0).astype(BF16)
        parts.append(rows * keep)
    return jnp.concatenate(parts, axis=0)


def cross_kernel(ids, e00, e01, e10, e11, e20, e21, e30, e31, *rest):
    blocks = (e00, e01, e10, e11, e20, e21, e30, e31)
    q, g, qm_t, gm_t, kw, vw, kw_t, vw_t, cross = rest[:9]
    outs, (table, held, sent, dk, dv, zero, in_sem, out_sem) = rest[9:17], rest[17:]
    z, yh = lax.axis_index("z"), lax.axis_index("yh")
    n_named = held.shape[0]
    spans = n_named // 2
    scale = 1.0 / math.sqrt(HSIZE)

    for i in range(16):
        table[i] = jnp.int32(-1)
    for n in range(n_named):
        slot = ids[n // 2, n % 2]
        dz = lax.rem(slot // 4 - z + NX, NX)
        dy = jnp.bitwise_xor(lax.rem(slot // 2, 2), yh)
        table[dz * 4 + dy * 2 + lax.rem(slot, 2)] = jnp.int32(n)
    zero[...] = jnp.zeros_like(zero)
    places = [4, 5, 0, 1, 2, 3, 6, 7]
    places = [(i, t) for i in places for t in range(2)]
    for i, t in places:
        n = table[2 * i + t]

        @pl.when(n >= 0)
        def _():
            pltpu.make_async_copy(blocks[i].at[t], held.at[n], in_sem.at[n]).start()

    for i, t in places:

        @pl.when(table[2 * i + t] < 0)
        def _():
            pltpu.make_async_copy(zero, outs[i].at[t], out_sem.at[2 * i + t]).start()

    heads = q.shape[1] // HSIZE
    for half in range(2):
        first = half * (n_named // 2)
        for n in range(first, first + n_named // 2):
            pltpu.make_async_copy(e00.at[0], held.at[n], in_sem.at[n]).wait()
        e = held[first : first + n_named // 2].reshape(n_named // 2 * NL, -1)
        ck_all = mm(e, kw[...]).astype(BF16)
        cv_all = mm(e, vw[...]).astype(BF16)
        for i in range(spans // 2):
            c = half * (spans // 2) + i
            ck = ck_all[i * 2 * NL : (i + 1) * 2 * NL]
            cv = cv_all[i * 2 * NL : (i + 1) * 2 * NL]
            qm = head_blocks(q[c * CL : (c + 1) * CL])
            gm = head_blocks(g[c * CL : (c + 1) * CL])
            s = mm(ck, qm_t[c]) * scale
            dp = mm(cv, gm_t[c])
            p = jnp.exp(s - jnp.max(s, axis=0, keepdims=True))
            p = p / jnp.sum(p, axis=0, keepdims=True)
            pb = p.astype(BF16)
            ds = p * (dp - jnp.sum(p * dp, axis=0, keepdims=True)) * scale
            dk[i * 2 * NL : (i + 1) * 2 * NL] = mm(ds.astype(BF16), qm).astype(BF16)
            dv[i * 2 * NL : (i + 1) * 2 * NL] = mm(pb, gm).astype(BF16)
            o = mm_tn(pb, cv)
            for h in range(heads):
                cross[c * CL : (c + 1) * CL, h * HSIZE : (h + 1) * HSIZE] = o[
                    h * CL : (h + 1) * CL, h * HSIZE : (h + 1) * HSIZE
                ]
        de = mm(dk[...], kw_t[...]) + mm(dv[...], vw_t[...])
        sent[first : first + n_named // 2] = de.astype(BF16).reshape(n_named // 2, NL, -1)
        for i, t in places:
            n = table[2 * i + t]

            @pl.when((n >= first) & (n < first + n_named // 2))
            def _():
                pltpu.make_async_copy(sent.at[n], outs[i].at[t], out_sem.at[2 * i + t]).start()

    for i, t in places:
        pltpu.make_async_copy(zero, outs[i].at[t], out_sem.at[2 * i + t]).wait()


def shift(n, by):
    return [(i, (i + by) % n) for i in range(n)]


def local(
    self_q,
    self_k,
    self_v,
    cross_q,
    cross_k_weight,
    cross_v_weight,
    span_ctx,
    neighbours,
    neighbour_ids,
    enc_q,
    enc_k,
    enc_v,
    enc_o,
    mixed_grad,
):
    rows, width = self_q.shape
    slots, nl, ew = neighbours.shape
    spans, per_span = neighbour_ids.shape
    n_named = spans * per_span
    struct = jax.ShapeDtypeStruct
    after = lax.optimization_barrier

    enc, wt, ek, ev = call(
        encode_kernel,
        mib=56,
        out_shape=[
            struct((slots, nl, ew), BF16),
            struct((slots, EHEADS * CL, nl), F32),
            struct((slots, CL, ew), BF16),
            struct((slots, CL, ew), BF16),
        ],
        in_specs=[smem(), vmem(), vmem()] + [hbm()] * 4,
        out_specs=[vmem()] * 4,
        scratch_shapes=[pltpu.VMEM((ew, ew), BF16)] * 4 + [pltpu.SemaphoreType.DMA((4,))],
    )(neighbour_ids, neighbours, span_ctx, enc_q, enc_k, enc_v, enc_o)

    e00 = enc
    e01 = lax.ppermute(e00, "yh", shift(2, 1))
    e30 = lax.ppermute(e00, "z", shift(NX, 1))
    e10 = lax.ppermute(e00, "z", shift(NX, -1))

    self_q, self_k, self_v, _ = after((self_q, self_k, self_v, wt))
    packed = call(
        pack_kernel,
        out_shape=[struct((3, rows, HSIZE), BF16)] * NX,
        in_specs=[hbm()] * 3,
        out_specs=[hbm()] * NX,
        scratch_shapes=[pltpu.SemaphoreType.DMA((NX, 3))],
    )(self_q, self_k, self_v)
    pieces = [packed[0]] + [lax.ppermute(packed[d], "x", shift(NX, d)) for d in range(1, NX)]

    own_kv = jnp.stack([p[1:] for p in pieces])
    e01, e30, e10, own_kv = after((e01, e30, e10, own_kv))
    e11 = lax.ppermute(e01, "z", shift(NX, -1))
    e31 = lax.ppermute(e01, "z", shift(NX, 1))
    e20 = lax.ppermute(e30, "z", shift(NX, 1))
    e21 = lax.ppermute(e11, "z", shift(NX, -1))

    kv = lax.all_gather(own_kv, ("yl", "core"), axis=0)

    kw_t, vw_t, wq_t, wo_t, qm_t, gm_t = call(
        prep_kernel,
        out_shape=[struct((width, ew), BF16)] * 2
        + [struct((ew, ew), BF16)] * 2
        + [struct((spans, width, width // HSIZE * CL), BF16)] * 2,
        in_specs=[vmem()] * 6,
        out_specs=[vmem()] * 6,
    )(*after((cross_k_weight, cross_v_weight, enc_q, enc_o, cross_q, mixed_grad, wt))[:6])

    kv, e21 = after((kv, e21))
    cross, *p = call(
        cross_kernel,
        out_shape=[struct((rows, width), F32)] + [struct((slots, nl, ew), BF16)] * 8,
        in_specs=[smem()] + [hbm()] * 8 + [vmem()] * 8,
        out_specs=[vmem()] + [hbm()] * 8,
        scratch_shapes=[
            pltpu.SMEM((16,), jnp.int32),
            pltpu.VMEM((n_named, nl, ew), BF16),
            pltpu.VMEM((n_named, nl, ew), BF16),
            pltpu.VMEM((n_named // 2 * nl, width), BF16),
            pltpu.VMEM((n_named // 2 * nl, width), BF16),
            pltpu.VMEM((nl, ew), BF16),
            pltpu.SemaphoreType.DMA((n_named,)),
            pltpu.SemaphoreType.DMA((16,)),
        ],
    )(
        neighbour_ids,
        e00,
        e01,
        e10,
        e11,
        e20,
        e21,
        e30,
        e31,
        cross_q,
        mixed_grad,
        qm_t,
        gm_t,
        cross_k_weight,
        cross_v_weight,
        kw_t,
        vw_t,
    )
    p00, p01, p10, p11, p20, p21, p30, p31 = p

    def add(a, b):
        return (a.astype(F32) + b.astype(F32)).astype(BF16)

    far1 = lax.ppermute(p21, "z", shift(NX, -1))
    far0 = lax.ppermute(p20, "z", shift(NX, 1))
    up1 = lax.ppermute(p11, "z", shift(NX, 1))
    down0 = lax.ppermute(p30, "z", shift(NX, -1))
    down1 = lax.ppermute(add(p31, far1), "z", shift(NX, -1))
    up0 = lax.ppermute(add(p10, far0), "z", shift(NX, 1))
    theirs = (p01.astype(F32) + up1.astype(F32) + down1.astype(F32)).astype(BF16)
    other = lax.ppermute(theirs, "yh", shift(2, 1))

    kv, _ = after((kv, cross))
    outs = call(
        attend_kernel,
        out_shape=[struct((rows, HSIZE), BF16)] * NX,
        in_specs=[vmem()] * 5,
        out_specs=[vmem()] * NX,
        scratch_shapes=[
            pltpu.VMEM((rows, HSIZE), F32),
            pltpu.VMEM((rows, 1), F32),
            pltpu.VMEM((rows, 1), F32),
        ],
    )(*pieces, kv)
    selfs = [outs[0]] + [lax.ppermute(outs[d], "x", shift(NX, -d)) for d in range(1, NX)]

    mixed = call(
        mix_kernel,
        out_shape=struct((rows, width), BF16),
        in_specs=[vmem()] * 5,
        out_specs=vmem(),
    )(*selfs, cross)

    grad = call(
        pullback_kernel,
        out_shape=struct((slots, nl, ew), F32),
        in_specs=[vmem()] * 7 + [hbm()] * 2,
        out_specs=vmem(),
        scratch_shapes=[pltpu.VMEM((ew, ew), BF16)] * 2 + [pltpu.SemaphoreType.DMA((2,))],
    )(p00, up0, down0, other, wt, ek, ev, wq_t, wo_t)
    return mixed, grad


def solution(mesh):
    fine = Mesh(mesh.devices.reshape(4, 2, 2, 4, 2), ("x", "yl", "core", "z", "yh"))
    ctx, enc = ("x", "yl", "core"), ("z", "yh")
    tokens = P(ctx, enc)
    return jax.shard_map(
        local,
        mesh=fine,
        in_specs=(
            tokens,
            tokens,
            tokens,
            tokens,
            P(None, enc),
            P(None, enc),
            P(ctx, None),
            P(ctx + enc, None, None),
            P(ctx, None),
            P(),
            P(),
            P(),
            P(),
            tokens,
        ),
        out_specs=(tokens, P(ctx + enc, None, None)),
        check_vma=False,
    )
```

```python
import math

import jax
import jax.numpy as jnp
from jax import lax
from jax.experimental import pallas as pl
from jax.experimental.pallas import tpu as pltpu
from jax.sharding import Mesh
from jax.sharding import PartitionSpec as P

HSIZE = 128
EHEADS = 4
CL = 64
NL = 128
NX = 4
LOG2E = math.log2(math.e)
BF16 = jnp.bfloat16
F32 = jnp.float32

NT = (((1,), (1,)), ((), ()))
TN = (((0,), (0,)), ((), ()))


def mm(a, b):
    return jnp.dot(a, b, preferred_element_type=F32)


def mm_nt(a, b):
    return lax.dot_general(a, b, NT, preferred_element_type=F32)


def mm_tn(a, b):
    return lax.dot_general(a, b, TN, preferred_element_type=F32)


def call(kernel, mib=58, **kw):
    return pl.pallas_call(
        kernel,
        compiler_params=pltpu.CompilerParams(vmem_limit_bytes=mib * 1024 * 1024),
        **kw,
    )


def smem():
    return pl.BlockSpec(memory_space=pltpu.SMEM)


def vmem():
    return pl.BlockSpec(memory_space=pltpu.VMEM)


def hbm():
    return pl.BlockSpec(memory_space=pl.ANY)


def pack_kernel(q_ref, k_ref, v_ref, out):
    for h in range(NX):
        cols = slice(h * HSIZE, (h + 1) * HSIZE)
        for i, src in enumerate((q_ref, k_ref, v_ref)):
            out[h, i] = src[:, cols]


def attend_kernel(pieces, kv, out, acc, top, total):
    r = lax.axis_index("yl") * 2 + lax.axis_index("core")
    scale = LOG2E / math.sqrt(HSIZE)
    for xq in range(NX):
        q = pieces[xq, 0]
        rows = q.shape[0]
        acc[...] = jnp.zeros_like(acc)
        top[...] = jnp.full_like(top, -1e30)
        total[...] = jnp.zeros_like(total)

        def group(xk, masked):
            scores = [mm_nt(q, kv[i, xk, 0]) for i in range(4)]
            if masked:
                at = lax.broadcasted_iota(jnp.int32, (rows, rows), 1)
                upto = lax.broadcasted_iota(jnp.int32, (rows, rows), 0)
                scores = [
                    jnp.where(at + i * rows <= upto + r * rows, s, -1e30)
                    for i, s in enumerate(scores)
                ]
            best = jnp.maximum(
                jnp.maximum(scores[0], scores[1]), jnp.maximum(scores[2], scores[3])
            )
            old = top[...]
            new = jnp.maximum(old, jnp.max(best, axis=-1, keepdims=True))
            fade = jnp.exp2((old - new) * scale)
            weights = [jnp.exp2((s - new) * scale) for s in scores]
            added = (weights[0] + weights[1]) + (weights[2] + weights[3])
            total[...] = total[...] * fade + jnp.sum(added, axis=-1, keepdims=True)
            out = mm(weights[0].astype(BF16), kv[0, xk, 1])
            for i in range(1, 4):
                out = out + mm(weights[i].astype(BF16), kv[i, xk, 1])
            acc[...] = acc[...] * fade + out
            top[...] = new

        for xk in range(xq):
            group(xk, False)
        group(xq, True)
        out[xq] = (acc[...] / total[...]).astype(BF16)


def mix_kernel(pieces, cross, out):
    for h in range(NX):
        cols = slice(h * HSIZE, (h + 1) * HSIZE)
        out[:, cols] = (pieces[h].astype(F32) + cross[:, cols]).astype(BF16)


def head_rows(rows):
    width = rows.shape[1]
    each = width // EHEADS
    at = lax.broadcasted_iota(jnp.int32, (1, width), 1)
    parts = []
    for h in range(EHEADS):
        keep = jnp.where((at >= h * each) & (at < (h + 1) * each), 1.0, 0.0).astype(BF16)
        parts.append(rows * keep)
    return jnp.concatenate(parts, axis=0)


def encode_kernel(
    ids, nb_h, ctx_h, wq_h, wk_h, wv_h, wo_h, enc, wt, ek_out, ev_out, *scratch
):
    nb, ctx, wq, wk, wv, wo, sems = scratch
    both = ((nb_h, nb), (wq_h, wq), (ctx_h, ctx), (wk_h, wk), (wv_h, wv), (wo_h, wo))
    copies = [pltpu.make_async_copy(a, b, sems.at[i]) for i, (a, b) in enumerate(both)]
    for c in copies:
        c.start()
    slots, rows, width = nb.shape
    each = width // EHEADS
    copies[0].wait()
    x = nb[...].reshape(slots * rows, width)
    copies[1].wait()
    eq = mm(x, wq[...]).astype(BF16)
    copies[2].wait()
    contexts = []
    for t in range(slots):
        mine = (lax.axis_index("z") * 2 + lax.axis_index("yh")) * slots + t
        span = jnp.int32(0)
        for c in range(1, ids.shape[1]):
            span = jnp.where((ids[0, c] == mine) | (ids[1, c] == mine), c, span)
        contexts.append(ctx[pl.ds(pl.multiple_of(span * CL, CL), CL), :])
    m = jnp.concatenate(contexts, axis=0)
    copies[3].wait()
    ek = mm(m, wk[...]).astype(BF16)
    copies[4].wait()
    ev = mm(m, wv[...]).astype(BF16)
    mixed = []
    for t in range(slots):
        ek_t = ek[t * CL : (t + 1) * CL]
        ev_t = ev[t * CL : (t + 1) * CL]
        ek_out[t] = ek_t
        ev_out[t] = ev_t
        s = mm_nt(head_rows(ek_t), eq[t * rows : (t + 1) * rows]) * (1.0 / math.sqrt(each))
        s = s.reshape(EHEADS, CL, rows)
        p = jnp.exp(s - jnp.max(s, axis=1, keepdims=True))
        w = (p / jnp.sum(p, axis=1, keepdims=True)).reshape(EHEADS * CL, rows)
        wt[t] = w
        mixed.append(mm_tn(w.astype(BF16), head_rows(ev_t)).astype(BF16))
    copies[5].wait()
    out = x.astype(F32) + mm(jnp.concatenate(mixed, axis=0), wo[...])
    enc[...] = out.astype(BF16).reshape(slots, rows, width)


def pullback_kernel(d0, d1, d2, d3, wt, ek, ev, wq_h, wo_h, out, wq, wo, sems):
    load_o = pltpu.make_async_copy(wo_h, wo, sems.at[0])
    load_q = pltpu.make_async_copy(wq_h, wq, sems.at[1])
    load_o.start()
    load_q.start()
    slots, rows, width = d0.shape
    each = width // EHEADS
    d = (d0[...].astype(F32) + d1[...].astype(F32)) + (d2[...].astype(F32) + d3[...].astype(F32))
    d = d.reshape(slots * rows, width)
    load_o.wait()
    de = mm(d.astype(BF16), wo[...]).astype(BF16)
    back = []
    for t in range(slots):
        w = wt[t]
        dw = mm_nt(head_rows(ev[t]), de[t * rows : (t + 1) * rows])
        dw = dw.astype(BF16).astype(F32).reshape(EHEADS, CL, rows)
        w = w.reshape(EHEADS, CL, rows)
        ds = w * (dw - jnp.sum(w * dw, axis=1, keepdims=True)) * (1.0 / math.sqrt(each))
        ds = ds.reshape(EHEADS * CL, rows).astype(BF16)
        back.append(mm_tn(ds, head_rows(ek[t])).astype(BF16))
    load_q.wait()
    out[...] = (d + mm(jnp.concatenate(back, axis=0), wq[...])).reshape(slots, rows, width)


def prep_kernel(kw, vw, wq, wo, q, g, kw_t, vw_t, wq_t, wo_t, qm_t, gm_t):
    kw_t[...] = kw[...].T
    vw_t[...] = vw[...].T
    wq_t[...] = wq[...].T
    wo_t[...] = wo[...].T
    for c in range(qm_t.shape[0]):
        qm_t[c] = head_blocks(q[c * CL : (c + 1) * CL]).T
        gm_t[c] = head_blocks(g[c * CL : (c + 1) * CL]).T


def head_blocks(rows):
    width = rows.shape[1]
    at = lax.broadcasted_iota(jnp.int32, (1, width), 1)
    parts = []
    for h in range(width // HSIZE):
        keep = jnp.where((at >= h * HSIZE) & (at < (h + 1) * HSIZE), 1.0, 0.0).astype(BF16)
        parts.append(rows * keep)
    return jnp.concatenate(parts, axis=0)


def cross_kernel(ids, e00, e01, e10, e11, e20, e21, e30, e31, *rest):
    blocks = (e00, e01, e10, e11, e20, e21, e30, e31)
    given, cross, outs = rest[:8], rest[8], rest[9:17]
    table, held, sent, dk, dv, zero, in_sem, out_sem, given_sem = rest[17:26]
    here = rest[26:]
    kw, vw, qm_t, gm_t, q, g, kw_t, vw_t = here
    loads = [
        pltpu.make_async_copy(a, b, given_sem.at[i]) for i, (a, b) in enumerate(zip(given, here))
    ]
    loads[0].start()
    loads[1].start()
    z, yh = lax.axis_index("z"), lax.axis_index("yh")
    n_named = held.shape[0]
    spans = n_named // 2
    scale = 1.0 / math.sqrt(HSIZE)

    for i in range(16):
        table[i] = jnp.int32(-1)
    for n in range(n_named):
        slot = ids[n % 2, n // 2]
        dz = lax.rem(slot // 4 - z + NX, NX)
        dy = jnp.bitwise_xor(lax.rem(slot // 2, 2), yh)
        table[dz * 4 + dy * 2 + lax.rem(slot, 2)] = jnp.int32(n)
    zero[...] = jnp.zeros_like(zero)
    places = [4, 5, 0, 1, 2, 3, 6, 7]
    places = [(i, t) for i in places for t in range(2)]
    for i, t in places:
        n = table[2 * i + t]

        @pl.when(n >= 0)
        def _():
            pltpu.make_async_copy(blocks[i].at[t], held.at[n], in_sem.at[n]).start()

    for c in loads[2:]:
        c.start()
    for i, t in places:

        @pl.when(table[2 * i + t] < 0)
        def _():
            pltpu.make_async_copy(zero, outs[i].at[t], out_sem.at[2 * i + t]).start()

    heads = q.shape[1] // HSIZE
    for half in range(2):
        first = half * (n_named // 2)
        for n in range(first, first + n_named // 2):
            pltpu.make_async_copy(e00.at[0], held.at[n], in_sem.at[n]).wait()
        e = held[first : first + n_named // 2].reshape(n_named // 2 * NL, -1)
        if half == 0:
            loads[0].wait()
        ck_all = mm(e, kw[...]).astype(BF16)
        if half == 0:
            loads[1].wait()
        cv_all = mm(e, vw[...]).astype(BF16)
        if half == 0:
            for c in loads[2:6]:
                c.wait()
        for i in range(spans // 2):
            c = half * (spans // 2) + i
            ck = ck_all[i * 2 * NL : (i + 1) * 2 * NL]
            cv = cv_all[i * 2 * NL : (i + 1) * 2 * NL]
            qm = head_blocks(q[c * CL : (c + 1) * CL])
            gm = head_blocks(g[c * CL : (c + 1) * CL])
            s = mm(ck, qm_t[c]) * scale
            dp = mm(cv, gm_t[c])
            p = jnp.exp(s - jnp.max(s, axis=0, keepdims=True))
            p = p / jnp.sum(p, axis=0, keepdims=True)
            pb = p.astype(BF16)
            ds = p * (dp - jnp.sum(p * dp, axis=0, keepdims=True)) * scale
            dk[i * 2 * NL : (i + 1) * 2 * NL] = mm(ds.astype(BF16), qm).astype(BF16)
            dv[i * 2 * NL : (i + 1) * 2 * NL] = mm(pb, gm).astype(BF16)
            o = mm_tn(pb, cv)
            for h in range(heads):
                cross[c * CL : (c + 1) * CL, h * HSIZE : (h + 1) * HSIZE] = o[
                    h * CL : (h + 1) * CL, h * HSIZE : (h + 1) * HSIZE
                ]
        if half == 0:
            loads[6].wait()
            loads[7].wait()
        de = mm(dk[...], kw_t[...]) + mm(dv[...], vw_t[...])
        sent[first : first + n_named // 2] = de.astype(BF16).reshape(n_named // 2, NL, -1)
        for i, t in places:
            n = table[2 * i + t]

            @pl.when((n >= first) & (n < first + n_named // 2))
            def _():
                pltpu.make_async_copy(sent.at[n], outs[i].at[t], out_sem.at[2 * i + t]).start()

    for i, t in places:
        pltpu.make_async_copy(zero, outs[i].at[t], out_sem.at[2 * i + t]).wait()


def shift(n, by):
    return [(i, (i + by) % n) for i in range(n)]


def local(
    self_q,
    self_k,
    self_v,
    cross_q,
    cross_k_weight,
    cross_v_weight,
    span_ctx,
    neighbours,
    neighbour_ids,
    enc_q,
    enc_k,
    enc_v,
    enc_o,
    mixed_grad,
):
    rows, width = self_q.shape
    slots, nl, ew = neighbours.shape
    spans, per_span = neighbour_ids.shape
    n_named = spans * per_span
    struct = jax.ShapeDtypeStruct
    after = lax.optimization_barrier

    ids = neighbour_ids.T

    enc, wt, ek, ev = call(
        encode_kernel,
        out_shape=[
            struct((slots, nl, ew), BF16),
            struct((slots, EHEADS * CL, nl), F32),
            struct((slots, CL, ew), BF16),
            struct((slots, CL, ew), BF16),
        ],
        in_specs=[smem()] + [hbm()] * 6,
        out_specs=[vmem()] * 4,
        scratch_shapes=[pltpu.VMEM(neighbours.shape, BF16), pltpu.VMEM(span_ctx.shape, BF16)]
        + [pltpu.VMEM((ew, ew), BF16)] * 4
        + [pltpu.SemaphoreType.DMA((6,))],
    )(ids, neighbours, span_ctx, enc_q, enc_k, enc_v, enc_o)

    e00 = enc
    e01 = lax.ppermute(e00, "yh", shift(2, 1))
    e30 = lax.ppermute(e00, "z", shift(NX, 1))
    e10 = lax.ppermute(e00, "z", shift(NX, -1))

    self_q, self_k, self_v, _ = after((self_q, self_k, self_v, wt))
    packed = call(
        pack_kernel,
        out_shape=struct((NX, 3, rows, HSIZE), BF16),
        in_specs=[vmem()] * 3,
        out_specs=vmem(),
    )(self_q, self_k, self_v)
    pieces = lax.all_to_all(packed, "x", 0, 0)
    own_kv = pieces[:, 1:]

    e01, e30, e10, packed = after((e01, e30, e10, packed))
    e11 = lax.ppermute(e01, "z", shift(NX, -1))
    e31 = lax.ppermute(e01, "z", shift(NX, 1))

    weights = after((cross_k_weight, cross_v_weight, enc_q, enc_o, cross_q, mixed_grad, e01))[:6]
    prepared = call(
        prep_kernel,
        out_shape=[struct((width, ew), BF16)] * 2
        + [struct((ew, ew), BF16)] * 2
        + [struct((spans, width, width // HSIZE * CL), BF16)] * 2,
        in_specs=[vmem()] * 6,
        out_specs=[vmem()] * 6,
    )(*weights)

    e11, e31, e30, own_kv, *prepared = after((e11, e31, e30, own_kv, *prepared))
    kw_t, vw_t, wq_t, wo_t, qm_t, gm_t = prepared
    e20 = lax.ppermute(e30, "z", shift(NX, 1))
    e21 = lax.ppermute(e11, "z", shift(NX, -1))
    kv = lax.all_gather(own_kv, ("yl", "core"), axis=0)

    cross, *p = call(
        cross_kernel,
        out_shape=[struct((rows, width), F32)] + [struct((slots, nl, ew), BF16)] * 8,
        in_specs=[smem()] + [hbm()] * 16,
        out_specs=[vmem()] + [hbm()] * 8,
        scratch_shapes=[
            pltpu.SMEM((16,), jnp.int32),
            pltpu.VMEM((n_named, nl, ew), BF16),
            pltpu.VMEM((n_named, nl, ew), BF16),
            pltpu.VMEM((n_named // 2 * nl, width), BF16),
            pltpu.VMEM((n_named // 2 * nl, width), BF16),
            pltpu.VMEM((nl, ew), BF16),
            pltpu.SemaphoreType.DMA((n_named,)),
            pltpu.SemaphoreType.DMA((16,)),
            pltpu.SemaphoreType.DMA((8,)),
        ]
        + [pltpu.VMEM((ew, width), BF16)] * 2
        + [pltpu.VMEM((spans, width, width // HSIZE * CL), BF16)] * 2
        + [pltpu.VMEM((rows, width), BF16)] * 2
        + [pltpu.VMEM((width, ew), BF16)] * 2,
    )(
        ids,
        e00,
        e01,
        e10,
        e11,
        e20,
        e21,
        e30,
        e31,
        cross_k_weight,
        cross_v_weight,
        qm_t,
        gm_t,
        cross_q,
        mixed_grad,
        kw_t,
        vw_t,
    )
    p00, p01, p10, p11, p20, p21, p30, p31 = p

    def add(a, b):
        return (a.astype(F32) + b.astype(F32)).astype(BF16)

    far1 = lax.ppermute(p21, "z", shift(NX, -1))
    far0 = lax.ppermute(p20, "z", shift(NX, 1))
    kv, _ = after((kv, cross))
    outs = call(
        attend_kernel,
        mib=20,
        out_shape=struct((NX, rows, HSIZE), BF16),
        in_specs=[vmem()] * 2,
        out_specs=vmem(),
        scratch_shapes=[
            pltpu.VMEM((rows, HSIZE), F32),
            pltpu.VMEM((rows, 1), F32),
            pltpu.VMEM((rows, 1), F32),
        ],
    )(pieces, kv)
    far1, far0, p11, outs = after((far1, far0, p11, outs))
    selfs = lax.all_to_all(outs, "x", 0, 0)
    down1 = lax.ppermute(add(p31, far1), "z", shift(NX, -1))
    up1 = lax.ppermute(p11, "z", shift(NX, 1))
    near0 = add(p10, far0)
    down1, up1, near0, p30, selfs = after((down1, up1, near0, p30, selfs))
    theirs = (p01.astype(F32) + up1.astype(F32) + down1.astype(F32)).astype(BF16)
    other = lax.ppermute(theirs, "yh", shift(2, 1))
    up0 = lax.ppermute(near0, "z", shift(NX, 1))
    down0 = lax.ppermute(p30, "z", shift(NX, -1))

    grad = call(
        pullback_kernel,
        mib=20,
        out_shape=struct((slots, nl, ew), F32),
        in_specs=[vmem()] * 7 + [hbm()] * 2,
        out_specs=vmem(),
        scratch_shapes=[pltpu.VMEM((ew, ew), BF16)] * 2 + [pltpu.SemaphoreType.DMA((2,))],
    )(p00, up0, down0, other, wt, ek, ev, wq_t, wo_t)

    mixed = call(
        mix_kernel,
        mib=20,
        out_shape=struct((rows, width), BF16),
        in_specs=[vmem()] * 2,
        out_specs=vmem(),
    )(selfs, cross)
    return mixed, grad


def solution(mesh):
    fine = Mesh(mesh.devices.reshape(4, 2, 2, 4, 2), ("x", "yl", "core", "z", "yh"))
    ctx, enc = ("x", "yl", "core"), ("z", "yh")
    tokens = P(ctx, enc)
    return jax.shard_map(
        local,
        mesh=fine,
        in_specs=(
            tokens,
            tokens,
            tokens,
            tokens,
            P(None, enc),
            P(None, enc),
            P(ctx, None),
            P(ctx + enc, None, None),
            P(ctx, None),
            P(),
            P(),
            P(),
            P(),
            tokens,
        ),
        out_specs=(tokens, P(ctx + enc, None, None)),
        check_vma=False,
    )
```

```python
import functools
import math

import jax
import jax.numpy as jnp
from jax import lax
from jax.experimental import pallas as pl
from jax.experimental.pallas import tpu as pltpu
from jax.sharding import Mesh
from jax.sharding import PartitionSpec as P

HSIZE = 128
EHEADS = 4
CL = 64
NL = 128
NX = 4
LOG2E = math.log2(math.e)
BF16 = jnp.bfloat16
F32 = jnp.float32

NT = (((1,), (1,)), ((), ()))
TN = (((0,), (0,)), ((), ()))


def mm(a, b):
    return jnp.dot(a, b, preferred_element_type=F32)


def mm_nt(a, b):
    return lax.dot_general(a, b, NT, preferred_element_type=F32)


def mm_tn(a, b):
    return lax.dot_general(a, b, TN, preferred_element_type=F32)


def call(kernel, mib=58, **kw):
    return pl.pallas_call(
        kernel,
        compiler_params=pltpu.CompilerParams(vmem_limit_bytes=mib * 1024 * 1024),
        **kw,
    )


def smem():
    return pl.BlockSpec(memory_space=pltpu.SMEM)


def vmem():
    return pl.BlockSpec(memory_space=pltpu.VMEM)


def hbm():
    return pl.BlockSpec(memory_space=pl.ANY)


def pack_kernel(q_ref, k_ref, v_ref, out):
    for h in range(NX):
        cols = slice(h * HSIZE, (h + 1) * HSIZE)
        for i, src in enumerate((q_ref, k_ref, v_ref)):
            out[h, i] = src[:, cols]


def attend_kernel(pieces, kv, out, acc, top, total):
    r = lax.axis_index("yl") * 2 + lax.axis_index("core")
    scale = LOG2E / math.sqrt(HSIZE)
    for xq in range(NX):
        q = pieces[xq, 0]
        rows = q.shape[0]
        acc[...] = jnp.zeros_like(acc)
        top[...] = jnp.full_like(top, -1e30)
        total[...] = jnp.zeros_like(total)

        def group(xk, masked):
            scores = [mm_nt(q, kv[i, xk, 0]) for i in range(4)]
            if masked:
                at = lax.broadcasted_iota(jnp.int32, (rows, rows), 1)
                upto = lax.broadcasted_iota(jnp.int32, (rows, rows), 0)
                scores = [
                    jnp.where(at + i * rows <= upto + r * rows, s, -1e30)
                    for i, s in enumerate(scores)
                ]
            best = jnp.maximum(
                jnp.maximum(scores[0], scores[1]), jnp.maximum(scores[2], scores[3])
            )
            old = top[...]
            new = jnp.maximum(old, jnp.max(best, axis=-1, keepdims=True))
            fade = jnp.exp2((old - new) * scale)
            weights = [jnp.exp2((s - new) * scale) for s in scores]
            added = (weights[0] + weights[1]) + (weights[2] + weights[3])
            total[...] = total[...] * fade + jnp.sum(added, axis=-1, keepdims=True)
            out = mm(weights[0].astype(BF16), kv[0, xk, 1])
            for i in range(1, 4):
                out = out + mm(weights[i].astype(BF16), kv[i, xk, 1])
            acc[...] = acc[...] * fade + out
            top[...] = new

        for xk in range(xq):
            group(xk, False)
        group(xq, True)
        out[xq] = (acc[...] / total[...]).astype(BF16)


def mix_kernel(pieces, cross, out):
    for h in range(NX):
        cols = slice(h * HSIZE, (h + 1) * HSIZE)
        out[:, cols] = (pieces[h].astype(F32) + cross[:, cols]).astype(BF16)


def head_rows(rows):
    width = rows.shape[1]
    each = width // EHEADS
    at = lax.broadcasted_iota(jnp.int32, (1, width), 1)
    parts = []
    for h in range(EHEADS):
        keep = jnp.where((at >= h * each) & (at < (h + 1) * each), 1.0, 0.0).astype(BF16)
        parts.append(rows * keep)
    return jnp.concatenate(parts, axis=0)


def encode_kernel(other, ids, nb_h, ctx_h, wq_h, wk_h, wv_h, wo_h, enc, *rest):
    kept, (nb, ctx, wq, wk, wv, wo, sems) = rest[:-7], rest[-7:]
    both = ((nb_h, nb), (wq_h, wq), (ctx_h, ctx), (wk_h, wk), (wv_h, wv), (wo_h, wo))
    copies = [pltpu.make_async_copy(a, b, sems.at[i]) for i, (a, b) in enumerate(both)]
    for c in copies:
        c.start()
    slots, rows, width = nb.shape
    each = width // EHEADS
    copies[0].wait()
    x = nb[...].reshape(slots * rows, width)
    copies[1].wait()
    eq = mm(x, wq[...]).astype(BF16)
    copies[2].wait()
    contexts = []
    for t in range(slots):
        pair = jnp.bitwise_xor(lax.axis_index("yh"), other)
        mine = (lax.axis_index("z") * 2 + pair) * slots + t
        span = jnp.int32(0)
        for c in range(1, ids.shape[1]):
            span = jnp.where((ids[0, c] == mine) | (ids[1, c] == mine), c, span)
        contexts.append(ctx[pl.ds(pl.multiple_of(span * CL, CL), CL), :])
    m = jnp.concatenate(contexts, axis=0)
    copies[3].wait()
    ek = mm(m, wk[...]).astype(BF16)
    copies[4].wait()
    ev = mm(m, wv[...]).astype(BF16)
    mixed = []
    for t in range(slots):
        ek_t = ek[t * CL : (t + 1) * CL]
        ev_t = ev[t * CL : (t + 1) * CL]
        s = mm_nt(head_rows(ek_t), eq[t * rows : (t + 1) * rows]) * (1.0 / math.sqrt(each))
        s = s.reshape(EHEADS, CL, rows)
        p = jnp.exp(s - jnp.max(s, axis=1, keepdims=True))
        w = (p * (1.0 / jnp.sum(p, axis=1, keepdims=True))).reshape(EHEADS * CL, rows)
        for ref, value in zip(kept, (w, ek_t, ev_t)):
            ref[t] = value
        mixed.append(mm_tn(w.astype(BF16), head_rows(ev_t)).astype(BF16))
    copies[5].wait()
    out = x.astype(F32) + mm(jnp.concatenate(mixed, axis=0), wo[...])
    enc[...] = out.astype(BF16).reshape(slots, rows, width)


def pullback_kernel(*refs):
    given, out, here, sems = refs[:9], refs[9], refs[10:19], refs[19]
    d0, d1, d2, d3, wo, ev, wt, ek, wq = here
    loads = [pltpu.make_async_copy(a, b, sems.at[i]) for i, (a, b) in enumerate(zip(given, here))]
    for c in loads:
        c.start()
    slots, rows, width = d0.shape
    each = width // EHEADS
    for c in loads[:4]:
        c.wait()
    d = (d0[...].astype(F32) + d1[...].astype(F32)) + (d2[...].astype(F32) + d3[...].astype(F32))
    d = d.reshape(slots * rows, width)
    loads[4].wait()
    de = mm(d.astype(BF16), wo[...]).astype(BF16)
    for c in loads[5:8]:
        c.wait()
    back = []
    for t in range(slots):
        w = wt[t]
        dw = mm_nt(head_rows(ev[t]), de[t * rows : (t + 1) * rows])
        dw = dw.astype(BF16).astype(F32).reshape(EHEADS, CL, rows)
        w = w.reshape(EHEADS, CL, rows)
        ds = w * (dw - jnp.sum(w * dw, axis=1, keepdims=True)) * (1.0 / math.sqrt(each))
        ds = ds.reshape(EHEADS * CL, rows).astype(BF16)
        back.append(mm_tn(ds, head_rows(ek[t])).astype(BF16))
    loads[8].wait()
    out[...] = (d + mm(jnp.concatenate(back, axis=0), wq[...])).reshape(slots, rows, width)


def turn_kernel(kw, vw, wq, wo, kw_t, vw_t, wq_t, wo_t):
    kw_t[...] = kw[...].T
    vw_t[...] = vw[...].T
    wq_t[...] = wq[...].T
    wo_t[...] = wo[...].T


def blocks_kernel(q, g, qm_t, gm_t):
    for c in range(qm_t.shape[0]):
        qm_t[c] = head_blocks(q[c * CL : (c + 1) * CL]).T
        gm_t[c] = head_blocks(g[c * CL : (c + 1) * CL]).T


def head_blocks(rows):
    width = rows.shape[1]
    at = lax.broadcasted_iota(jnp.int32, (1, width), 1)
    parts = []
    for h in range(width // HSIZE):
        keep = jnp.where((at >= h * HSIZE) & (at < (h + 1) * HSIZE), 1.0, 0.0).astype(BF16)
        parts.append(rows * keep)
    return jnp.concatenate(parts, axis=0)


def cross_kernel(ids, e00, e01, e10, e11, e20, e21, e30, e31, *rest):
    blocks = (e00, e01, e10, e11, e20, e21, e30, e31)
    given, cross, outs = rest[:8], rest[8], rest[9:17]
    table, held, sent, ck, cv, dk, dv, zero, in_sem, out_sem, given_sem = rest[17:28]
    here = rest[28:]
    kw, vw, qm_t, gm_t, q, g, kw_t, vw_t = here
    loads = [
        pltpu.make_async_copy(a, b, given_sem.at[i]) for i, (a, b) in enumerate(zip(given, here))
    ]
    loads[0].start()
    loads[1].start()
    z, yh = lax.axis_index("z"), lax.axis_index("yh")
    n_named = held.shape[0]
    spans = n_named // 2
    scale = 1.0 / math.sqrt(HSIZE)

    for i in range(16):
        table[i] = jnp.int32(-1)
    for n in range(n_named):
        slot = ids[n % 2, n // 2]
        dz = lax.rem(slot // 4 - z + NX, NX)
        dy = jnp.bitwise_xor(lax.rem(slot // 2, 2), yh)
        table[dz * 4 + dy * 2 + lax.rem(slot, 2)] = jnp.int32(n)
    zero[...] = jnp.zeros_like(zero)
    places = [4, 5, 0, 1, 2, 3, 6, 7]
    places = [(i, t) for i in places for t in range(2)]
    for i, t in places:
        n = table[2 * i + t]

        @pl.when(n >= 0)
        def _():
            pltpu.make_async_copy(blocks[i].at[t], held.at[n], in_sem.at[n]).start()

    for c in loads[2:]:
        c.start()
    for i, t in places:

        @pl.when(table[2 * i + t] < 0)
        def _():
            pltpu.make_async_copy(zero, outs[i].at[t], out_sem.at[2 * i + t]).start()

    heads = q.shape[1] // HSIZE
    pair = 2 * NL
    for half in range(2):
        first = half * (n_named // 2)
        for n in range(first, first + n_named // 2):
            pltpu.make_async_copy(e00.at[0], held.at[n], in_sem.at[n]).wait()
        e = held[first : first + n_named // 2].reshape(n_named // 2 * NL, -1)
        at = slice(first * NL, (first + n_named // 2) * NL)
        if half == 0:
            loads[0].wait()
        ck[at] = mm(e, kw[...]).astype(BF16)
        if half == 0:
            loads[1].wait()
        cv[at] = mm(e, vw[...]).astype(BF16)
    for c in loads[2:]:
        c.wait()

    def scores(c):
        at = slice(c * pair, (c + 1) * pair)
        return mm(ck[at], qm_t[c]) * scale, mm(cv[at], gm_t[c])

    def soften(s, dp):
        p = jnp.exp(s - jnp.max(s, axis=0, keepdims=True))
        p = p * (1.0 / jnp.sum(p, axis=0, keepdims=True))
        ds = p * (dp - jnp.sum(p * dp, axis=0, keepdims=True)) * scale
        return p.astype(BF16), ds.astype(BF16)

    def products(c, pb, ds):
        at = slice(c * pair, (c + 1) * pair)
        dk[at] = mm(ds, head_blocks(q[c * CL : (c + 1) * CL])).astype(BF16)
        dv[at] = mm(pb, head_blocks(g[c * CL : (c + 1) * CL])).astype(BF16)
        o = mm_tn(pb, cv[at])
        for h in range(heads):
            cross[c * CL : (c + 1) * CL, h * HSIZE : (h + 1) * HSIZE] = o[
                h * CL : (h + 1) * CL, h * HSIZE : (h + 1) * HSIZE
            ]

    def back(c):
        at = slice(c * pair, (c + 1) * pair)
        de = mm(dk[at], kw_t[...]) + mm(dv[at], vw_t[...])
        sent[2 * c : 2 * c + 2] = de.astype(BF16).reshape(2, NL, -1)

    ahead = scores(0)
    for c in range(spans):
        now = ahead
        if c + 1 < spans:
            ahead = scores(c + 1)
        soft = soften(*now)
        if c >= 1:
            back(c - 1)
        products(c, *soft)
    back(spans - 1)
    for i, t in places:
        n = table[2 * i + t]

        @pl.when(n >= 0)
        def _():
            pltpu.make_async_copy(sent.at[n], outs[i].at[t], out_sem.at[2 * i + t]).start()

    for i, t in places:
        pltpu.make_async_copy(zero, outs[i].at[t], out_sem.at[2 * i + t]).wait()


def shift(n, by):
    return [(i, (i + by) % n) for i in range(n)]


def local(
    self_q,
    self_k,
    self_v,
    cross_q,
    cross_k_weight,
    cross_v_weight,
    span_ctx,
    neighbours,
    neighbour_ids,
    enc_q,
    enc_k,
    enc_v,
    enc_o,
    mixed_grad,
):
    rows, width = self_q.shape
    slots, nl, ew = neighbours.shape
    spans, per_span = neighbour_ids.shape
    n_named = spans * per_span
    struct = jax.ShapeDtypeStruct
    after = lax.optimization_barrier

    ids = neighbour_ids.T

    raw = lax.ppermute(neighbours, "yh", shift(2, 1))

    def encode(other, blocks, kept):
        return call(
            functools.partial(encode_kernel, other),
            out_shape=[struct((slots, nl, ew), BF16)] + kept,
            in_specs=[smem()] + [hbm()] * 6,
            out_specs=[vmem()] * (1 + len(kept)),
            scratch_shapes=[pltpu.VMEM(neighbours.shape, BF16), pltpu.VMEM(span_ctx.shape, BF16)]
            + [pltpu.VMEM((ew, ew), BF16)] * 4
            + [pltpu.SemaphoreType.DMA((6,))],
        )(ids, blocks, span_ctx, enc_q, enc_k, enc_v, enc_o)

    e00, wt, ek, ev = encode(
        0,
        neighbours,
        [
            struct((slots, EHEADS * CL, nl), F32),
            struct((slots, CL, ew), BF16),
            struct((slots, CL, ew), BF16),
        ],
    )

    e30 = lax.ppermute(e00, "z", shift(NX, 1))
    e10 = lax.ppermute(e00, "z", shift(NX, -1))

    self_q, self_k, self_v, _ = after((self_q, self_k, self_v, wt))
    packed = call(
        pack_kernel,
        out_shape=struct((NX, 3, rows, HSIZE), BF16),
        in_specs=[vmem()] * 3,
        out_specs=vmem(),
    )(self_q, self_k, self_v)
    raw, _ = after((raw, wt))
    (e01,) = encode(1, raw, [])
    e01, e30, e10, packed = after((e01, e30, e10, packed))
    e11 = lax.ppermute(e01, "z", shift(NX, -1))
    e31 = lax.ppermute(e01, "z", shift(NX, 1))
    pieces = lax.all_to_all(packed, "x", 0, 0)

    weights = after((cross_k_weight, cross_v_weight, enc_q, enc_o, e01))[:4]
    turned = call(
        turn_kernel,
        out_shape=[struct((width, ew), BF16)] * 2 + [struct((ew, ew), BF16)] * 2,
        in_specs=[vmem()] * 4,
        out_specs=[vmem()] * 4,
    )(*weights)

    e30, e11, e31, *turned = after((e30, e11, e31, *turned))
    kw_t, vw_t, wq_t, wo_t = turned
    e20 = lax.ppermute(e30, "z", shift(NX, 1))
    e21 = lax.ppermute(e11, "z", shift(NX, -1))
    kv = lax.all_gather(pieces[:, 1:], ("yl", "core"), axis=0)

    queries, grads, _ = after((cross_q, mixed_grad, e11))
    qm_t, gm_t = call(
        blocks_kernel,
        out_shape=[struct((spans, width, width // HSIZE * CL), BF16)] * 2,
        in_specs=[vmem()] * 2,
        out_specs=[vmem()] * 2,
    )(queries, grads)

    cross, *p = call(
        cross_kernel,
        out_shape=[struct((rows, width), F32)] + [struct((slots, nl, ew), BF16)] * 8,
        in_specs=[smem()] + [hbm()] * 16,
        out_specs=[vmem()] + [hbm()] * 8,
        scratch_shapes=[
            pltpu.SMEM((16,), jnp.int32),
            pltpu.VMEM((n_named, nl, ew), BF16),
            pltpu.VMEM((n_named, nl, ew), BF16),
            pltpu.VMEM((n_named * nl, width), BF16),
            pltpu.VMEM((n_named * nl, width), BF16),
            pltpu.VMEM((n_named * nl, width), BF16),
            pltpu.VMEM((n_named * nl, width), BF16),
            pltpu.VMEM((nl, ew), BF16),
            pltpu.SemaphoreType.DMA((n_named,)),
            pltpu.SemaphoreType.DMA((16,)),
            pltpu.SemaphoreType.DMA((8,)),
        ]
        + [pltpu.VMEM((ew, width), BF16)] * 2
        + [pltpu.VMEM((spans, width, width // HSIZE * CL), BF16)] * 2
        + [pltpu.VMEM((rows, width), BF16)] * 2
        + [pltpu.VMEM((width, ew), BF16)] * 2,
    )(
        ids,
        e00,
        e01,
        e10,
        e11,
        e20,
        e21,
        e30,
        e31,
        cross_k_weight,
        cross_v_weight,
        qm_t,
        gm_t,
        cross_q,
        mixed_grad,
        kw_t,
        vw_t,
    )
    p00, p01, p10, p11, p20, p21, p30, p31 = p

    def add(a, b):
        return (a.astype(F32) + b.astype(F32)).astype(BF16)

    far1 = lax.ppermute(p21, "z", shift(NX, -1))
    far0 = lax.ppermute(p20, "z", shift(NX, 1))
    far1, far0, p11 = after((far1, far0, p11))
    down1 = lax.ppermute(add(p31, far1), "z", shift(NX, -1))
    up1 = lax.ppermute(p11, "z", shift(NX, 1))
    near0 = add(p10, far0)
    kv, _ = after((kv, far1))
    outs = call(
        attend_kernel,
        out_shape=struct((NX, rows, HSIZE), BF16),
        in_specs=[vmem()] * 2,
        out_specs=vmem(),
        scratch_shapes=[
            pltpu.VMEM((rows, HSIZE), F32),
            pltpu.VMEM((rows, 1), F32),
            pltpu.VMEM((rows, 1), F32),
        ],
    )(pieces, kv)
    down1, up1, near0, p30, outs = after((down1, up1, near0, p30, outs))
    selfs = lax.all_to_all(outs, "x", 0, 0)
    theirs = (p01.astype(F32) + up1.astype(F32) + down1.astype(F32)).astype(BF16)
    other = lax.ppermute(theirs, "yh", shift(2, 1))
    up0 = lax.ppermute(near0, "z", shift(NX, 1))
    down0 = lax.ppermute(p30, "z", shift(NX, -1))

    grad = call(
        pullback_kernel,
        out_shape=struct((slots, nl, ew), F32),
        in_specs=[hbm()] * 9,
        out_specs=vmem(),
        scratch_shapes=[pltpu.VMEM((slots, nl, ew), BF16)] * 4
        + [
            pltpu.VMEM((ew, ew), BF16),
            pltpu.VMEM(ev.shape, BF16),
            pltpu.VMEM(wt.shape, F32),
            pltpu.VMEM(ek.shape, BF16),
            pltpu.VMEM((ew, ew), BF16),
            pltpu.SemaphoreType.DMA((9,)),
        ],
    )(p00, up0, down0, other, wo_t, ev, wt, ek, wq_t)

    mixed = call(
        mix_kernel,
        out_shape=struct((rows, width), BF16),
        in_specs=[vmem()] * 2,
        out_specs=vmem(),
    )(selfs, cross)
    return mixed, grad


def solution(mesh):
    fine = Mesh(mesh.devices.reshape(4, 2, 2, 4, 2), ("x", "yl", "core", "z", "yh"))
    ctx, enc = ("x", "yl", "core"), ("z", "yh")
    tokens = P(ctx, enc)
    return jax.shard_map(
        local,
        mesh=fine,
        in_specs=(
            tokens,
            tokens,
            tokens,
            tokens,
            P(None, enc),
            P(None, enc),
            P(ctx, None),
            P(ctx + enc, None, None),
            P(ctx, None),
            P(),
            P(),
            P(),
            P(),
            tokens,
        ),
        out_specs=(tokens, P(ctx + enc, None, None)),
        check_vma=False,
    )
```

```python
import math

import jax
import jax.numpy as jnp
from jax import lax
from jax.experimental import pallas as pl
from jax.experimental.pallas import tpu as pltpu
from jax.sharding import Mesh
from jax.sharding import PartitionSpec as P

HSIZE = 128
EHEADS = 4
CL = 64
NL = 128
NX = 4
LOG2E = math.log2(math.e)
BF16 = jnp.bfloat16
F32 = jnp.float32

NT = (((1,), (1,)), ((), ()))
TN = (((0,), (0,)), ((), ()))


def mm(a, b):
    return jnp.dot(a, b, preferred_element_type=F32)


def mm_nt(a, b):
    return lax.dot_general(a, b, NT, preferred_element_type=F32)


def mm_tn(a, b):
    return lax.dot_general(a, b, TN, preferred_element_type=F32)


def call(kernel, mib=58, **kw):
    return pl.pallas_call(
        kernel,
        compiler_params=pltpu.CompilerParams(vmem_limit_bytes=mib * 1024 * 1024),
        **kw,
    )


def smem():
    return pl.BlockSpec(memory_space=pltpu.SMEM)


def vmem():
    return pl.BlockSpec(memory_space=pltpu.VMEM)


def hbm():
    return pl.BlockSpec(memory_space=pl.ANY)


def pack_kernel(q_ref, k_ref, v_ref, out):
    for h in range(NX):
        cols = slice(h * HSIZE, (h + 1) * HSIZE)
        for i, src in enumerate((q_ref, k_ref, v_ref)):
            out[h, i] = src[:, cols]


def attend_kernel(pieces, kv, out, acc, top, total):
    r = lax.axis_index("yl") * 2 + lax.axis_index("core")
    scale = LOG2E / math.sqrt(HSIZE)
    for xq in range(NX):
        q = pieces[xq, 0]
        rows = q.shape[0]
        acc[...] = jnp.zeros_like(acc)
        top[...] = jnp.full_like(top, -1e30)
        total[...] = jnp.zeros_like(total)

        def group(xk, masked):
            scores = [mm_nt(q, kv[i, xk, 0]) for i in range(4)]
            if masked:
                at = lax.broadcasted_iota(jnp.int32, (rows, rows), 1)
                upto = lax.broadcasted_iota(jnp.int32, (rows, rows), 0)
                scores = [
                    jnp.where(at + i * rows <= upto + r * rows, s, -1e30)
                    for i, s in enumerate(scores)
                ]
            best = jnp.maximum(
                jnp.maximum(scores[0], scores[1]), jnp.maximum(scores[2], scores[3])
            )
            old = top[...]
            new = jnp.maximum(old, jnp.max(best, axis=-1, keepdims=True))
            fade = jnp.exp2((old - new) * scale)
            weights = [jnp.exp2((s - new) * scale) for s in scores]
            added = (weights[0] + weights[1]) + (weights[2] + weights[3])
            total[...] = total[...] * fade + jnp.sum(added, axis=-1, keepdims=True)
            out = mm(weights[0].astype(BF16), kv[0, xk, 1])
            for i in range(1, 4):
                out = out + mm(weights[i].astype(BF16), kv[i, xk, 1])
            acc[...] = acc[...] * fade + out
            top[...] = new

        for xk in range(xq):
            group(xk, False)
        group(xq, True)
        out[xq] = (acc[...] / total[...]).astype(BF16)


def mix_kernel(pieces, cross, out):
    for h in range(NX):
        cols = slice(h * HSIZE, (h + 1) * HSIZE)
        out[:, cols] = (pieces[h].astype(F32) + cross[:, cols]).astype(BF16)


def head_rows(rows):
    width = rows.shape[1]
    each = width // EHEADS
    at = lax.broadcasted_iota(jnp.int32, (1, width), 1)
    parts = []
    for h in range(EHEADS):
        keep = jnp.where((at >= h * each) & (at < (h + 1) * each), 1.0, 0.0).astype(BF16)
        parts.append(rows * keep)
    return jnp.concatenate(parts, axis=0)


def encode_kernel(
    ids, nb_h, ctx_h, wq_h, wk_h, wv_h, wo_h, enc, wt, ek_out, ev_out, *scratch
):
    nb, ctx, wq, wk, wv, wo, sems = scratch
    both = ((nb_h, nb), (wq_h, wq), (ctx_h, ctx), (wk_h, wk), (wv_h, wv), (wo_h, wo))
    copies = [pltpu.make_async_copy(a, b, sems.at[i]) for i, (a, b) in enumerate(both)]
    for c in copies[:3]:
        c.start()
    slots, rows, width = nb.shape
    each = width // EHEADS
    copies[0].wait()
    x = nb[...].reshape(slots * rows, width)
    copies[1].wait()
    for c in copies[3:]:
        c.start()
    eq = mm(x, wq[...]).astype(BF16)
    copies[2].wait()
    contexts = []
    for t in range(slots):
        mine = (lax.axis_index("z") * 2 + lax.axis_index("yh")) * slots + t
        span = jnp.int32(0)
        for c in range(1, ids.shape[1]):
            span = jnp.where((ids[0, c] == mine) | (ids[1, c] == mine), c, span)
        contexts.append(ctx[pl.ds(pl.multiple_of(span * CL, CL), CL), :])
    m = jnp.concatenate(contexts, axis=0)
    copies[3].wait()
    ek = mm(m, wk[...]).astype(BF16)
    copies[4].wait()
    ev = mm(m, wv[...]).astype(BF16)
    mixed = []
    for t in range(slots):
        ek_t = ek[t * CL : (t + 1) * CL]
        ev_t = ev[t * CL : (t + 1) * CL]
        s = mm_nt(head_rows(ek_t), eq[t * rows : (t + 1) * rows]) * (1.0 / math.sqrt(each))
        s = s.reshape(EHEADS, CL, rows)
        p = jnp.exp(s - jnp.max(s, axis=1, keepdims=True))
        w = (p * (1.0 / jnp.sum(p, axis=1, keepdims=True))).reshape(EHEADS * CL, rows)
        wt[t] = w
        ek_out[t] = ek_t
        ev_out[t] = ev_t
        mixed.append(mm_tn(w.astype(BF16), head_rows(ev_t)).astype(BF16))
    copies[5].wait()
    out = x.astype(F32) + mm(jnp.concatenate(mixed, axis=0), wo[...])
    enc[...] = out.astype(BF16).reshape(slots, rows, width)


def pullback_kernel(*refs):
    given, out, here, sems = refs[:9], refs[9], refs[10:19], refs[19]
    d0, d1, d2, d3, wo, ev, wt, ek, wq = here
    loads = [pltpu.make_async_copy(a, b, sems.at[i]) for i, (a, b) in enumerate(zip(given, here))]
    for c in loads[:5]:
        c.start()
    slots, rows, width = d0.shape
    each = width // EHEADS
    for c in loads[:4]:
        c.wait()
    for c in loads[5:]:
        c.start()
    d = (d0[...].astype(F32) + d1[...].astype(F32)) + (d2[...].astype(F32) + d3[...].astype(F32))
    d = d.reshape(slots * rows, width)
    loads[4].wait()
    de = mm(d.astype(BF16), wo[...]).astype(BF16)
    for c in loads[5:8]:
        c.wait()
    back = []
    for t in range(slots):
        w = wt[t]
        dw = mm_nt(head_rows(ev[t]), de[t * rows : (t + 1) * rows])
        dw = dw.astype(BF16).astype(F32).reshape(EHEADS, CL, rows)
        w = w.reshape(EHEADS, CL, rows)
        ds = w * (dw - jnp.sum(w * dw, axis=1, keepdims=True)) * (1.0 / math.sqrt(each))
        ds = ds.reshape(EHEADS * CL, rows).astype(BF16)
        back.append(mm_tn(ds, head_rows(ek[t])).astype(BF16))
    loads[8].wait()
    out[...] = (d + mm(jnp.concatenate(back, axis=0), wq[...])).reshape(slots, rows, width)


def turn_kernel(kw, vw, wq, wo, kv_t, wq_t, wo_t):
    width = kw.shape[1]
    kv_t[:width] = kw[...].T
    kv_t[width:] = vw[...].T
    wq_t[...] = wq[...].T
    wo_t[...] = wo[...].T


def blocks_kernel(q, g, qm_t, gm_t):
    for c in range(qm_t.shape[0]):
        qm_t[c] = head_blocks(q[c * CL : (c + 1) * CL]).T
        gm_t[c] = head_blocks(g[c * CL : (c + 1) * CL]).T


def head_blocks(rows):
    width = rows.shape[1]
    at = lax.broadcasted_iota(jnp.int32, (1, width), 1)
    parts = []
    for h in range(width // HSIZE):
        keep = jnp.where((at >= h * HSIZE) & (at < (h + 1) * HSIZE), 1.0, 0.0).astype(BF16)
        parts.append(rows * keep)
    return jnp.concatenate(parts, axis=0)


def cross_kernel(ids, e00, e01, e10, e11, e20, e21, e30, e31, *rest):
    blocks = (e00, e01, e10, e11, e20, e21, e30, e31)
    given, cross, outs = rest[:7], rest[7], rest[8:16]
    table, held, sent, ckv, dkv, zero, in_sem, out_sem, given_sem = rest[16:25]
    kvw, qm_t, gm_t, q, g, kv_t = rest[25:]
    width = q.shape[1]
    here = (kvw.at[:, :width], kvw.at[:, width:], qm_t, gm_t, q, g, kv_t)
    loads = [
        pltpu.make_async_copy(a, b, given_sem.at[i]) for i, (a, b) in enumerate(zip(given, here))
    ]
    loads[0].start()
    loads[1].start()
    z, yh = lax.axis_index("z"), lax.axis_index("yh")
    n_named = held.shape[0]
    spans = n_named // 2
    scale = 1.0 / math.sqrt(HSIZE)

    for i in range(16):
        table[i] = jnp.int32(-1)
    for n in range(n_named):
        slot = ids[n % 2, n // 2]
        dz = lax.rem(slot // 4 - z + NX, NX)
        dy = jnp.bitwise_xor(lax.rem(slot // 2, 2), yh)
        table[dz * 4 + dy * 2 + lax.rem(slot, 2)] = jnp.int32(n)
    zero[...] = jnp.zeros_like(zero)
    places = [4, 5, 0, 1, 2, 3, 6, 7]
    places = [(i, t) for i in places for t in range(2)]
    for i, t in places:
        n = table[2 * i + t]

        @pl.when(n >= 0)
        def _():
            pltpu.make_async_copy(blocks[i].at[t], held.at[n], in_sem.at[n]).start()

    for i, t in places:

        @pl.when(table[2 * i + t] < 0)
        def _():
            pltpu.make_async_copy(zero, outs[i].at[t], out_sem.at[2 * i + t]).start()

    heads = width // HSIZE
    pair = 2 * NL
    for half in range(2):
        first = half * (n_named // 2)
        for n in range(first, first + n_named // 2):
            pltpu.make_async_copy(e00.at[0], held.at[n], in_sem.at[n]).wait()
        e = held[first : first + n_named // 2].reshape(n_named // 2 * NL, -1)
        if half == 0:
            loads[0].wait()
            loads[1].wait()
            for c in loads[2:]:
                c.start()
        ckv[first * NL : (first + n_named // 2) * NL] = mm(e, kvw[...]).astype(BF16)
    for c in loads[2:]:
        c.wait()

    def scores(c):
        at = slice(c * pair, (c + 1) * pair)
        return mm(ckv[at, :width], qm_t[c]), mm(ckv[at, width:], gm_t[c])

    def soften(s, dp):
        p = jnp.exp2((s - jnp.max(s, axis=0, keepdims=True)) * (scale * LOG2E))
        p = p * (1.0 / jnp.sum(p, axis=0, keepdims=True))
        ds = p * ((dp - jnp.sum(p * dp, axis=0, keepdims=True)) * scale)
        return p.astype(BF16), ds.astype(BF16)

    def products(c, pb, ds):
        at = slice(c * pair, (c + 1) * pair)
        dkv[at, :width] = mm(ds, head_blocks(q[c * CL : (c + 1) * CL])).astype(BF16)
        dkv[at, width:] = mm(pb, head_blocks(g[c * CL : (c + 1) * CL])).astype(BF16)
        pt = pb.T
        for h in range(heads):
            cols = slice(h * HSIZE, (h + 1) * HSIZE)
            cross[c * CL : (c + 1) * CL, cols] = mm(
                pt[h * CL : (h + 1) * CL], ckv[at, width + h * HSIZE : width + (h + 1) * HSIZE]
            )

    def back(c):
        at = slice(c * pair, (c + 1) * pair)
        sent[2 * c : 2 * c + 2] = mm(dkv[at], kv_t[...]).astype(BF16).reshape(2, NL, -1)

    def send(low, high):
        for i, t in places:
            n = table[2 * i + t]

            @pl.when((n >= low) & (n < high))
            def _():
                pltpu.make_async_copy(sent.at[n], outs[i].at[t], out_sem.at[2 * i + t]).start()

    ahead = scores(0)
    for c in range(spans):
        now = ahead
        if c + 1 < spans:
            ahead = scores(c + 1)
        soft = soften(*now)
        if c >= 1:
            back(c - 1)
        products(c, *soft)
    send(0, n_named - 2)
    back(spans - 1)
    send(n_named - 2, n_named)
    for i, t in places:
        pltpu.make_async_copy(zero, outs[i].at[t], out_sem.at[2 * i + t]).wait()


def shift(n, by):
    return [(i, (i + by) % n) for i in range(n)]


def local(
    self_q,
    self_k,
    self_v,
    cross_q,
    cross_k_weight,
    cross_v_weight,
    span_ctx,
    neighbours,
    neighbour_ids,
    enc_q,
    enc_k,
    enc_v,
    enc_o,
    mixed_grad,
):
    rows, width = self_q.shape
    slots, nl, ew = neighbours.shape
    spans, per_span = neighbour_ids.shape
    n_named = spans * per_span
    struct = jax.ShapeDtypeStruct
    after = lax.optimization_barrier

    ids = neighbour_ids.T

    e00, wt, ek, ev = call(
        encode_kernel,
        out_shape=[
            struct((slots, nl, ew), BF16),
            struct((slots, EHEADS * CL, nl), F32),
            struct((slots, CL, ew), BF16),
            struct((slots, CL, ew), BF16),
        ],
        in_specs=[smem()] + [hbm()] * 6,
        out_specs=[vmem()] * 4,
        scratch_shapes=[pltpu.VMEM(neighbours.shape, BF16), pltpu.VMEM(span_ctx.shape, BF16)]
        + [pltpu.VMEM((ew, ew), BF16)] * 4
        + [pltpu.SemaphoreType.DMA((6,))],
    )(ids, neighbours, span_ctx, enc_q, enc_k, enc_v, enc_o)

    e01 = lax.ppermute(e00, "yh", shift(2, 1))
    e30 = lax.ppermute(e00, "z", shift(NX, 1))
    e10 = lax.ppermute(e00, "z", shift(NX, -1))

    self_q, self_k, self_v, _ = after((self_q, self_k, self_v, wt))
    packed = call(
        pack_kernel,
        out_shape=struct((NX, 3, rows, HSIZE), BF16),
        in_specs=[vmem()] * 3,
        out_specs=vmem(),
    )(self_q, self_k, self_v)
    pieces = lax.all_to_all(packed, "x", 0, 0)
    own_kv = pieces[:, 1:]

    e01, e30, e10, packed = after((e01, e30, e10, packed))
    e11 = lax.ppermute(e01, "z", shift(NX, -1))
    e31 = lax.ppermute(e01, "z", shift(NX, 1))

    weights = after((cross_k_weight, cross_v_weight, enc_q, enc_o, e01))[:4]
    turned = call(
        turn_kernel,
        out_shape=[struct((2 * width, ew), BF16)] + [struct((ew, ew), BF16)] * 2,
        in_specs=[vmem()] * 4,
        out_specs=[vmem()] * 3,
    )(*weights)

    e30, e11, e31, own_kv, *turned = after((e30, e11, e31, own_kv, *turned))
    kv_t, wq_t, wo_t = turned
    e20 = lax.ppermute(e30, "z", shift(NX, 1))
    e21 = lax.ppermute(e11, "z", shift(NX, -1))
    kv = lax.all_gather(own_kv, ("yl", "core"), axis=0)

    queries, grads, _ = after((cross_q, mixed_grad, e11))
    qm_t, gm_t = call(
        blocks_kernel,
        out_shape=[struct((spans, width, width // HSIZE * CL), BF16)] * 2,
        in_specs=[vmem()] * 2,
        out_specs=[vmem()] * 2,
    )(queries, grads)

    cross, *p = call(
        cross_kernel,
        out_shape=[struct((rows, width), F32)] + [struct((slots, nl, ew), BF16)] * 8,
        in_specs=[smem()] + [hbm()] * 15,
        out_specs=[vmem()] + [hbm()] * 8,
        scratch_shapes=[
            pltpu.SMEM((16,), jnp.int32),
            pltpu.VMEM((n_named, nl, ew), BF16),
            pltpu.VMEM((n_named, nl, ew), BF16),
            pltpu.VMEM((n_named * nl, 2 * width), BF16),
            pltpu.VMEM((n_named * nl, 2 * width), BF16),
            pltpu.VMEM((nl, ew), BF16),
            pltpu.SemaphoreType.DMA((n_named,)),
            pltpu.SemaphoreType.DMA((16,)),
            pltpu.SemaphoreType.DMA((7,)),
            pltpu.VMEM((ew, 2 * width), BF16),
        ]
        + [pltpu.VMEM((spans, width, width // HSIZE * CL), BF16)] * 2
        + [pltpu.VMEM((rows, width), BF16)] * 2
        + [pltpu.VMEM((2 * width, ew), BF16)],
    )(
        ids,
        e00,
        e01,
        e10,
        e11,
        e20,
        e21,
        e30,
        e31,
        cross_k_weight,
        cross_v_weight,
        qm_t,
        gm_t,
        cross_q,
        mixed_grad,
        kv_t,
    )
    p00, p01, p10, p11, p20, p21, p30, p31 = p

    def add(a, b):
        return (a.astype(F32) + b.astype(F32)).astype(BF16)

    far1 = lax.ppermute(p21, "z", shift(NX, -1))
    far0 = lax.ppermute(p20, "z", shift(NX, 1))
    kv, _ = after((kv, cross))
    outs = call(
        attend_kernel,
        out_shape=struct((NX, rows, HSIZE), BF16),
        in_specs=[vmem()] * 2,
        out_specs=vmem(),
        scratch_shapes=[
            pltpu.VMEM((rows, HSIZE), F32),
            pltpu.VMEM((rows, 1), F32),
            pltpu.VMEM((rows, 1), F32),
        ],
    )(pieces, kv)
    far1, far0, p11, outs = after((far1, far0, p11, outs))
    selfs = lax.all_to_all(outs, "x", 0, 0)
    down1 = lax.ppermute(add(p31, far1), "z", shift(NX, -1))
    up1 = lax.ppermute(p11, "z", shift(NX, 1))
    near0 = add(p10, far0)
    down1, up1, near0, p30 = after((down1, up1, near0, p30))
    theirs = (p01.astype(F32) + up1.astype(F32) + down1.astype(F32)).astype(BF16)
    other = lax.ppermute(theirs, "yh", shift(2, 1))
    up0 = lax.ppermute(near0, "z", shift(NX, 1))
    down0 = lax.ppermute(p30, "z", shift(NX, -1))

    grad = call(
        pullback_kernel,
        out_shape=struct((slots, nl, ew), F32),
        in_specs=[hbm()] * 9,
        out_specs=vmem(),
        scratch_shapes=[pltpu.VMEM((slots, nl, ew), BF16)] * 4
        + [
            pltpu.VMEM((ew, ew), BF16),
            pltpu.VMEM(ev.shape, BF16),
            pltpu.VMEM(wt.shape, F32),
            pltpu.VMEM(ek.shape, BF16),
            pltpu.VMEM((ew, ew), BF16),
            pltpu.SemaphoreType.DMA((9,)),
        ],
    )(p00, up0, down0, other, wo_t, ev, wt, ek, wq_t)

    mixed = call(
        mix_kernel,
        out_shape=struct((rows, width), BF16),
        in_specs=[vmem()] * 2,
        out_specs=vmem(),
    )(selfs, cross)
    return mixed, grad


def solution(mesh):
    fine = Mesh(mesh.devices.reshape(4, 2, 2, 4, 2), ("x", "yl", "core", "z", "yh"))
    ctx, enc = ("x", "yl", "core"), ("z", "yh")
    tokens = P(ctx, enc)
    return jax.shard_map(
        local,
        mesh=fine,
        in_specs=(
            tokens,
            tokens,
            tokens,
            tokens,
            P(None, enc),
            P(None, enc),
            P(ctx, None),
            P(ctx + enc, None, None),
            P(ctx, None),
            P(),
            P(),
            P(),
            P(),
            tokens,
        ),
        out_specs=(tokens, P(ctx + enc, None, None)),
        check_vma=False,
    )
```

```python
import math

import jax
import jax.numpy as jnp
from jax import lax
from jax.experimental import pallas as pl
from jax.experimental.pallas import tpu as pltpu
from jax.sharding import Mesh
from jax.sharding import PartitionSpec as P

HSIZE = 128
EHEADS = 4
CL = 64
NL = 128
NX = 4
LOG2E = math.log2(math.e)
BF16 = jnp.bfloat16
F32 = jnp.float32

NT = (((1,), (1,)), ((), ()))
TN = (((0,), (0,)), ((), ()))


def mm(a, b):
    return jnp.dot(a, b, preferred_element_type=F32)


def mm_nt(a, b):
    return lax.dot_general(a, b, NT, preferred_element_type=F32)


def mm_tn(a, b):
    return lax.dot_general(a, b, TN, preferred_element_type=F32)


def call(kernel, mib=58, **kw):
    return pl.pallas_call(
        kernel,
        compiler_params=pltpu.CompilerParams(vmem_limit_bytes=mib * 1024 * 1024),
        **kw,
    )


def smem():
    return pl.BlockSpec(memory_space=pltpu.SMEM)


def vmem():
    return pl.BlockSpec(memory_space=pltpu.VMEM)


def hbm():
    return pl.BlockSpec(memory_space=pl.ANY)


def pack_kernel(q_ref, k_ref, v_ref, out):
    for h in range(NX):
        cols = slice(h * HSIZE, (h + 1) * HSIZE)
        for i, src in enumerate((q_ref, k_ref, v_ref)):
            out[h, i] = src[:, cols]


def attend_kernel(pieces, kv, o0, o1, o2, o3, acc, top, total):
    x = lax.axis_index("x")
    r = lax.axis_index("yl") * 2 + lax.axis_index("core")
    scale = LOG2E / math.sqrt(HSIZE)
    for xq in range(NX):
        q = pieces[xq, 0]
        rows = q.shape[0]
        acc[...] = jnp.zeros_like(acc)
        top[...] = jnp.full_like(top, -1e30)
        total[...] = jnp.zeros_like(total)

        def group(xk, masked):
            scores = [mm_nt(q, kv[i, xk, 0]) for i in range(4)]
            if masked:
                at = lax.broadcasted_iota(jnp.int32, (rows, rows), 1)
                upto = lax.broadcasted_iota(jnp.int32, (rows, rows), 0)
                scores = [
                    jnp.where(at + i * rows <= upto + r * rows, s, -1e30)
                    for i, s in enumerate(scores)
                ]
            best = jnp.maximum(
                jnp.maximum(scores[0], scores[1]), jnp.maximum(scores[2], scores[3])
            )
            old = top[...]
            new = jnp.maximum(old, jnp.max(best, axis=-1, keepdims=True))
            fade = jnp.exp2((old - new) * scale)
            weights = [jnp.exp2((s - new) * scale) for s in scores]
            added = (weights[0] + weights[1]) + (weights[2] + weights[3])
            total[...] = total[...] * fade + jnp.sum(added, axis=-1, keepdims=True)
            out = mm(weights[0].astype(BF16), kv[0, xk, 1])
            for i in range(1, 4):
                out = out + mm(weights[i].astype(BF16), kv[i, xk, 1])
            acc[...] = acc[...] * fade + out
            top[...] = new

        for xk in range(xq):
            group(xk, False)
        group(xq, True)
        result = (acc[...] / total[...]).astype(BF16)
        for d, out in enumerate((o0, o1, o2, o3)):

            @pl.when(lax.rem(xq + d, NX) == x)
            def _():
                out[...] = result


def mix_kernel(s0, s1, s2, s3, cross, out):
    x = lax.axis_index("x")
    for d, piece in enumerate((s0, s1, s2, s3)):
        cols = pl.ds(pl.multiple_of(lax.rem(x + d, NX) * HSIZE, HSIZE), HSIZE)
        out[:, cols] = (piece[...].astype(F32) + cross[:, cols]).astype(BF16)


def head_rows(rows):
    width = rows.shape[1]
    each = width // EHEADS
    at = lax.broadcasted_iota(jnp.int32, (1, width), 1)
    parts = []
    for h in range(EHEADS):
        keep = jnp.where((at >= h * each) & (at < (h + 1) * each), 1.0, 0.0).astype(BF16)
        parts.append(rows * keep)
    return jnp.concatenate(parts, axis=0)


def encode_kernel(
    ids, nb_h, ctx_h, wq_h, wk_h, wv_h, wo_h, enc, wt, ek_out, ev_out, *scratch
):
    nb, ctx, wq, wk, wv, wo, sems = scratch
    both = ((nb_h, nb), (wq_h, wq), (ctx_h, ctx), (wk_h, wk), (wv_h, wv), (wo_h, wo))
    copies = [pltpu.make_async_copy(a, b, sems.at[i]) for i, (a, b) in enumerate(both)]
    for c in copies:
        c.start()
    slots, rows, width = nb.shape
    each = width // EHEADS
    copies[0].wait()
    x = nb[...].reshape(slots * rows, width)
    copies[1].wait()
    eq = mm(x, wq[...]).astype(BF16)
    copies[2].wait()
    contexts = []
    for t in range(slots):
        mine = (lax.axis_index("z") * 2 + lax.axis_index("yh")) * slots + t
        span = jnp.int32(0)
        for c in range(1, ids.shape[1]):
            span = jnp.where((ids[0, c] == mine) | (ids[1, c] == mine), c, span)
        contexts.append(ctx[pl.ds(pl.multiple_of(span * CL, CL), CL), :])
    m = jnp.concatenate(contexts, axis=0)
    copies[3].wait()
    ek = mm(m, wk[...]).astype(BF16)
    copies[4].wait()
    ev = mm(m, wv[...]).astype(BF16)
    mixed = []
    for t in range(slots):
        ek_t = ek[t * CL : (t + 1) * CL]
        ev_t = ev[t * CL : (t + 1) * CL]
        s = mm_nt(head_rows(ek_t), eq[t * rows : (t + 1) * rows]) * (1.0 / math.sqrt(each))
        s = s.reshape(EHEADS, CL, rows)
        p = jnp.exp(s - jnp.max(s, axis=1, keepdims=True))
        w = (p * (1.0 / jnp.sum(p, axis=1, keepdims=True))).reshape(EHEADS * CL, rows)
        wt[t] = w
        ek_out[t] = ek_t
        ev_out[t] = ev_t
        mixed.append(mm_tn(w.astype(BF16), head_rows(ev_t)).astype(BF16))
    copies[5].wait()
    out = x.astype(F32) + mm(jnp.concatenate(mixed, axis=0), wo[...])
    enc[...] = out.astype(BF16).reshape(slots, rows, width)


def pullback_kernel(*refs):
    given, out, here, sems = refs[:9], refs[9], refs[10:19], refs[19]
    d0, d1, d2, d3, wo, ev, wt, ek, wq = here
    loads = [pltpu.make_async_copy(a, b, sems.at[i]) for i, (a, b) in enumerate(zip(given, here))]
    for c in loads[:5]:
        c.start()
    slots, rows, width = d0.shape
    each = width // EHEADS
    for c in loads[:4]:
        c.wait()
    for c in loads[5:]:
        c.start()
    d = (d0[...].astype(F32) + d1[...].astype(F32)) + (d2[...].astype(F32) + d3[...].astype(F32))
    d = d.reshape(slots * rows, width)
    loads[4].wait()
    de = mm(d.astype(BF16), wo[...]).astype(BF16)
    for c in loads[5:8]:
        c.wait()
    back = []
    for t in range(slots):
        w = wt[t]
        dw = mm_nt(head_rows(ev[t]), de[t * rows : (t + 1) * rows])
        dw = dw.astype(BF16).astype(F32).reshape(EHEADS, CL, rows)
        w = w.reshape(EHEADS, CL, rows)
        ds = w * (dw - jnp.sum(w * dw, axis=1, keepdims=True)) * (1.0 / math.sqrt(each))
        ds = ds.reshape(EHEADS * CL, rows).astype(BF16)
        back.append(mm_tn(ds, head_rows(ek[t])).astype(BF16))
    loads[8].wait()
    out[...] = (d + mm(jnp.concatenate(back, axis=0), wq[...])).reshape(slots, rows, width)


def turn_kernel(kw, vw, wq, wo, kv_t, wq_t, wo_t):
    width = kw.shape[1]
    kv_t[:width] = kw[...].T
    kv_t[width:] = vw[...].T
    wq_t[...] = wq[...].T
    wo_t[...] = wo[...].T


def blocks_kernel(q, g, qm_t, gm_t):
    for c in range(qm_t.shape[0]):
        qm_t[c] = head_blocks(q[c * CL : (c + 1) * CL]).T
        gm_t[c] = head_blocks(g[c * CL : (c + 1) * CL]).T


def head_blocks(rows):
    width = rows.shape[1]
    at = lax.broadcasted_iota(jnp.int32, (1, width), 1)
    parts = []
    for h in range(width // HSIZE):
        keep = jnp.where((at >= h * HSIZE) & (at < (h + 1) * HSIZE), 1.0, 0.0).astype(BF16)
        parts.append(rows * keep)
    return jnp.concatenate(parts, axis=0)


def cross_kernel(ids, e00, e01, e10, e11, e20, e21, e30, e31, *rest):
    blocks = (e00, e01, e10, e11, e20, e21, e30, e31)
    given, cross, outs = rest[:7], rest[7], rest[8:16]
    table, held, sent, ckv, dkv, zero, in_sem, out_sem, given_sem, mine, mine_sem = rest[16:27]
    kvw, qm_t, gm_t, q, g, kv_t = rest[27:]
    width = q.shape[1]
    here = (kvw.at[:, :width], kvw.at[:, width:], qm_t, gm_t, q, g, kv_t)
    loads = [
        pltpu.make_async_copy(a, b, given_sem.at[i]) for i, (a, b) in enumerate(zip(given, here))
    ]
    loads[0].start()
    loads[1].start()
    z, yh = lax.axis_index("z"), lax.axis_index("yh")
    n_named = held.shape[0]
    spans = n_named // 2
    scale = 1.0 / math.sqrt(HSIZE)

    for i in range(16):
        table[i] = jnp.int32(-1)
    for n in range(n_named):
        slot = ids[n % 2, n // 2]
        dz = lax.rem(slot // 4 - z + NX, NX)
        dy = jnp.bitwise_xor(lax.rem(slot // 2, 2), yh)
        table[dz * 4 + dy * 2 + lax.rem(slot, 2)] = jnp.int32(n)
    zero[...] = jnp.zeros_like(zero)
    places = [4, 5, 0, 1, 2, 3, 6, 7]
    places = [(i, t) for i in places for t in range(2)]
    for i, t in places:
        n = table[2 * i + t]

        @pl.when(n >= 0)
        def _():
            pltpu.make_async_copy(blocks[i].at[t], held.at[n], in_sem.at[n]).start()

    for i, t in places:

        @pl.when(table[2 * i + t] < 0)
        def _():
            pltpu.make_async_copy(zero, outs[i].at[t], out_sem.at[2 * i + t]).start()

    heads = width // HSIZE
    pair = 2 * NL
    for half in range(2):
        first = half * (n_named // 2)
        for n in range(first, first + n_named // 2):
            pltpu.make_async_copy(e00.at[0], held.at[n], in_sem.at[n]).wait()
        e = held[first : first + n_named // 2].reshape(n_named // 2 * NL, -1)
        if half == 0:
            loads[0].wait()
            loads[1].wait()
            for c in loads[2:]:
                c.start()
        ckv[first * NL : (first + n_named // 2) * NL] = mm(e, kvw[...]).astype(BF16)
    for c in loads[2:]:
        c.wait()

    def scores(c):
        at = slice(c * pair, (c + 1) * pair)
        return mm(ckv[at, :width], qm_t[c]), mm(ckv[at, width:], gm_t[c])

    def soften(s, dp):
        p = jnp.exp2((s - jnp.max(s, axis=0, keepdims=True)) * (scale * LOG2E))
        p = p * (1.0 / jnp.sum(p, axis=0, keepdims=True))
        ds = p * ((dp - jnp.sum(p * dp, axis=0, keepdims=True)) * scale)
        return p.astype(BF16), ds.astype(BF16)

    def products(c, pb, ds):
        at = slice(c * pair, (c + 1) * pair)
        dkv[at, :width] = mm(ds, head_blocks(q[c * CL : (c + 1) * CL])).astype(BF16)
        dkv[at, width:] = mm(pb, head_blocks(g[c * CL : (c + 1) * CL])).astype(BF16)
        pt = pb.T
        for h in range(heads):
            cols = slice(h * HSIZE, (h + 1) * HSIZE)
            mine[c * CL : (c + 1) * CL, cols] = mm(
                pt[h * CL : (h + 1) * CL], ckv[at, width + h * HSIZE : width + (h + 1) * HSIZE]
            )

    def back(c):
        at = slice(c * pair, (c + 1) * pair)
        sent[2 * c : 2 * c + 2] = mm(dkv[at], kv_t[...]).astype(BF16).reshape(2, NL, -1)

    def send(low, high):
        for i, t in places:
            n = table[2 * i + t]

            @pl.when((n >= low) & (n < high))
            def _():
                pltpu.make_async_copy(sent.at[n], outs[i].at[t], out_sem.at[2 * i + t]).start()

    ahead = scores(0)
    for c in range(spans):
        now = ahead
        if c + 1 < spans:
            ahead = scores(c + 1)
        soft = soften(*now)
        if c >= 1:
            back(c - 1)
        products(c, *soft)
    leave = pltpu.make_async_copy(mine, cross, mine_sem)
    leave.start()
    send(0, n_named - 2)
    back(spans - 1)
    send(n_named - 2, n_named)
    leave.wait()
    for i, t in places:
        pltpu.make_async_copy(zero, outs[i].at[t], out_sem.at[2 * i + t]).wait()


def shift(n, by):
    return [(i, (i + by) % n) for i in range(n)]


def local(
    self_q,
    self_k,
    self_v,
    cross_q,
    cross_k_weight,
    cross_v_weight,
    span_ctx,
    neighbours,
    neighbour_ids,
    enc_q,
    enc_k,
    enc_v,
    enc_o,
    mixed_grad,
):
    rows, width = self_q.shape
    slots, nl, ew = neighbours.shape
    spans, per_span = neighbour_ids.shape
    n_named = spans * per_span
    struct = jax.ShapeDtypeStruct
    after = lax.optimization_barrier

    ids = neighbour_ids.T

    e00, wt, ek, ev = call(
        encode_kernel,
        out_shape=[
            struct((slots, nl, ew), BF16),
            struct((slots, EHEADS * CL, nl), F32),
            struct((slots, CL, ew), BF16),
            struct((slots, CL, ew), BF16),
        ],
        in_specs=[smem()] + [hbm()] * 6,
        out_specs=[vmem()] * 4,
        scratch_shapes=[pltpu.VMEM(neighbours.shape, BF16), pltpu.VMEM(span_ctx.shape, BF16)]
        + [pltpu.VMEM((ew, ew), BF16)] * 4
        + [pltpu.SemaphoreType.DMA((6,))],
    )(ids, neighbours, span_ctx, enc_q, enc_k, enc_v, enc_o)

    e01 = lax.ppermute(e00, "yh", shift(2, 1))
    e30 = lax.ppermute(e00, "z", shift(NX, 1))
    e10 = lax.ppermute(e00, "z", shift(NX, -1))

    self_q, self_k, self_v, _ = after((self_q, self_k, self_v, wt))
    packed = call(
        pack_kernel,
        out_shape=struct((NX, 3, rows, HSIZE), BF16),
        in_specs=[vmem()] * 3,
        out_specs=vmem(),
    )(self_q, self_k, self_v)
    pieces = lax.all_to_all(packed, "x", 0, 0)
    own_kv = pieces[:, 1:]

    e01, e30, e10, packed = after((e01, e30, e10, packed))
    e11 = lax.ppermute(e01, "z", shift(NX, -1))
    e31 = lax.ppermute(e01, "z", shift(NX, 1))

    weights = after((cross_k_weight, cross_v_weight, enc_q, enc_o, e01))[:4]
    turned = call(
        turn_kernel,
        out_shape=[struct((2 * width, ew), BF16)] + [struct((ew, ew), BF16)] * 2,
        in_specs=[vmem()] * 4,
        out_specs=[vmem()] * 3,
    )(*weights)

    e30, e11, e31, own_kv, *turned = after((e30, e11, e31, own_kv, *turned))
    kv_t, wq_t, wo_t = turned
    e20 = lax.ppermute(e30, "z", shift(NX, 1))
    e21 = lax.ppermute(e11, "z", shift(NX, -1))
    kv = lax.all_gather(own_kv, ("yl", "core"), axis=0)

    queries, grads, _ = after((cross_q, mixed_grad, e11))
    qm_t, gm_t = call(
        blocks_kernel,
        out_shape=[struct((spans, width, width // HSIZE * CL), BF16)] * 2,
        in_specs=[vmem()] * 2,
        out_specs=[vmem()] * 2,
    )(queries, grads)

    cross, *p = call(
        cross_kernel,
        out_shape=[struct((rows, width), F32)] + [struct((slots, nl, ew), BF16)] * 8,
        in_specs=[smem()] + [hbm()] * 15,
        out_specs=[hbm()] * 9,
        scratch_shapes=[
            pltpu.SMEM((16,), jnp.int32),
            pltpu.VMEM((n_named, nl, ew), BF16),
            pltpu.VMEM((n_named, nl, ew), BF16),
            pltpu.VMEM((n_named * nl, 2 * width), BF16),
            pltpu.VMEM((n_named * nl, 2 * width), BF16),
            pltpu.VMEM((nl, ew), BF16),
            pltpu.SemaphoreType.DMA((n_named,)),
            pltpu.SemaphoreType.DMA((16,)),
            pltpu.SemaphoreType.DMA((7,)),
            pltpu.VMEM((rows, width), F32),
            pltpu.SemaphoreType.DMA,
            pltpu.VMEM((ew, 2 * width), BF16),
        ]
        + [pltpu.VMEM((spans, width, width // HSIZE * CL), BF16)] * 2
        + [pltpu.VMEM((rows, width), BF16)] * 2
        + [pltpu.VMEM((2 * width, ew), BF16)],
    )(
        ids,
        e00,
        e01,
        e10,
        e11,
        e20,
        e21,
        e30,
        e31,
        cross_k_weight,
        cross_v_weight,
        qm_t,
        gm_t,
        cross_q,
        mixed_grad,
        kv_t,
    )
    p00, p01, p10, p11, p20, p21, p30, p31 = p

    def add(a, b):
        return (a.astype(F32) + b.astype(F32)).astype(BF16)

    far1 = lax.ppermute(p21, "z", shift(NX, -1))
    far0 = lax.ppermute(p20, "z", shift(NX, 1))
    far1, far0, p11 = after((far1, far0, p11))
    down1 = lax.ppermute(add(p31, far1), "z", shift(NX, -1))
    up1 = lax.ppermute(p11, "z", shift(NX, 1))
    near0 = add(p10, far0)
    kv, _ = after((kv, far1))
    outs = call(
        attend_kernel,
        out_shape=[struct((rows, HSIZE), BF16)] * NX,
        in_specs=[vmem()] * 2,
        out_specs=[vmem()] * NX,
        scratch_shapes=[
            pltpu.VMEM((rows, HSIZE), F32),
            pltpu.VMEM((rows, 1), F32),
            pltpu.VMEM((rows, 1), F32),
        ],
    )(pieces, kv)
    down1, up1, near0, p30, *outs = after((down1, up1, near0, p30, *outs))
    theirs = (p01.astype(F32) + up1.astype(F32) + down1.astype(F32)).astype(BF16)
    other = lax.ppermute(theirs, "yh", shift(2, 1))
    up0 = lax.ppermute(near0, "z", shift(NX, 1))
    down0 = lax.ppermute(p30, "z", shift(NX, -1))
    selfs = [outs[0]] + [lax.ppermute(outs[d], "x", shift(NX, -d)) for d in range(1, NX)]

    grad = call(
        pullback_kernel,
        out_shape=struct((slots, nl, ew), F32),
        in_specs=[hbm()] * 9,
        out_specs=vmem(),
        scratch_shapes=[pltpu.VMEM((slots, nl, ew), BF16)] * 4
        + [
            pltpu.VMEM((ew, ew), BF16),
            pltpu.VMEM(ev.shape, BF16),
            pltpu.VMEM(wt.shape, F32),
            pltpu.VMEM(ek.shape, BF16),
            pltpu.VMEM((ew, ew), BF16),
            pltpu.SemaphoreType.DMA((9,)),
        ],
    )(p00, up0, down0, other, wo_t, ev, wt, ek, wq_t)

    mixed = call(
        mix_kernel,
        out_shape=struct((rows, width), BF16),
        in_specs=[vmem()] * 5,
        out_specs=vmem(),
    )(*selfs, cross)
    return mixed, grad


def solution(mesh):
    fine = Mesh(mesh.devices.reshape(4, 2, 2, 4, 2), ("x", "yl", "core", "z", "yh"))
    ctx, enc = ("x", "yl", "core"), ("z", "yh")
    tokens = P(ctx, enc)
    return jax.shard_map(
        local,
        mesh=fine,
        in_specs=(
            tokens,
            tokens,
            tokens,
            tokens,
            P(None, enc),
            P(None, enc),
            P(ctx, None),
            P(ctx + enc, None, None),
            P(ctx, None),
            P(),
            P(),
            P(),
            P(),
            tokens,
        ),
        out_specs=(tokens, P(ctx + enc, None, None)),
        check_vma=False,
    )
```

```python
import math

import jax
import jax.numpy as jnp
from jax import lax
from jax.experimental import pallas as pl
from jax.experimental.pallas import tpu as pltpu
from jax.sharding import Mesh
from jax.sharding import PartitionSpec as P

HSIZE = 128
EHEADS = 4
CL = 64
NL = 128
NX = 4
LOG2E = math.log2(math.e)
BF16 = jnp.bfloat16
F32 = jnp.float32

NT = (((1,), (1,)), ((), ()))
TN = (((0,), (0,)), ((), ()))


def mm(a, b):
    return jnp.dot(a, b, preferred_element_type=F32)


def mm_nt(a, b):
    return lax.dot_general(a, b, NT, preferred_element_type=F32)


def mm_tn(a, b):
    return lax.dot_general(a, b, TN, preferred_element_type=F32)


def call(kernel, mib=58, **kw):
    return pl.pallas_call(
        kernel,
        compiler_params=pltpu.CompilerParams(vmem_limit_bytes=mib * 1024 * 1024),
        **kw,
    )


def smem():
    return pl.BlockSpec(memory_space=pltpu.SMEM)


def vmem():
    return pl.BlockSpec(memory_space=pltpu.VMEM)


def hbm():
    return pl.BlockSpec(memory_space=pl.ANY)


def pack_kernel(q_ref, k_ref, v_ref, out):
    for h in range(NX):
        cols = slice(h * HSIZE, (h + 1) * HSIZE)
        for i, src in enumerate((q_ref, k_ref, v_ref)):
            out[h, i] = src[:, cols]


def attend_kernel(pieces, kv_h, o0, o1, o2, o3, kv, acc, top, sems):
    loads = [pltpu.make_async_copy(kv_h.at[:, c], kv.at[:, c], sems.at[c]) for c in range(NX)]
    for c in loads:
        c.start()
    x = lax.axis_index("x")
    r = lax.axis_index("yl") * 2 + lax.axis_index("core")
    scale = LOG2E / math.sqrt(HSIZE)
    rows = pieces.shape[2]
    ones = jnp.ones((rows, HSIZE), BF16)
    for xq in range(NX):
        loads[xq].wait()
        q = pieces[xq, 0]

        def group(xk):
            scores = [mm_nt(q, kv[i, xk, 0]) for i in range(4)]
            if xk == xq:
                at = lax.broadcasted_iota(jnp.int32, (rows, rows), 1)
                upto = lax.broadcasted_iota(jnp.int32, (rows, rows), 0)
                scores = [
                    jnp.where(at + (i % 2 * 2 + i // 2) * rows <= upto + r * rows, s, -1e30)
                    for i, s in enumerate(scores)
                ]
            best = jnp.maximum(
                jnp.maximum(scores[0], scores[1]), jnp.maximum(scores[2], scores[3])
            )
            new = jnp.max(best, axis=-1, keepdims=True)
            if xk > 0:
                old = top[...]
                new = jnp.maximum(old, new)
            out = None
            for i, s in enumerate(scores):
                weights = jnp.exp2((s - new) * scale).astype(BF16)
                term = mm(weights, jnp.concatenate([kv[i, xk, 1], ones], axis=1))
                out = term if out is None else out + term
            if xk > 0:
                out = acc[...] * jnp.exp2((old - new) * scale) + out
            acc[...] = out
            top[...] = new

        for xk in range(xq + 1):
            group(xk)
        total = acc[...]
        result = (total[:, :HSIZE] / total[:, HSIZE:]).astype(BF16)
        for d, out in enumerate((o0, o1, o2, o3)):

            @pl.when(lax.rem(xq + d, NX) == x)
            def _():
                out[...] = result


def mix_kernel(s0, s1, s2, s3, cross, out):
    x = lax.axis_index("x")
    for d, piece in enumerate((s0, s1, s2, s3)):
        cols = pl.ds(pl.multiple_of(lax.rem(x + d, NX) * HSIZE, HSIZE), HSIZE)
        out[:, cols] = (piece[...].astype(F32) + cross[:, cols]).astype(BF16)


def head_rows(rows):
    width = rows.shape[1]
    each = width // EHEADS
    at = lax.broadcasted_iota(jnp.int32, (1, width), 1)
    parts = []
    for h in range(EHEADS):
        keep = jnp.where((at >= h * each) & (at < (h + 1) * each), 1.0, 0.0).astype(BF16)
        parts.append(rows * keep)
    return jnp.concatenate(parts, axis=0)


def encode_kernel(
    ids, nb_h, ctx_h, wq_h, wk_h, wv_h, wo_h, enc, wt, ek_out, ev_out, *scratch
):
    nb, ctx, wq, wk, wv, wo, sems = scratch
    both = ((nb_h, nb), (wq_h, wq), (ctx_h, ctx), (wk_h, wk), (wv_h, wv), (wo_h, wo))
    copies = [pltpu.make_async_copy(a, b, sems.at[i]) for i, (a, b) in enumerate(both)]
    for c in copies:
        c.start()
    slots, rows, width = nb.shape
    each = width // EHEADS
    copies[0].wait()
    x = nb[...].reshape(slots * rows, width)
    copies[1].wait()
    eq = mm(x, wq[...]).astype(BF16)
    copies[2].wait()
    contexts = []
    for t in range(slots):
        mine = (lax.axis_index("z") * 2 + lax.axis_index("yh")) * slots + t
        span = jnp.int32(0)
        for c in range(1, ids.shape[1]):
            span = jnp.where((ids[0, c] == mine) | (ids[1, c] == mine), c, span)
        contexts.append(ctx[pl.ds(pl.multiple_of(span * CL, CL), CL), :])
    m = jnp.concatenate(contexts, axis=0)
    copies[3].wait()
    ek = mm(m, wk[...]).astype(BF16)
    copies[4].wait()
    ev = mm(m, wv[...]).astype(BF16)
    mixed = []
    for t in range(slots):
        ek_t = ek[t * CL : (t + 1) * CL]
        ev_t = ev[t * CL : (t + 1) * CL]
        s = mm_nt(head_rows(ek_t), eq[t * rows : (t + 1) * rows]) * (1.0 / math.sqrt(each))
        s = s.reshape(EHEADS, CL, rows)
        p = jnp.exp(s - jnp.max(s, axis=1, keepdims=True))
        w = (p * (1.0 / jnp.sum(p, axis=1, keepdims=True))).reshape(EHEADS * CL, rows)
        wt[t] = w
        ek_out[t] = ek_t
        ev_out[t] = ev_t
        mixed.append(mm_tn(w.astype(BF16), head_rows(ev_t)).astype(BF16))
    copies[5].wait()
    out = x.astype(F32) + mm(jnp.concatenate(mixed, axis=0), wo[...])
    enc[...] = out.astype(BF16).reshape(slots, rows, width)


def pullback_kernel(*refs):
    given, out, here, sems = refs[:9], refs[9], refs[10:19], refs[19]
    d0, d1, d2, d3, wo, ev, wt, ek, wq = here
    loads = [pltpu.make_async_copy(a, b, sems.at[i]) for i, (a, b) in enumerate(zip(given, here))]
    for c in loads[:5]:
        c.start()
    slots, rows, width = d0.shape
    each = width // EHEADS
    for c in loads[:4]:
        c.wait()
    for c in loads[5:]:
        c.start()
    d = (d0[...].astype(F32) + d1[...].astype(F32)) + (d2[...].astype(F32) + d3[...].astype(F32))
    d = d.reshape(slots * rows, width)
    loads[4].wait()
    de = mm(d.astype(BF16), wo[...]).astype(BF16)
    for c in loads[5:8]:
        c.wait()
    back = []
    for t in range(slots):
        w = wt[t]
        dw = mm_nt(head_rows(ev[t]), de[t * rows : (t + 1) * rows])
        dw = dw.astype(BF16).astype(F32).reshape(EHEADS, CL, rows)
        w = w.reshape(EHEADS, CL, rows)
        ds = w * (dw - jnp.sum(w * dw, axis=1, keepdims=True)) * (1.0 / math.sqrt(each))
        ds = ds.reshape(EHEADS * CL, rows).astype(BF16)
        back.append(mm_tn(ds, head_rows(ek[t])).astype(BF16))
    loads[8].wait()
    out[...] = (d + mm(jnp.concatenate(back, axis=0), wq[...])).reshape(slots, rows, width)


def turn_kernel(kw, vw, wq, wo, kv_t, wq_t, wo_t):
    width = kw.shape[1]
    kv_t[:width] = kw[...].T
    kv_t[width:] = vw[...].T
    wq_t[...] = wq[...].T
    wo_t[...] = wo[...].T


def blocks_kernel(q, g, qm_t, gm_t):
    for c in range(qm_t.shape[0]):
        qm_t[c] = head_blocks(q[c * CL : (c + 1) * CL]).T
        gm_t[c] = head_blocks(g[c * CL : (c + 1) * CL]).T


def head_blocks(rows):
    width = rows.shape[1]
    at = lax.broadcasted_iota(jnp.int32, (1, width), 1)
    parts = []
    for h in range(width // HSIZE):
        keep = jnp.where((at >= h * HSIZE) & (at < (h + 1) * HSIZE), 1.0, 0.0).astype(BF16)
        parts.append(rows * keep)
    return jnp.concatenate(parts, axis=0)


def cross_kernel(ids, e00, e01, e10, e11, e20, e21, e30, e31, *rest):
    blocks = (e00, e01, e10, e11, e20, e21, e30, e31)
    given, cross, outs = rest[:7], rest[7], rest[8:16]
    table, held, sent, ckv, dkv, zero, in_sem, out_sem, given_sem, mine, mine_sem = rest[16:27]
    kvw, qm_t, gm_t, q, g, kv_t = rest[27:]
    width = q.shape[1]
    here = (kvw.at[:, :width], kvw.at[:, width:], qm_t, gm_t, q, g, kv_t)
    loads = [
        pltpu.make_async_copy(a, b, given_sem.at[i]) for i, (a, b) in enumerate(zip(given, here))
    ]
    loads[0].start()
    loads[1].start()
    z, yh = lax.axis_index("z"), lax.axis_index("yh")
    n_named = held.shape[0]
    spans = n_named // 2
    scale = 1.0 / math.sqrt(HSIZE)

    for i in range(16):
        table[i] = jnp.int32(-1)
    for n in range(n_named):
        slot = ids[n % 2, n // 2]
        dz = lax.rem(slot // 4 - z + NX, NX)
        dy = jnp.bitwise_xor(lax.rem(slot // 2, 2), yh)
        table[dz * 4 + dy * 2 + lax.rem(slot, 2)] = jnp.int32(n)
    zero[...] = jnp.zeros_like(zero)
    places = [4, 5, 0, 1, 2, 3, 6, 7]
    places = [(i, t) for i in places for t in range(2)]
    for i, t in places:
        n = table[2 * i + t]

        @pl.when(n >= 0)
        def _():
            pltpu.make_async_copy(blocks[i].at[t], held.at[n], in_sem.at[n]).start()

    for i, t in places:

        @pl.when(table[2 * i + t] < 0)
        def _():
            pltpu.make_async_copy(zero, outs[i].at[t], out_sem.at[2 * i + t]).start()

    heads = width // HSIZE
    pair = 2 * NL
    for half in range(2):
        first = half * (n_named // 2)
        for n in range(first, first + n_named // 2):
            pltpu.make_async_copy(e00.at[0], held.at[n], in_sem.at[n]).wait()
        e = held[first : first + n_named // 2].reshape(n_named // 2 * NL, -1)
        if half == 0:
            loads[0].wait()
            loads[1].wait()
            for c in loads[2:]:
                c.start()
        ckv[first * NL : (first + n_named // 2) * NL] = mm(e, kvw[...]).astype(BF16)
    for c in loads[2:]:
        c.wait()

    def scores(c):
        at = slice(c * pair, (c + 1) * pair)
        return mm(ckv[at, :width], qm_t[c]), mm(ckv[at, width:], gm_t[c])

    def soften(s, dp):
        p = jnp.exp2((s - jnp.max(s, axis=0, keepdims=True)) * (scale * LOG2E))
        p = p * (1.0 / jnp.sum(p, axis=0, keepdims=True))
        ds = p * ((dp - jnp.sum(p * dp, axis=0, keepdims=True)) * scale)
        return p.astype(BF16), ds.astype(BF16)

    def products(c, pb, ds):
        at = slice(c * pair, (c + 1) * pair)
        dkv[at, :width] = mm(ds, head_blocks(q[c * CL : (c + 1) * CL])).astype(BF16)
        dkv[at, width:] = mm(pb, head_blocks(g[c * CL : (c + 1) * CL])).astype(BF16)
        pt = pb.T
        for h in range(heads):
            cols = slice(h * HSIZE, (h + 1) * HSIZE)
            mine[c * CL : (c + 1) * CL, cols] = mm(
                pt[h * CL : (h + 1) * CL], ckv[at, width + h * HSIZE : width + (h + 1) * HSIZE]
            )

    def back(c):
        at = slice(c * pair, (c + 1) * pair)
        sent[2 * c : 2 * c + 2] = mm(dkv[at], kv_t[...]).astype(BF16).reshape(2, NL, -1)

    def send(low, high):
        for i, t in places:
            n = table[2 * i + t]

            @pl.when((n >= low) & (n < high))
            def _():
                pltpu.make_async_copy(sent.at[n], outs[i].at[t], out_sem.at[2 * i + t]).start()

    ahead = scores(0)
    for c in range(spans):
        now = ahead
        if c + 1 < spans:
            ahead = scores(c + 1)
        soft = soften(*now)
        if c >= 1:
            back(c - 1)
        products(c, *soft)
    leave = pltpu.make_async_copy(mine, cross, mine_sem)
    leave.start()
    send(0, n_named - 2)
    back(spans - 1)
    send(n_named - 2, n_named)
    leave.wait()
    for i, t in places:
        pltpu.make_async_copy(zero, outs[i].at[t], out_sem.at[2 * i + t]).wait()


def shift(n, by):
    return [(i, (i + by) % n) for i in range(n)]


def local(
    self_q,
    self_k,
    self_v,
    cross_q,
    cross_k_weight,
    cross_v_weight,
    span_ctx,
    neighbours,
    neighbour_ids,
    enc_q,
    enc_k,
    enc_v,
    enc_o,
    mixed_grad,
):
    rows, width = self_q.shape
    slots, nl, ew = neighbours.shape
    spans, per_span = neighbour_ids.shape
    n_named = spans * per_span
    struct = jax.ShapeDtypeStruct
    after = lax.optimization_barrier

    ids = neighbour_ids.T

    e00, wt, ek, ev = call(
        encode_kernel,
        out_shape=[
            struct((slots, nl, ew), BF16),
            struct((slots, EHEADS * CL, nl), F32),
            struct((slots, CL, ew), BF16),
            struct((slots, CL, ew), BF16),
        ],
        in_specs=[smem()] + [hbm()] * 6,
        out_specs=[vmem()] * 4,
        scratch_shapes=[pltpu.VMEM(neighbours.shape, BF16), pltpu.VMEM(span_ctx.shape, BF16)]
        + [pltpu.VMEM((ew, ew), BF16)] * 4
        + [pltpu.SemaphoreType.DMA((6,))],
    )(ids, neighbours, span_ctx, enc_q, enc_k, enc_v, enc_o)

    e01 = lax.ppermute(e00, "yh", shift(2, 1))
    e30 = lax.ppermute(e00, "z", shift(NX, 1))
    e10 = lax.ppermute(e00, "z", shift(NX, -1))

    self_q, self_k, self_v, _ = after((self_q, self_k, self_v, wt))
    packed = call(
        pack_kernel,
        out_shape=struct((NX, 3, rows, HSIZE), BF16),
        in_specs=[vmem()] * 3,
        out_specs=vmem(),
    )(self_q, self_k, self_v)
    pieces = lax.all_to_all(packed, "x", 0, 0)

    e01, e30, e10, packed = after((e01, e30, e10, packed))
    e11 = lax.ppermute(e01, "z", shift(NX, -1))
    e31 = lax.ppermute(e01, "z", shift(NX, 1))


    weights = after((cross_k_weight, cross_v_weight, enc_q, enc_o, e01))[:4]
    turned = call(
        turn_kernel,
        out_shape=[struct((2 * width, ew), BF16)] + [struct((ew, ew), BF16)] * 2,
        in_specs=[vmem()] * 4,
        out_specs=[vmem()] * 3,
    )(*weights)

    own_kv = pieces[:, 1:]
    e30, e11, e31, own_kv, *turned = after((e30, e11, e31, own_kv, *turned))
    half_kv = lax.all_gather(own_kv, "yl", axis=0)
    kv_t, wq_t, wo_t = turned
    e20 = lax.ppermute(e30, "z", shift(NX, 1))
    e21 = lax.ppermute(e11, "z", shift(NX, -1))

    half_kv, _ = after((half_kv, e20))
    kv = lax.all_gather(half_kv, "core", axis=0).reshape((4,) + own_kv.shape)

    queries, grads, _ = after((cross_q, mixed_grad, e11))
    qm_t, gm_t = call(
        blocks_kernel,
        out_shape=[struct((spans, width, width // HSIZE * CL), BF16)] * 2,
        in_specs=[vmem()] * 2,
        out_specs=[vmem()] * 2,
    )(queries, grads)

    cross, *p = call(
        cross_kernel,
        out_shape=[struct((rows, width), F32)] + [struct((slots, nl, ew), BF16)] * 8,
        in_specs=[smem()] + [hbm()] * 15,
        out_specs=[hbm()] * 9,
        scratch_shapes=[
            pltpu.SMEM((16,), jnp.int32),
            pltpu.VMEM((n_named, nl, ew), BF16),
            pltpu.VMEM((n_named, nl, ew), BF16),
            pltpu.VMEM((n_named * nl, 2 * width), BF16),
            pltpu.VMEM((n_named * nl, 2 * width), BF16),
            pltpu.VMEM((nl, ew), BF16),
            pltpu.SemaphoreType.DMA((n_named,)),
            pltpu.SemaphoreType.DMA((16,)),
            pltpu.SemaphoreType.DMA((7,)),
            pltpu.VMEM((rows, width), F32),
            pltpu.SemaphoreType.DMA,
            pltpu.VMEM((ew, 2 * width), BF16),
        ]
        + [pltpu.VMEM((spans, width, width // HSIZE * CL), BF16)] * 2
        + [pltpu.VMEM((rows, width), BF16)] * 2
        + [pltpu.VMEM((2 * width, ew), BF16)],
    )(
        ids,
        e00,
        e01,
        e10,
        e11,
        e20,
        e21,
        e30,
        e31,
        cross_k_weight,
        cross_v_weight,
        qm_t,
        gm_t,
        cross_q,
        mixed_grad,
        kv_t,
    )
    p00, p01, p10, p11, p20, p21, p30, p31 = p

    def add(a, b):
        return (a.astype(F32) + b.astype(F32)).astype(BF16)

    far1 = lax.ppermute(p21, "z", shift(NX, -1))
    far0 = lax.ppermute(p20, "z", shift(NX, 1))
    kv, _ = after((kv, cross))
    outs = call(
        attend_kernel,
        out_shape=[struct((rows, HSIZE), BF16)] * NX,
        in_specs=[vmem(), hbm()],
        out_specs=[vmem()] * NX,
        scratch_shapes=[
            pltpu.VMEM(kv.shape, BF16),
            pltpu.VMEM((rows, 2 * HSIZE), F32),
            pltpu.VMEM((rows, 1), F32),
            pltpu.SemaphoreType.DMA((NX,)),
        ],
    )(pieces, kv)
    far1, far0, p11, *outs = after((far1, far0, p11, *outs))
    selfs = [outs[0]] + [lax.ppermute(outs[d], "x", shift(NX, -d)) for d in range(1, NX)]
    down1 = lax.ppermute(add(p31, far1), "z", shift(NX, -1))
    up1 = lax.ppermute(p11, "z", shift(NX, 1))
    near0 = add(p10, far0)
    down1, up1, near0, p30, *selfs = after((down1, up1, near0, p30, *selfs))
    theirs = (p01.astype(F32) + up1.astype(F32) + down1.astype(F32)).astype(BF16)
    other = lax.ppermute(theirs, "yh", shift(2, 1))
    up0 = lax.ppermute(near0, "z", shift(NX, 1))
    down0 = lax.ppermute(p30, "z", shift(NX, -1))

    grad = call(
        pullback_kernel,
        out_shape=struct((slots, nl, ew), F32),
        in_specs=[hbm()] * 9,
        out_specs=vmem(),
        scratch_shapes=[pltpu.VMEM((slots, nl, ew), BF16)] * 4
        + [
            pltpu.VMEM((ew, ew), BF16),
            pltpu.VMEM(ev.shape, BF16),
            pltpu.VMEM(wt.shape, F32),
            pltpu.VMEM(ek.shape, BF16),
            pltpu.VMEM((ew, ew), BF16),
            pltpu.SemaphoreType.DMA((9,)),
        ],
    )(p00, up0, down0, other, wo_t, ev, wt, ek, wq_t)

    mixed = call(
        mix_kernel,
        out_shape=struct((rows, width), BF16),
        in_specs=[vmem()] * 5,
        out_specs=vmem(),
    )(*selfs, cross)
    return mixed, grad


def solution(mesh):
    fine = Mesh(mesh.devices.reshape(4, 2, 2, 4, 2), ("x", "yl", "core", "z", "yh"))
    ctx, enc = ("x", "yl", "core"), ("z", "yh")
    tokens = P(ctx, enc)
    return jax.shard_map(
        local,
        mesh=fine,
        in_specs=(
            tokens,
            tokens,
            tokens,
            tokens,
            P(None, enc),
            P(None, enc),
            P(ctx, None),
            P(ctx + enc, None, None),
            P(ctx, None),
            P(),
            P(),
            P(),
            P(),
            tokens,
        ),
        out_specs=(tokens, P(ctx + enc, None, None)),
        check_vma=False,
    )
```

```python
import math

import jax
import jax.numpy as jnp
from jax import lax
from jax.experimental import pallas as pl
from jax.experimental.pallas import tpu as pltpu
from jax.sharding import Mesh
from jax.sharding import PartitionSpec as P

HSIZE = 128
EHEADS = 4
CL = 64
NL = 128
NX = 4
LOG2E = math.log2(math.e)
BF16 = jnp.bfloat16
F32 = jnp.float32

NT = (((1,), (1,)), ((), ()))
TN = (((0,), (0,)), ((), ()))


def mm(a, b):
    return jnp.dot(a, b, preferred_element_type=F32)


def mm_nt(a, b):
    return lax.dot_general(a, b, NT, preferred_element_type=F32)


def mm_tn(a, b):
    return lax.dot_general(a, b, TN, preferred_element_type=F32)


def call(kernel, mib=58, **kw):
    return pl.pallas_call(
        kernel,
        compiler_params=pltpu.CompilerParams(vmem_limit_bytes=mib * 1024 * 1024),
        **kw,
    )


def smem():
    return pl.BlockSpec(memory_space=pltpu.SMEM)


def vmem():
    return pl.BlockSpec(memory_space=pltpu.VMEM)


def hbm():
    return pl.BlockSpec(memory_space=pl.ANY)


def pack_kernel(q_ref, k_ref, v_ref, out):
    for h in range(NX):
        cols = slice(h * HSIZE, (h + 1) * HSIZE)
        for i, src in enumerate((q_ref, k_ref, v_ref)):
            out[h, i] = src[:, cols]


def attend_kernel(pieces, kv0, kv1, kv2, kv3, o0, o1, o2, o3, kv, acc, top, sems):
    loads = [
        [
            pltpu.make_async_copy(a.at[c], kv.at[i, c], sems.at[c, i])
            for i, a in enumerate((kv0, kv1, kv2, kv3))
        ]
        for c in range(NX)
    ]
    for chunk in loads:
        for c in chunk:
            c.start()
    x = lax.axis_index("x")
    r = lax.axis_index("yl") * 2 + lax.axis_index("core")
    scale = LOG2E / math.sqrt(HSIZE)
    rows = pieces.shape[2]
    ones = jnp.ones((rows, HSIZE), BF16)
    for xq in range(NX):
        for c in loads[xq]:
            c.wait()
        q = pieces[xq, 0]

        def group(xk):
            scores = [mm_nt(q, kv[i, xk, 0]) for i in range(4)]
            if xk == xq:
                at = lax.broadcasted_iota(jnp.int32, (rows, rows), 1)
                upto = lax.broadcasted_iota(jnp.int32, (rows, rows), 0)
                scores = [
                    jnp.where(at + jnp.bitwise_xor(r, i) * rows <= upto + r * rows, s, -1e30)
                    for i, s in enumerate(scores)
                ]
            best = jnp.maximum(
                jnp.maximum(scores[0], scores[1]), jnp.maximum(scores[2], scores[3])
            )
            new = jnp.max(best, axis=-1, keepdims=True)
            if xk > 0:
                old = top[...]
                new = jnp.maximum(old, new)
            out = None
            for i, s in enumerate(scores):
                weights = jnp.exp2((s - new) * scale).astype(BF16)
                term = mm(weights, jnp.concatenate([kv[i, xk, 1], ones], axis=1))
                out = term if out is None else out + term
            if xk > 0:
                out = acc[...] * jnp.exp2((old - new) * scale) + out
            acc[...] = out
            top[...] = new

        for xk in range(xq + 1):
            group(xk)
        total = acc[...]
        result = (total[:, :HSIZE] / total[:, HSIZE:]).astype(BF16)
        for d, out in enumerate((o0, o1, o2, o3)):

            @pl.when(lax.rem(xq + d, NX) == x)
            def _():
                out[...] = result


def mix_kernel(s0, s1, s2, s3, cross, out):
    x = lax.axis_index("x")
    for d, piece in enumerate((s0, s1, s2, s3)):
        cols = pl.ds(pl.multiple_of(lax.rem(x + d, NX) * HSIZE, HSIZE), HSIZE)
        out[:, cols] = (piece[...].astype(F32) + cross[:, cols]).astype(BF16)


def head_rows(rows):
    width = rows.shape[1]
    each = width // EHEADS
    at = lax.broadcasted_iota(jnp.int32, (1, width), 1)
    parts = []
    for h in range(EHEADS):
        keep = jnp.where((at >= h * each) & (at < (h + 1) * each), 1.0, 0.0).astype(BF16)
        parts.append(rows * keep)
    return jnp.concatenate(parts, axis=0)


def encode_kernel(
    ids, nb_h, ctx_h, wq_h, wk_h, wv_h, wo_h, enc, wt, ek_out, ev_out, *scratch
):
    nb, ctx, wq, wk, wv, wo, sems = scratch
    both = ((nb_h, nb), (wq_h, wq), (ctx_h, ctx), (wk_h, wk), (wv_h, wv), (wo_h, wo))
    copies = [pltpu.make_async_copy(a, b, sems.at[i]) for i, (a, b) in enumerate(both)]
    for c in copies:
        c.start()
    slots, rows, width = nb.shape
    each = width // EHEADS
    copies[0].wait()
    x = nb[...].reshape(slots * rows, width)
    copies[1].wait()
    eq = mm(x, wq[...]).astype(BF16)
    copies[2].wait()
    contexts = []
    for t in range(slots):
        mine = (lax.axis_index("z") * 2 + lax.axis_index("yh")) * slots + t
        span = jnp.int32(0)
        for c in range(1, ids.shape[1]):
            span = jnp.where((ids[0, c] == mine) | (ids[1, c] == mine), c, span)
        contexts.append(ctx[pl.ds(pl.multiple_of(span * CL, CL), CL), :])
    m = jnp.concatenate(contexts, axis=0)
    copies[3].wait()
    ek = mm(m, wk[...]).astype(BF16)
    copies[4].wait()
    ev = mm(m, wv[...]).astype(BF16)
    mixed = []
    for t in range(slots):
        ek_t = ek[t * CL : (t + 1) * CL]
        ev_t = ev[t * CL : (t + 1) * CL]
        s = mm_nt(head_rows(ek_t), eq[t * rows : (t + 1) * rows]) * (1.0 / math.sqrt(each))
        s = s.reshape(EHEADS, CL, rows)
        p = jnp.exp(s - jnp.max(s, axis=1, keepdims=True))
        w = (p * (1.0 / jnp.sum(p, axis=1, keepdims=True))).reshape(EHEADS * CL, rows)
        wt[t] = w
        ek_out[t] = ek_t
        ev_out[t] = ev_t
        mixed.append(mm_tn(w.astype(BF16), head_rows(ev_t)).astype(BF16))
    copies[5].wait()
    out = x.astype(F32) + mm(jnp.concatenate(mixed, axis=0), wo[...])
    enc[...] = out.astype(BF16).reshape(slots, rows, width)


def pullback_kernel(*refs):
    given, out, here, sems = refs[:9], refs[9], refs[10:19], refs[19]
    d0, d1, d2, d3, wo, ev, wt, ek, wq = here
    loads = [pltpu.make_async_copy(a, b, sems.at[i]) for i, (a, b) in enumerate(zip(given, here))]
    for c in loads[:5]:
        c.start()
    slots, rows, width = d0.shape
    each = width // EHEADS
    for c in loads[:4]:
        c.wait()
    for c in loads[5:]:
        c.start()
    d = (d0[...].astype(F32) + d1[...].astype(F32)) + (d2[...].astype(F32) + d3[...].astype(F32))
    d = d.reshape(slots * rows, width)
    loads[4].wait()
    de = mm(d.astype(BF16), wo[...]).astype(BF16)
    for c in loads[5:8]:
        c.wait()
    back = []
    for t in range(slots):
        w = wt[t]
        dw = mm_nt(head_rows(ev[t]), de[t * rows : (t + 1) * rows])
        dw = dw.astype(BF16).astype(F32).reshape(EHEADS, CL, rows)
        w = w.reshape(EHEADS, CL, rows)
        ds = w * (dw - jnp.sum(w * dw, axis=1, keepdims=True)) * (1.0 / math.sqrt(each))
        ds = ds.reshape(EHEADS * CL, rows).astype(BF16)
        back.append(mm_tn(ds, head_rows(ek[t])).astype(BF16))
    loads[8].wait()
    out[...] = (d + mm(jnp.concatenate(back, axis=0), wq[...])).reshape(slots, rows, width)


def turn_kernel(kw, vw, wq, wo, kv_t, wq_t, wo_t):
    width = kw.shape[1]
    kv_t[:width] = kw[...].T
    kv_t[width:] = vw[...].T
    wq_t[...] = wq[...].T
    wo_t[...] = wo[...].T


def blocks_kernel(q, g, qm_t, gm_t):
    for c in range(qm_t.shape[0]):
        qm_t[c] = head_blocks(q[c * CL : (c + 1) * CL]).T
        gm_t[c] = head_blocks(g[c * CL : (c + 1) * CL]).T


def head_blocks(rows):
    width = rows.shape[1]
    at = lax.broadcasted_iota(jnp.int32, (1, width), 1)
    parts = []
    for h in range(width // HSIZE):
        keep = jnp.where((at >= h * HSIZE) & (at < (h + 1) * HSIZE), 1.0, 0.0).astype(BF16)
        parts.append(rows * keep)
    return jnp.concatenate(parts, axis=0)


def cross_kernel(ids, e00, e01, e10, e11, e20, e21, e30, e31, *rest):
    blocks = (e00, e01, e10, e11, e20, e21, e30, e31)
    given, cross, outs = rest[:7], rest[7], rest[8:16]
    table, held, sent, ckv, dkv, zero, in_sem, out_sem, given_sem, mine, mine_sem = rest[16:27]
    kvw, qm_t, gm_t, q, g, kv_t = rest[27:]
    width = q.shape[1]
    here = (kvw.at[:, :width], kvw.at[:, width:], qm_t, gm_t, q, g, kv_t)
    loads = [
        pltpu.make_async_copy(a, b, given_sem.at[i]) for i, (a, b) in enumerate(zip(given, here))
    ]
    loads[0].start()
    loads[1].start()
    z, yh = lax.axis_index("z"), lax.axis_index("yh")
    n_named = held.shape[0]
    spans = n_named // 2
    scale = 1.0 / math.sqrt(HSIZE)

    for i in range(16):
        table[i] = jnp.int32(-1)
    for n in range(n_named):
        slot = ids[n % 2, n // 2]
        dz = lax.rem(slot // 4 - z + NX, NX)
        dy = jnp.bitwise_xor(lax.rem(slot // 2, 2), yh)
        table[dz * 4 + dy * 2 + lax.rem(slot, 2)] = jnp.int32(n)
    zero[...] = jnp.zeros_like(zero)
    places = [4, 5, 0, 1, 2, 3, 6, 7]
    places = [(i, t) for i in places for t in range(2)]
    for i, t in places:
        n = table[2 * i + t]

        @pl.when(n >= 0)
        def _():
            pltpu.make_async_copy(blocks[i].at[t], held.at[n], in_sem.at[n]).start()

    for i, t in places:

        @pl.when(table[2 * i + t] < 0)
        def _():
            pltpu.make_async_copy(zero, outs[i].at[t], out_sem.at[2 * i + t]).start()

    heads = width // HSIZE
    pair = 2 * NL
    for half in range(2):
        first = half * (n_named // 2)
        for n in range(first, first + n_named // 2):
            pltpu.make_async_copy(e00.at[0], held.at[n], in_sem.at[n]).wait()
        e = held[first : first + n_named // 2].reshape(n_named // 2 * NL, -1)
        if half == 0:
            loads[0].wait()
            loads[1].wait()
            for c in loads[2:]:
                c.start()
        ckv[first * NL : (first + n_named // 2) * NL] = mm(e, kvw[...]).astype(BF16)
    for c in loads[2:]:
        c.wait()

    def scores(c):
        at = slice(c * pair, (c + 1) * pair)
        return mm(ckv[at, :width], qm_t[c]), mm(ckv[at, width:], gm_t[c])

    def soften(s, dp):
        p = jnp.exp2((s - jnp.max(s, axis=0, keepdims=True)) * (scale * LOG2E))
        p = p * (1.0 / jnp.sum(p, axis=0, keepdims=True))
        ds = p * ((dp - jnp.sum(p * dp, axis=0, keepdims=True)) * scale)
        return p.astype(BF16), ds.astype(BF16)

    def products(c, pb, ds):
        at = slice(c * pair, (c + 1) * pair)
        dkv[at, :width] = mm(ds, head_blocks(q[c * CL : (c + 1) * CL])).astype(BF16)
        dkv[at, width:] = mm(pb, head_blocks(g[c * CL : (c + 1) * CL])).astype(BF16)
        pt = pb.T
        for h in range(heads):
            cols = slice(h * HSIZE, (h + 1) * HSIZE)
            mine[c * CL : (c + 1) * CL, cols] = mm(
                pt[h * CL : (h + 1) * CL], ckv[at, width + h * HSIZE : width + (h + 1) * HSIZE]
            )

    def back(c):
        at = slice(c * pair, (c + 1) * pair)
        sent[2 * c : 2 * c + 2] = mm(dkv[at], kv_t[...]).astype(BF16).reshape(2, NL, -1)

    def send(low, high):
        for i, t in places:
            n = table[2 * i + t]

            @pl.when((n >= low) & (n < high))
            def _():
                pltpu.make_async_copy(sent.at[n], outs[i].at[t], out_sem.at[2 * i + t]).start()

    ahead = scores(0)
    for c in range(spans):
        now = ahead
        if c + 1 < spans:
            ahead = scores(c + 1)
        soft = soften(*now)
        if c >= 1:
            back(c - 1)
        products(c, *soft)
    leave = pltpu.make_async_copy(mine, cross, mine_sem)
    leave.start()
    send(0, n_named - 2)
    back(spans - 1)
    send(n_named - 2, n_named)
    leave.wait()
    for i, t in places:
        pltpu.make_async_copy(zero, outs[i].at[t], out_sem.at[2 * i + t]).wait()


def shift(n, by):
    return [(i, (i + by) % n) for i in range(n)]


def local(
    self_q,
    self_k,
    self_v,
    cross_q,
    cross_k_weight,
    cross_v_weight,
    span_ctx,
    neighbours,
    neighbour_ids,
    enc_q,
    enc_k,
    enc_v,
    enc_o,
    mixed_grad,
):
    rows, width = self_q.shape
    slots, nl, ew = neighbours.shape
    spans, per_span = neighbour_ids.shape
    n_named = spans * per_span
    struct = jax.ShapeDtypeStruct
    after = lax.optimization_barrier

    ids = neighbour_ids.T

    e00, wt, ek, ev = call(
        encode_kernel,
        out_shape=[
            struct((slots, nl, ew), BF16),
            struct((slots, EHEADS * CL, nl), F32),
            struct((slots, CL, ew), BF16),
            struct((slots, CL, ew), BF16),
        ],
        in_specs=[smem()] + [hbm()] * 6,
        out_specs=[vmem()] * 4,
        scratch_shapes=[pltpu.VMEM(neighbours.shape, BF16), pltpu.VMEM(span_ctx.shape, BF16)]
        + [pltpu.VMEM((ew, ew), BF16)] * 4
        + [pltpu.SemaphoreType.DMA((6,))],
    )(ids, neighbours, span_ctx, enc_q, enc_k, enc_v, enc_o)

    e01 = lax.ppermute(e00, "yh", shift(2, 1))
    e30 = lax.ppermute(e00, "z", shift(NX, 1))
    e10 = lax.ppermute(e00, "z", shift(NX, -1))

    self_q, self_k, self_v, _ = after((self_q, self_k, self_v, wt))
    packed = call(
        pack_kernel,
        out_shape=struct((NX, 3, rows, HSIZE), BF16),
        in_specs=[vmem()] * 3,
        out_specs=vmem(),
    )(self_q, self_k, self_v)
    pieces = lax.all_to_all(packed, "x", 0, 0)

    e01, e30, e10, packed = after((e01, e30, e10, packed))
    e11 = lax.ppermute(e01, "z", shift(NX, -1))
    e31 = lax.ppermute(e01, "z", shift(NX, 1))


    weights = after((cross_k_weight, cross_v_weight, enc_q, enc_o, e01))[:4]
    turned = call(
        turn_kernel,
        out_shape=[struct((2 * width, ew), BF16)] + [struct((ew, ew), BF16)] * 2,
        in_specs=[vmem()] * 4,
        out_specs=[vmem()] * 3,
    )(*weights)

    own_kv = pieces[:, 1:]
    e30, e11, e31, own_kv, *turned = after((e30, e11, e31, own_kv, *turned))
    swap = [(0, 3), (1, 2), (2, 1), (3, 0)]
    kvs = [
        own_kv,
        lax.ppermute(own_kv, "core", shift(2, 1)),
        lax.ppermute(own_kv, "yl", shift(2, 1)),
        lax.ppermute(own_kv, ("yl", "core"), swap),
    ]
    kv_t, wq_t, wo_t = turned
    e20 = lax.ppermute(e30, "z", shift(NX, 1))
    e21 = lax.ppermute(e11, "z", shift(NX, -1))

    queries, grads, _ = after((cross_q, mixed_grad, e11))
    qm_t, gm_t = call(
        blocks_kernel,
        out_shape=[struct((spans, width, width // HSIZE * CL), BF16)] * 2,
        in_specs=[vmem()] * 2,
        out_specs=[vmem()] * 2,
    )(queries, grads)

    cross, *p = call(
        cross_kernel,
        out_shape=[struct((rows, width), F32)] + [struct((slots, nl, ew), BF16)] * 8,
        in_specs=[smem()] + [hbm()] * 15,
        out_specs=[hbm()] * 9,
        scratch_shapes=[
            pltpu.SMEM((16,), jnp.int32),
            pltpu.VMEM((n_named, nl, ew), BF16),
            pltpu.VMEM((n_named, nl, ew), BF16),
            pltpu.VMEM((n_named * nl, 2 * width), BF16),
            pltpu.VMEM((n_named * nl, 2 * width), BF16),
            pltpu.VMEM((nl, ew), BF16),
            pltpu.SemaphoreType.DMA((n_named,)),
            pltpu.SemaphoreType.DMA((16,)),
            pltpu.SemaphoreType.DMA((7,)),
            pltpu.VMEM((rows, width), F32),
            pltpu.SemaphoreType.DMA,
            pltpu.VMEM((ew, 2 * width), BF16),
        ]
        + [pltpu.VMEM((spans, width, width // HSIZE * CL), BF16)] * 2
        + [pltpu.VMEM((rows, width), BF16)] * 2
        + [pltpu.VMEM((2 * width, ew), BF16)],
    )(
        ids,
        e00,
        e01,
        e10,
        e11,
        e20,
        e21,
        e30,
        e31,
        cross_k_weight,
        cross_v_weight,
        qm_t,
        gm_t,
        cross_q,
        mixed_grad,
        kv_t,
    )
    p00, p01, p10, p11, p20, p21, p30, p31 = p

    def add(a, b):
        return (a.astype(F32) + b.astype(F32)).astype(BF16)

    far1 = lax.ppermute(p21, "z", shift(NX, -1))
    far0 = lax.ppermute(p20, "z", shift(NX, 1))
    *kvs, _ = after((*kvs, cross))
    outs = call(
        attend_kernel,
        out_shape=[struct((rows, HSIZE), BF16)] * NX,
        in_specs=[vmem()] + [hbm()] * 4,
        out_specs=[vmem()] * NX,
        scratch_shapes=[
            pltpu.VMEM((4,) + own_kv.shape, BF16),
            pltpu.VMEM((rows, 2 * HSIZE), F32),
            pltpu.VMEM((rows, 1), F32),
            pltpu.SemaphoreType.DMA((NX, 4)),
        ],
    )(pieces, *kvs)
    far1, far0, p11, *outs = after((far1, far0, p11, *outs))
    selfs = [outs[0]] + [lax.ppermute(outs[d], "x", shift(NX, -d)) for d in range(1, NX)]
    down1 = lax.ppermute(add(p31, far1), "z", shift(NX, -1))
    up1 = lax.ppermute(p11, "z", shift(NX, 1))
    near0 = add(p10, far0)
    down1, up1, near0, p30, *selfs = after((down1, up1, near0, p30, *selfs))
    theirs = (p01.astype(F32) + up1.astype(F32) + down1.astype(F32)).astype(BF16)
    other = lax.ppermute(theirs, "yh", shift(2, 1))
    up0 = lax.ppermute(near0, "z", shift(NX, 1))
    down0 = lax.ppermute(p30, "z", shift(NX, -1))

    grad = call(
        pullback_kernel,
        out_shape=struct((slots, nl, ew), F32),
        in_specs=[hbm()] * 9,
        out_specs=vmem(),
        scratch_shapes=[pltpu.VMEM((slots, nl, ew), BF16)] * 4
        + [
            pltpu.VMEM((ew, ew), BF16),
            pltpu.VMEM(ev.shape, BF16),
            pltpu.VMEM(wt.shape, F32),
            pltpu.VMEM(ek.shape, BF16),
            pltpu.VMEM((ew, ew), BF16),
            pltpu.SemaphoreType.DMA((9,)),
        ],
    )(p00, up0, down0, other, wo_t, ev, wt, ek, wq_t)

    mixed = call(
        mix_kernel,
        out_shape=struct((rows, width), BF16),
        in_specs=[vmem()] * 5,
        out_specs=vmem(),
    )(*selfs, cross)
    return mixed, grad


def solution(mesh):
    fine = Mesh(mesh.devices.reshape(4, 2, 2, 4, 2), ("x", "yl", "core", "z", "yh"))
    ctx, enc = ("x", "yl", "core"), ("z", "yh")
    tokens = P(ctx, enc)
    return jax.shard_map(
        local,
        mesh=fine,
        in_specs=(
            tokens,
            tokens,
            tokens,
            tokens,
            P(None, enc),
            P(None, enc),
            P(ctx, None),
            P(ctx + enc, None, None),
            P(ctx, None),
            P(),
            P(),
            P(),
            P(),
            tokens,
        ),
        out_specs=(tokens, P(ctx + enc, None, None)),
        check_vma=False,
    )
```

```python
import math

import jax
import jax.numpy as jnp
from jax import lax
from jax.experimental import pallas as pl
from jax.experimental.pallas import tpu as pltpu
from jax.sharding import Mesh
from jax.sharding import PartitionSpec as P

HSIZE = 128
EHEADS = 4
CL = 64
NL = 128
NX = 4
LOG2E = math.log2(math.e)
BF16 = jnp.bfloat16
F32 = jnp.float32

NT = (((1,), (1,)), ((), ()))
TN = (((0,), (0,)), ((), ()))


def mm(a, b):
    return jnp.dot(a, b, preferred_element_type=F32)


def mm_nt(a, b):
    return lax.dot_general(a, b, NT, preferred_element_type=F32)


def mm_tn(a, b):
    return lax.dot_general(a, b, TN, preferred_element_type=F32)


def call(kernel, mib=24, **kw):
    return pl.pallas_call(
        kernel,
        compiler_params=pltpu.CompilerParams(vmem_limit_bytes=mib * 1024 * 1024),
        **kw,
    )


def smem():
    return pl.BlockSpec(memory_space=pltpu.SMEM)


def vmem():
    return pl.BlockSpec(memory_space=pltpu.VMEM)


def anywhere():
    return pl.BlockSpec(memory_space=pl.ANY)


def hbm():
    return pl.BlockSpec(memory_space=pltpu.HBM)


def pack_kernel(q_ref, k_ref, v_ref, out):
    for h in range(NX):
        cols = slice(h * HSIZE, (h + 1) * HSIZE)
        for i, src in enumerate((q_ref, k_ref, v_ref)):
            out[h, i] = src[:, cols]


def attend_kernel(pieces, kv0, kv1, kv2, kv3, o0, o1, o2, o3, acc, top):
    kv = (kv0, kv1, kv2, kv3)
    x = lax.axis_index("x")
    r = lax.axis_index("yl") * 2 + lax.axis_index("core")
    scale = LOG2E / math.sqrt(HSIZE)
    rows = pieces.shape[2]
    ones = jnp.ones((rows, HSIZE), BF16)
    for xq in range(NX):
        q = pieces[xq, 0]

        def group(xk):
            scores = [mm_nt(q, kv[i][xk, 0]) for i in range(4)]
            if xk == xq:
                at = lax.broadcasted_iota(jnp.int32, (rows, rows), 1)
                upto = lax.broadcasted_iota(jnp.int32, (rows, rows), 0)
                scores = [
                    jnp.where(at + jnp.bitwise_xor(r, i) * rows <= upto + r * rows, s, -1e30)
                    for i, s in enumerate(scores)
                ]
            best = jnp.maximum(
                jnp.maximum(scores[0], scores[1]), jnp.maximum(scores[2], scores[3])
            )
            new = jnp.max(best, axis=-1, keepdims=True)
            if xk > 0:
                old = top[...]
                new = jnp.maximum(old, new)
            out = None
            for i, s in enumerate(scores):
                weights = jnp.exp2((s - new) * scale).astype(BF16)
                term = mm(weights, jnp.concatenate([kv[i][xk, 1], ones], axis=1))
                out = term if out is None else out + term
            if xk > 0:
                out = acc[...] * jnp.exp2((old - new) * scale) + out
            acc[...] = out
            top[...] = new

        for xk in range(xq + 1):
            group(xk)
        total = acc[...]
        result = (total[:, :HSIZE] / total[:, HSIZE:]).astype(BF16)
        for d, out in enumerate((o0, o1, o2, o3)):

            @pl.when(lax.rem(xq + d, NX) == x)
            def _():
                out[...] = result


def mix_kernel(s0, s1, s2, s3, cross, out):
    x = lax.axis_index("x")
    for d, piece in enumerate((s0, s1, s2, s3)):
        cols = pl.ds(pl.multiple_of(lax.rem(x + d, NX) * HSIZE, HSIZE), HSIZE)
        out[:, cols] = (piece[...].astype(F32) + cross[:, cols]).astype(BF16)


def head_rows(rows):
    width = rows.shape[1]
    each = width // EHEADS
    at = lax.broadcasted_iota(jnp.int32, (1, width), 1)
    parts = []
    for h in range(EHEADS):
        keep = jnp.where((at >= h * each) & (at < (h + 1) * each), 1.0, 0.0).astype(BF16)
        parts.append(rows * keep)
    return jnp.concatenate(parts, axis=0)


def encode_kernel(
    ids, nb_h, ctx_h, wq_h, wk_h, wv_h, wo_h, enc, wt, ek_out, ev_out, *scratch
):
    nb, ctx, wq, wk, wv, wo, sems = scratch
    both = ((nb_h, nb), (wq_h, wq), (ctx_h, ctx), (wk_h, wk), (wv_h, wv), (wo_h, wo))
    copies = [pltpu.make_async_copy(a, b, sems.at[i]) for i, (a, b) in enumerate(both)]
    for c in copies:
        c.start()
    slots, rows, width = nb.shape
    each = width // EHEADS
    copies[0].wait()
    x = nb[...].reshape(slots * rows, width)
    copies[1].wait()
    eq = mm(x, wq[...]).astype(BF16)
    copies[2].wait()
    contexts = []
    for t in range(slots):
        mine = (lax.axis_index("z") * 2 + lax.axis_index("yh")) * slots + t
        span = jnp.int32(0)
        for c in range(1, ids.shape[1]):
            span = jnp.where((ids[0, c] == mine) | (ids[1, c] == mine), c, span)
        contexts.append(ctx[pl.ds(pl.multiple_of(span * CL, CL), CL), :])
    m = jnp.concatenate(contexts, axis=0)
    copies[3].wait()
    ek = mm(m, wk[...]).astype(BF16)
    copies[4].wait()
    ev = mm(m, wv[...]).astype(BF16)
    mixed = []
    for t in range(slots):
        ek_t = ek[t * CL : (t + 1) * CL]
        ev_t = ev[t * CL : (t + 1) * CL]
        s = mm_nt(head_rows(ek_t), eq[t * rows : (t + 1) * rows]) * (1.0 / math.sqrt(each))
        s = s.reshape(EHEADS, CL, rows)
        p = jnp.exp(s - jnp.max(s, axis=1, keepdims=True))
        w = (p * (1.0 / jnp.sum(p, axis=1, keepdims=True))).reshape(EHEADS * CL, rows)
        wt[t] = w
        ek_out[t] = ek_t
        ev_out[t] = ev_t
        mixed.append(mm_tn(w.astype(BF16), head_rows(ev_t)).astype(BF16))
    copies[5].wait()
    out = x.astype(F32) + mm(jnp.concatenate(mixed, axis=0), wo[...])
    enc[...] = out.astype(BF16).reshape(slots, rows, width)


def pullback_kernel(d0, d1, d2, d3, wo, ev, wt, ek, wq, out):
    slots, rows, width = d0.shape
    each = width // EHEADS
    d = (d0[...].astype(F32) + d1[...].astype(F32)) + (d2[...].astype(F32) + d3[...].astype(F32))
    d = d.reshape(slots * rows, width)
    de = mm(d.astype(BF16), wo[...]).astype(BF16)
    back = []
    for t in range(slots):
        w = wt[t]
        dw = mm_nt(head_rows(ev[t]), de[t * rows : (t + 1) * rows])
        dw = dw.astype(BF16).astype(F32).reshape(EHEADS, CL, rows)
        w = w.reshape(EHEADS, CL, rows)
        ds = w * (dw - jnp.sum(w * dw, axis=1, keepdims=True)) * (1.0 / math.sqrt(each))
        ds = ds.reshape(EHEADS * CL, rows).astype(BF16)
        back.append(mm_tn(ds, head_rows(ek[t])).astype(BF16))
    out[...] = (d + mm(jnp.concatenate(back, axis=0), wq[...])).reshape(slots, rows, width)


def turn_kernel(kw, vw, wq, wo, kvw, kv_t, wq_t, wo_t):
    width = kw.shape[1]
    kvw[:, :width] = kw[...]
    kvw[:, width:] = vw[...]
    kv_t[:width] = kw[...].T
    kv_t[width:] = vw[...].T
    wq_t[...] = wq[...].T
    wo_t[...] = wo[...].T


def blocks_kernel(q, g, qm_t, gm_t):
    for c in range(qm_t.shape[0]):
        qm_t[c] = head_blocks(q[c * CL : (c + 1) * CL]).T
        gm_t[c] = head_blocks(g[c * CL : (c + 1) * CL]).T


def head_blocks(rows):
    width = rows.shape[1]
    at = lax.broadcasted_iota(jnp.int32, (1, width), 1)
    parts = []
    for h in range(width // HSIZE):
        keep = jnp.where((at >= h * HSIZE) & (at < (h + 1) * HSIZE), 1.0, 0.0).astype(BF16)
        parts.append(rows * keep)
    return jnp.concatenate(parts, axis=0)


def cross_kernel(ids, e00, e01, e10, e11, e20, e21, e30, e31, *rest):
    blocks = (e00, e01, e10, e11, e20, e21, e30, e31)
    kvw, qm_t, gm_t, q, g, kv_t, cross = rest[:7]
    outs, (table, held, sent, ckv, dkv, zero, in_sem, out_sem) = rest[7:15], rest[15:]
    width = q.shape[1]
    z, yh = lax.axis_index("z"), lax.axis_index("yh")
    n_named = held.shape[0]
    spans = n_named // 2
    scale = 1.0 / math.sqrt(HSIZE)

    for i in range(16):
        table[i] = jnp.int32(-1)
    for n in range(n_named):
        slot = ids[n % 2, n // 2]
        dz = lax.rem(slot // 4 - z + NX, NX)
        dy = jnp.bitwise_xor(lax.rem(slot // 2, 2), yh)
        table[dz * 4 + dy * 2 + lax.rem(slot, 2)] = jnp.int32(n)
    zero[...] = jnp.zeros_like(zero)
    places = [4, 5, 0, 1, 2, 3, 6, 7]
    places = [(i, t) for i in places for t in range(2)]
    for i, t in places:
        n = table[2 * i + t]

        @pl.when(n >= 0)
        def _():
            pltpu.make_async_copy(blocks[i].at[t], held.at[n], in_sem.at[n]).start()

    for i, t in places:

        @pl.when(table[2 * i + t] < 0)
        def _():
            pltpu.make_async_copy(zero, outs[i].at[t], out_sem.at[2 * i + t]).start()

    heads = width // HSIZE
    pair = 2 * NL
    for half in range(2):
        first = half * (n_named // 2)
        for n in range(first, first + n_named // 2):
            pltpu.make_async_copy(e00.at[0], held.at[n], in_sem.at[n]).wait()
        e = held[first : first + n_named // 2].reshape(n_named // 2 * NL, -1)
        ckv[first * NL : (first + n_named // 2) * NL] = mm(e, kvw[...]).astype(BF16)

    def scores(c):
        at = slice(c * pair, (c + 1) * pair)
        return mm(ckv[at, :width], qm_t[c]), mm(ckv[at, width:], gm_t[c])

    def soften(s, dp):
        p = jnp.exp2((s - jnp.max(s, axis=0, keepdims=True)) * (scale * LOG2E))
        p = p * (1.0 / jnp.sum(p, axis=0, keepdims=True))
        ds = p * ((dp - jnp.sum(p * dp, axis=0, keepdims=True)) * scale)
        return p.astype(BF16), ds.astype(BF16)

    def products(c, pb, ds):
        at = slice(c * pair, (c + 1) * pair)
        dkv[at, :width] = mm(ds, head_blocks(q[c * CL : (c + 1) * CL])).astype(BF16)
        dkv[at, width:] = mm(pb, head_blocks(g[c * CL : (c + 1) * CL])).astype(BF16)
        pt = pb.T
        for h in range(heads):
            cols = slice(h * HSIZE, (h + 1) * HSIZE)
            cross[c * CL : (c + 1) * CL, cols] = mm(
                pt[h * CL : (h + 1) * CL], ckv[at, width + h * HSIZE : width + (h + 1) * HSIZE]
            )

    def back(c):
        at = slice(c * pair, (c + 1) * pair)
        sent[2 * c : 2 * c + 2] = mm(dkv[at], kv_t[...]).astype(BF16).reshape(2, NL, -1)

    def send(low, high):
        for i, t in places:
            n = table[2 * i + t]

            @pl.when((n >= low) & (n < high))
            def _():
                pltpu.make_async_copy(sent.at[n], outs[i].at[t], out_sem.at[2 * i + t]).start()

    ahead = scores(0)
    for c in range(spans):
        now = ahead
        if c + 1 < spans:
            ahead = scores(c + 1)
        soft = soften(*now)
        if c >= 1:
            back(c - 1)
        products(c, *soft)
    send(0, n_named - 2)
    back(spans - 1)
    send(n_named - 2, n_named)
    for i, t in places:
        pltpu.make_async_copy(zero, outs[i].at[t], out_sem.at[2 * i + t]).wait()


def shift(n, by):
    return [(i, (i + by) % n) for i in range(n)]


def local(
    self_q,
    self_k,
    self_v,
    cross_q,
    cross_k_weight,
    cross_v_weight,
    span_ctx,
    neighbours,
    neighbour_ids,
    enc_q,
    enc_k,
    enc_v,
    enc_o,
    mixed_grad,
):
    rows, width = self_q.shape
    slots, nl, ew = neighbours.shape
    spans, per_span = neighbour_ids.shape
    n_named = spans * per_span
    struct = jax.ShapeDtypeStruct
    after = lax.optimization_barrier

    ids = neighbour_ids.T

    e00, wt, ek, ev = call(
        encode_kernel,
        mib=56,
        out_shape=[
            struct((slots, nl, ew), BF16),
            struct((slots, EHEADS * CL, nl), F32),
            struct((slots, CL, ew), BF16),
            struct((slots, CL, ew), BF16),
        ],
        in_specs=[smem()] + [hbm()] * 6,
        out_specs=[vmem()] * 4,
        scratch_shapes=[pltpu.VMEM(neighbours.shape, BF16), pltpu.VMEM(span_ctx.shape, BF16)]
        + [pltpu.VMEM((ew, ew), BF16)] * 4
        + [pltpu.SemaphoreType.DMA((6,))],
    )(ids, neighbours, span_ctx, enc_q, enc_k, enc_v, enc_o)

    e01 = lax.ppermute(e00, "yh", shift(2, 1))
    e30 = lax.ppermute(e00, "z", shift(NX, 1))
    e10 = lax.ppermute(e00, "z", shift(NX, -1))

    self_q, self_k, self_v, _ = after((self_q, self_k, self_v, wt))
    packed = call(
        pack_kernel,
        out_shape=struct((NX, 3, rows, HSIZE), BF16),
        in_specs=[vmem()] * 3,
        out_specs=vmem(),
    )(self_q, self_k, self_v)
    pieces = lax.all_to_all(packed, "x", 0, 0)

    e01, e30, e10, packed = after((e01, e30, e10, packed))
    e11 = lax.ppermute(e01, "z", shift(NX, -1))
    e31 = lax.ppermute(e01, "z", shift(NX, 1))


    weights = after((cross_k_weight, cross_v_weight, enc_q, enc_o, e01))[:4]
    turned = call(
        turn_kernel,
        out_shape=[struct((ew, 2 * width), BF16), struct((2 * width, ew), BF16)]
        + [struct((ew, ew), BF16)] * 2,
        in_specs=[vmem()] * 4,
        out_specs=[vmem()] * 4,
    )(*weights)

    own_kv = pieces[:, 1:]
    e30, e11, e31, own_kv, *turned = after((e30, e11, e31, own_kv, *turned))
    swap = [(0, 3), (1, 2), (2, 1), (3, 0)]
    kvs = [
        own_kv,
        lax.ppermute(own_kv, "core", shift(2, 1)),
        lax.ppermute(own_kv, "yl", shift(2, 1)),
        lax.ppermute(own_kv, ("yl", "core"), swap),
    ]
    kvw, kv_t, wq_t, wo_t = turned
    e20 = lax.ppermute(e30, "z", shift(NX, 1))
    e21 = lax.ppermute(e11, "z", shift(NX, -1))

    queries, grads, _ = after((cross_q, mixed_grad, e11))
    qm_t, gm_t = call(
        blocks_kernel,
        out_shape=[struct((spans, width, width // HSIZE * CL), BF16)] * 2,
        in_specs=[vmem()] * 2,
        out_specs=[vmem()] * 2,
    )(queries, grads)

    cross, *p = call(
        cross_kernel,
        out_shape=[struct((rows, width), F32)] + [struct((slots, nl, ew), BF16)] * 8,
        in_specs=[smem()] + [anywhere()] * 8 + [vmem()] * 6,
        out_specs=[vmem()] + [anywhere()] * 8,
        scratch_shapes=[
            pltpu.SMEM((16,), jnp.int32),
            pltpu.VMEM((n_named, nl, ew), BF16),
            pltpu.VMEM((n_named, nl, ew), BF16),
            pltpu.VMEM((n_named * nl, 2 * width), BF16),
            pltpu.VMEM((n_named * nl, 2 * width), BF16),
            pltpu.VMEM((nl, ew), BF16),
            pltpu.SemaphoreType.DMA((n_named,)),
            pltpu.SemaphoreType.DMA((16,)),
        ],
    )(
        ids,
        e00,
        e01,
        e10,
        e11,
        e20,
        e21,
        e30,
        e31,
        kvw,
        qm_t,
        gm_t,
        cross_q,
        mixed_grad,
        kv_t,
    )
    p00, p01, p10, p11, p20, p21, p30, p31 = p

    def add(a, b):
        return (a.astype(F32) + b.astype(F32)).astype(BF16)

    far1 = lax.ppermute(p21, "z", shift(NX, -1))
    far0 = lax.ppermute(p20, "z", shift(NX, 1))
    *kvs, _ = after((*kvs, cross))
    outs = call(
        attend_kernel,
        out_shape=[struct((rows, HSIZE), BF16)] * NX,
        in_specs=[vmem()] * 5,
        out_specs=[vmem()] * NX,
        scratch_shapes=[
            pltpu.VMEM((rows, 2 * HSIZE), F32),
            pltpu.VMEM((rows, 1), F32),
        ],
    )(pieces, *kvs)
    far1, far0, p11, *outs = after((far1, far0, p11, *outs))
    selfs = [outs[0]] + [lax.ppermute(outs[d], "x", shift(NX, -d)) for d in range(1, NX)]
    down1 = lax.ppermute(add(p31, far1), "z", shift(NX, -1))
    up1 = lax.ppermute(p11, "z", shift(NX, 1))
    near0 = add(p10, far0)
    down1, up1, near0, p30, *selfs = after((down1, up1, near0, p30, *selfs))
    theirs = (p01.astype(F32) + up1.astype(F32) + down1.astype(F32)).astype(BF16)
    other = lax.ppermute(theirs, "yh", shift(2, 1))
    up0 = lax.ppermute(near0, "z", shift(NX, 1))
    down0 = lax.ppermute(p30, "z", shift(NX, -1))

    grad = call(
        pullback_kernel,
        out_shape=struct((slots, nl, ew), F32),
        in_specs=[vmem()] * 9,
        out_specs=vmem(),
    )(p00, up0, down0, other, wo_t, ev, wt, ek, wq_t)

    mixed = call(
        mix_kernel,
        out_shape=struct((rows, width), BF16),
        in_specs=[vmem()] * 5,
        out_specs=vmem(),
    )(*selfs, cross)
    return mixed, grad


def solution(mesh):
    fine = Mesh(mesh.devices.reshape(4, 2, 2, 4, 2), ("x", "yl", "core", "z", "yh"))
    ctx, enc = ("x", "yl", "core"), ("z", "yh")
    tokens = P(ctx, enc)
    return jax.shard_map(
        local,
        mesh=fine,
        in_specs=(
            tokens,
            tokens,
            tokens,
            tokens,
            P(None, enc),
            P(None, enc),
            P(ctx, None),
            P(ctx + enc, None, None),
            P(ctx, None),
            P(),
            P(),
            P(),
            P(),
            tokens,
        ),
        out_specs=(tokens, P(ctx + enc, None, None)),
        check_vma=False,
    )
```

```python
import math

import jax
import jax.numpy as jnp
from jax import lax
from jax.experimental import pallas as pl
from jax.experimental.pallas import tpu as pltpu
from jax.sharding import Mesh
from jax.sharding import PartitionSpec as P

HSIZE = 128
EHEADS = 4
CL = 64
NL = 128
NX = 4
LOG2E = math.log2(math.e)
BF16 = jnp.bfloat16
F32 = jnp.float32

NT = (((1,), (1,)), ((), ()))
TN = (((0,), (0,)), ((), ()))


def mm(a, b):
    return jnp.dot(a, b, preferred_element_type=F32)


def mm_nt(a, b):
    return lax.dot_general(a, b, NT, preferred_element_type=F32)


def mm_tn(a, b):
    return lax.dot_general(a, b, TN, preferred_element_type=F32)


def call(kernel, mib=24, **kw):
    return pl.pallas_call(
        kernel,
        compiler_params=pltpu.CompilerParams(vmem_limit_bytes=mib * 1024 * 1024),
        **kw,
    )


def smem():
    return pl.BlockSpec(memory_space=pltpu.SMEM)


def vmem():
    return pl.BlockSpec(memory_space=pltpu.VMEM)


def hbm():
    return pl.BlockSpec(memory_space=pltpu.HBM)


def pack_kernel(q_ref, k_ref, v_ref, out):
    for h in range(NX):
        cols = slice(h * HSIZE, (h + 1) * HSIZE)
        for i, src in enumerate((q_ref, k_ref, v_ref)):
            out[h, i] = src[:, cols]


def attend_kernel(pieces, kv0, kv1, kv2, kv3, o0, o1, o2, o3, acc, top):
    kv = (kv0, kv1, kv2, kv3)
    x = lax.axis_index("x")
    r = lax.axis_index("yl") * 2 + lax.axis_index("core")
    scale = LOG2E / math.sqrt(HSIZE)
    rows = pieces.shape[2]
    ones = jnp.ones((rows, HSIZE), BF16)
    for xq in range(NX):
        q = pieces[xq, 0]

        def group(xk):
            scores = [mm_nt(q, kv[i][xk, 0]) for i in range(4)]
            if xk == xq:
                at = lax.broadcasted_iota(jnp.int32, (rows, rows), 1)
                upto = lax.broadcasted_iota(jnp.int32, (rows, rows), 0)
                scores = [
                    jnp.where(at + jnp.bitwise_xor(r, i) * rows <= upto + r * rows, s, -1e30)
                    for i, s in enumerate(scores)
                ]
            best = jnp.maximum(
                jnp.maximum(scores[0], scores[1]), jnp.maximum(scores[2], scores[3])
            )
            new = jnp.max(best, axis=-1, keepdims=True)
            if xk > 0:
                old = top[...]
                new = jnp.maximum(old, new)
            out = None
            for i, s in enumerate(scores):
                weights = jnp.exp2((s - new) * scale).astype(BF16)
                term = mm(weights, jnp.concatenate([kv[i][xk, 1], ones], axis=1))
                out = term if out is None else out + term
            if xk > 0:
                out = acc[...] * jnp.exp2((old - new) * scale) + out
            acc[...] = out
            top[...] = new

        for xk in range(xq + 1):
            group(xk)
        total = acc[...]
        result = (total[:, :HSIZE] / total[:, HSIZE:]).astype(BF16)
        for d, out in enumerate((o0, o1, o2, o3)):

            @pl.when(lax.rem(xq + d, NX) == x)
            def _():
                out[...] = result


def mix_kernel(s0, s1, s2, s3, cross, out):
    x = lax.axis_index("x")
    for d, piece in enumerate((s0, s1, s2, s3)):
        cols = pl.ds(pl.multiple_of(lax.rem(x + d, NX) * HSIZE, HSIZE), HSIZE)
        out[:, cols] = (piece[...].astype(F32) + cross[:, cols]).astype(BF16)


def head_rows(rows):
    width = rows.shape[1]
    each = width // EHEADS
    at = lax.broadcasted_iota(jnp.int32, (1, width), 1)
    parts = []
    for h in range(EHEADS):
        keep = jnp.where((at >= h * each) & (at < (h + 1) * each), 1.0, 0.0).astype(BF16)
        parts.append(rows * keep)
    return jnp.concatenate(parts, axis=0)


def encode_kernel(
    ids, nb_h, ctx_h, wq_h, wk_h, wv_h, wo_h, enc, wt, ek_out, ev_out, *scratch
):
    nb, ctx, wq, wk, wv, wo, sems = scratch
    both = ((nb_h, nb), (wq_h, wq), (ctx_h, ctx), (wk_h, wk), (wv_h, wv), (wo_h, wo))
    copies = [pltpu.make_async_copy(a, b, sems.at[i]) for i, (a, b) in enumerate(both)]
    for c in copies:
        c.start()
    slots, rows, width = nb.shape
    each = width // EHEADS
    copies[0].wait()
    x = nb[...].reshape(slots * rows, width)
    copies[1].wait()
    eq = mm(x, wq[...]).astype(BF16)
    copies[2].wait()
    contexts = []
    for t in range(slots):
        mine = (lax.axis_index("z") * 2 + lax.axis_index("yh")) * slots + t
        span = jnp.int32(0)
        for c in range(1, ids.shape[1]):
            span = jnp.where((ids[0, c] == mine) | (ids[1, c] == mine), c, span)
        contexts.append(ctx[pl.ds(pl.multiple_of(span * CL, CL), CL), :])
    m = jnp.concatenate(contexts, axis=0)
    copies[3].wait()
    ek = mm(m, wk[...]).astype(BF16)
    copies[4].wait()
    ev = mm(m, wv[...]).astype(BF16)
    mixed = []
    for t in range(slots):
        ek_t = ek[t * CL : (t + 1) * CL]
        ev_t = ev[t * CL : (t + 1) * CL]
        s = mm_nt(head_rows(ek_t), eq[t * rows : (t + 1) * rows]) * (1.0 / math.sqrt(each))
        s = s.reshape(EHEADS, CL, rows)
        p = jnp.exp(s - jnp.max(s, axis=1, keepdims=True))
        w = (p * (1.0 / jnp.sum(p, axis=1, keepdims=True))).reshape(EHEADS * CL, rows)
        wt[t] = w
        ek_out[t] = ek_t
        ev_out[t] = ev_t
        mixed.append(mm_tn(w.astype(BF16), head_rows(ev_t)).astype(BF16))
    copies[5].wait()
    out = x.astype(F32) + mm(jnp.concatenate(mixed, axis=0), wo[...])
    enc[...] = out.astype(BF16).reshape(slots, rows, width)


def pullback_kernel(d0, d1, d2, d3, wo, ev, wt, ek, wq, out):
    slots, rows, width = d0.shape
    each = width // EHEADS
    d = (d0[...].astype(F32) + d1[...].astype(F32)) + (d2[...].astype(F32) + d3[...].astype(F32))
    d = d.reshape(slots * rows, width)
    de = mm(d.astype(BF16), wo[...]).astype(BF16)
    back = []
    for t in range(slots):
        w = wt[t]
        dw = mm_nt(head_rows(ev[t]), de[t * rows : (t + 1) * rows])
        dw = dw.astype(BF16).astype(F32).reshape(EHEADS, CL, rows)
        w = w.reshape(EHEADS, CL, rows)
        ds = w * (dw - jnp.sum(w * dw, axis=1, keepdims=True)) * (1.0 / math.sqrt(each))
        ds = ds.reshape(EHEADS * CL, rows).astype(BF16)
        back.append(mm_tn(ds, head_rows(ek[t])).astype(BF16))
    out[...] = (d + mm(jnp.concatenate(back, axis=0), wq[...])).reshape(slots, rows, width)


def turn_kernel(wq, wo, wq_t, wo_t):
    wq_t[...] = wq[...].T
    wo_t[...] = wo[...].T


def blocks_kernel(kw, vw, q, g, kvw, kv_t, qm_t, gm_t):
    width = kw.shape[1]
    kvw[:, :width] = kw[...]
    kvw[:, width:] = vw[...]
    kv_t[:width] = kw[...].T
    kv_t[width:] = vw[...].T
    for c in range(qm_t.shape[0]):
        qm_t[c] = head_blocks(q[c * CL : (c + 1) * CL]).T
        gm_t[c] = head_blocks(g[c * CL : (c + 1) * CL]).T


def head_blocks(rows):
    width = rows.shape[1]
    at = lax.broadcasted_iota(jnp.int32, (1, width), 1)
    parts = []
    for h in range(width // HSIZE):
        keep = jnp.where((at >= h * HSIZE) & (at < (h + 1) * HSIZE), 1.0, 0.0).astype(BF16)
        parts.append(rows * keep)
    return jnp.concatenate(parts, axis=0)


def cross_kernel(ids, e00, e01, e10, e11, e20, e21, e30, e31, *rest):
    blocks = (e00, e01, e10, e11, e20, e21, e30, e31)
    kvw, qm_t, gm_t, q, g, kv_t, cross = rest[:7]
    outs, (table, held, sent, ckv, dkv) = rest[7:15], rest[15:]
    width = q.shape[1]
    z, yh = lax.axis_index("z"), lax.axis_index("yh")
    n_named = held.shape[0]
    spans = n_named // 2
    scale = 1.0 / math.sqrt(HSIZE)

    for i in range(16):
        table[i] = jnp.int32(-1)
    for n in range(n_named):
        slot = ids[n % 2, n // 2]
        dz = lax.rem(slot // 4 - z + NX, NX)
        dy = jnp.bitwise_xor(lax.rem(slot // 2, 2), yh)
        table[dz * 4 + dy * 2 + lax.rem(slot, 2)] = jnp.int32(n)
    places = [(i, t) for i in range(8) for t in range(2)]
    for i, t in places:
        n = table[2 * i + t]

        @pl.when(n >= 0)
        def _():
            held[n] = blocks[i][t]

        @pl.when(n < 0)
        def _():
            outs[i][t] = jnp.zeros(outs[i].shape[1:], BF16)

    heads = width // HSIZE
    pair = 2 * NL
    for half in range(2):
        first = half * (n_named // 2)
        e = held[first : first + n_named // 2].reshape(n_named // 2 * NL, -1)
        ckv[first * NL : (first + n_named // 2) * NL] = mm(e, kvw[...]).astype(BF16)

    def scores(c):
        at = slice(c * pair, (c + 1) * pair)
        return mm(ckv[at, :width], qm_t[c]), mm(ckv[at, width:], gm_t[c])

    def soften(s, dp):
        p = jnp.exp2((s - jnp.max(s, axis=0, keepdims=True)) * (scale * LOG2E))
        p = p * (1.0 / jnp.sum(p, axis=0, keepdims=True))
        ds = p * ((dp - jnp.sum(p * dp, axis=0, keepdims=True)) * scale)
        return p.astype(BF16), ds.astype(BF16)

    def products(c, pb, ds):
        at = slice(c * pair, (c + 1) * pair)
        dkv[at, :width] = mm(ds, head_blocks(q[c * CL : (c + 1) * CL])).astype(BF16)
        dkv[at, width:] = mm(pb, head_blocks(g[c * CL : (c + 1) * CL])).astype(BF16)
        pt = pb.T
        for h in range(heads):
            cols = slice(h * HSIZE, (h + 1) * HSIZE)
            cross[c * CL : (c + 1) * CL, cols] = mm(
                pt[h * CL : (h + 1) * CL], ckv[at, width + h * HSIZE : width + (h + 1) * HSIZE]
            )

    def back(c):
        at = slice(c * pair, (c + 1) * pair)
        sent[2 * c : 2 * c + 2] = mm(dkv[at], kv_t[...]).astype(BF16).reshape(2, NL, -1)

    def send(low, high):
        for i, t in places:
            n = table[2 * i + t]

            @pl.when((n >= low) & (n < high))
            def _():
                outs[i][t] = sent[n]

    ahead = scores(0)
    for c in range(spans):
        now = ahead
        if c + 1 < spans:
            ahead = scores(c + 1)
        soft = soften(*now)
        if c >= 1:
            back(c - 1)
        products(c, *soft)
    send(0, n_named - 2)
    back(spans - 1)
    send(n_named - 2, n_named)


def shift(n, by):
    return [(i, (i + by) % n) for i in range(n)]


def local(
    self_q,
    self_k,
    self_v,
    cross_q,
    cross_k_weight,
    cross_v_weight,
    span_ctx,
    neighbours,
    neighbour_ids,
    enc_q,
    enc_k,
    enc_v,
    enc_o,
    mixed_grad,
):
    rows, width = self_q.shape
    slots, nl, ew = neighbours.shape
    spans, per_span = neighbour_ids.shape
    n_named = spans * per_span
    struct = jax.ShapeDtypeStruct
    after = lax.optimization_barrier

    ids = neighbour_ids.T

    e00, wt, ek, ev = call(
        encode_kernel,
        mib=56,
        out_shape=[
            struct((slots, nl, ew), BF16),
            struct((slots, EHEADS * CL, nl), F32),
            struct((slots, CL, ew), BF16),
            struct((slots, CL, ew), BF16),
        ],
        in_specs=[smem()] + [hbm()] * 6,
        out_specs=[vmem()] * 4,
        scratch_shapes=[pltpu.VMEM(neighbours.shape, BF16), pltpu.VMEM(span_ctx.shape, BF16)]
        + [pltpu.VMEM((ew, ew), BF16)] * 4
        + [pltpu.SemaphoreType.DMA((6,))],
    )(ids, neighbours, span_ctx, enc_q, enc_k, enc_v, enc_o)

    e01 = lax.ppermute(e00, "yh", shift(2, 1))
    e30 = lax.ppermute(e00, "z", shift(NX, 1))
    e10 = lax.ppermute(e00, "z", shift(NX, -1))

    self_q, self_k, self_v, _ = after((self_q, self_k, self_v, wt))
    packed = call(
        pack_kernel,
        out_shape=struct((NX, 3, rows, HSIZE), BF16),
        in_specs=[vmem()] * 3,
        out_specs=vmem(),
    )(self_q, self_k, self_v)
    pieces = lax.all_to_all(packed, "x", 0, 0)

    e01, e30, e10, packed = after((e01, e30, e10, packed))
    e11 = lax.ppermute(e01, "z", shift(NX, -1))
    e31 = lax.ppermute(e01, "z", shift(NX, 1))


    weights = after((enc_q, enc_o, e01))[:2]
    turned = call(
        turn_kernel,
        out_shape=[struct((ew, ew), BF16)] * 2,
        in_specs=[vmem()] * 2,
        out_specs=[vmem()] * 2,
    )(*weights)

    own_kv = pieces[:, 1:]
    e30, e11, e31, own_kv, *turned = after((e30, e11, e31, own_kv, *turned))
    swap = [(0, 3), (1, 2), (2, 1), (3, 0)]
    kvs = [
        own_kv,
        lax.ppermute(own_kv, "core", shift(2, 1)),
        lax.ppermute(own_kv, "yl", shift(2, 1)),
        lax.ppermute(own_kv, ("yl", "core"), swap),
    ]
    wq_t, wo_t = turned
    e20 = lax.ppermute(e30, "z", shift(NX, 1))
    e21 = lax.ppermute(e11, "z", shift(NX, -1))

    given = after((cross_k_weight, cross_v_weight, cross_q, mixed_grad, e11))[:4]
    kvw, kv_t, qm_t, gm_t = call(
        blocks_kernel,
        out_shape=[struct((ew, 2 * width), BF16), struct((2 * width, ew), BF16)]
        + [struct((spans, width, width // HSIZE * CL), BF16)] * 2,
        in_specs=[vmem()] * 4,
        out_specs=[vmem()] * 4,
    )(*given)

    cross, *p = call(
        cross_kernel,
        out_shape=[struct((rows, width), F32)] + [struct((slots, nl, ew), BF16)] * 8,
        in_specs=[smem()] + [vmem()] * 14,
        out_specs=[vmem()] * 9,
        scratch_shapes=[
            pltpu.SMEM((16,), jnp.int32),
            pltpu.VMEM((n_named, nl, ew), BF16),
            pltpu.VMEM((n_named, nl, ew), BF16),
            pltpu.VMEM((n_named * nl, 2 * width), BF16),
            pltpu.VMEM((n_named * nl, 2 * width), BF16),
        ],
    )(
        ids,
        e00,
        e01,
        e10,
        e11,
        e20,
        e21,
        e30,
        e31,
        kvw,
        qm_t,
        gm_t,
        cross_q,
        mixed_grad,
        kv_t,
    )
    p00, p01, p10, p11, p20, p21, p30, p31 = p

    def add(a, b):
        return (a.astype(F32) + b.astype(F32)).astype(BF16)

    far1 = lax.ppermute(p21, "z", shift(NX, -1))
    far0 = lax.ppermute(p20, "z", shift(NX, 1))
    *kvs, _ = after((*kvs, cross))
    outs = call(
        attend_kernel,
        out_shape=[struct((rows, HSIZE), BF16)] * NX,
        in_specs=[vmem()] * 5,
        out_specs=[vmem()] * NX,
        scratch_shapes=[
            pltpu.VMEM((rows, 2 * HSIZE), F32),
            pltpu.VMEM((rows, 1), F32),
        ],
    )(pieces, *kvs)
    far1, far0, p11, *outs = after((far1, far0, p11, *outs))
    selfs = [outs[0]] + [lax.ppermute(outs[d], "x", shift(NX, -d)) for d in range(1, NX)]
    down1 = lax.ppermute(add(p31, far1), "z", shift(NX, -1))
    up1 = lax.ppermute(p11, "z", shift(NX, 1))
    near0 = add(p10, far0)
    down1, up1, near0, p30, *selfs = after((down1, up1, near0, p30, *selfs))
    theirs = (p01.astype(F32) + up1.astype(F32) + down1.astype(F32)).astype(BF16)
    other = lax.ppermute(theirs, "yh", shift(2, 1))
    up0 = lax.ppermute(near0, "z", shift(NX, 1))
    down0 = lax.ppermute(p30, "z", shift(NX, -1))

    grad = call(
        pullback_kernel,
        out_shape=struct((slots, nl, ew), F32),
        in_specs=[vmem()] * 9,
        out_specs=vmem(),
    )(p00, up0, down0, other, wo_t, ev, wt, ek, wq_t)

    mixed = call(
        mix_kernel,
        out_shape=struct((rows, width), BF16),
        in_specs=[vmem()] * 5,
        out_specs=vmem(),
    )(*selfs, cross)
    return mixed, grad


def solution(mesh):
    fine = Mesh(mesh.devices.reshape(4, 2, 2, 4, 2), ("x", "yl", "core", "z", "yh"))
    ctx, enc = ("x", "yl", "core"), ("z", "yh")
    tokens = P(ctx, enc)
    return jax.shard_map(
        local,
        mesh=fine,
        in_specs=(
            tokens,
            tokens,
            tokens,
            tokens,
            P(None, enc),
            P(None, enc),
            P(ctx, None),
            P(ctx + enc, None, None),
            P(ctx, None),
            P(),
            P(),
            P(),
            P(),
            tokens,
        ),
        out_specs=(tokens, P(ctx + enc, None, None)),
        check_vma=False,
    )
```

```python
import math

import jax
import jax.numpy as jnp
from jax import lax
from jax.experimental import pallas as pl
from jax.experimental.pallas import tpu as pltpu
from jax.sharding import Mesh
from jax.sharding import PartitionSpec as P

HSIZE = 128
EHEADS = 4
CL = 64
NL = 128
NX = 4
LOG2E = math.log2(math.e)
BF16 = jnp.bfloat16
F32 = jnp.float32

NT = (((1,), (1,)), ((), ()))
TN = (((0,), (0,)), ((), ()))


def mm(a, b):
    return jnp.dot(a, b, preferred_element_type=F32)


def mm_nt(a, b):
    return lax.dot_general(a, b, NT, preferred_element_type=F32)


def mm_tn(a, b):
    return lax.dot_general(a, b, TN, preferred_element_type=F32)


def call(kernel, mib=24, **kw):
    return pl.pallas_call(
        kernel,
        compiler_params=pltpu.CompilerParams(vmem_limit_bytes=mib * 1024 * 1024),
        **kw,
    )


def smem():
    return pl.BlockSpec(memory_space=pltpu.SMEM)


def vmem():
    return pl.BlockSpec(memory_space=pltpu.VMEM)


def hbm():
    return pl.BlockSpec(memory_space=pltpu.HBM)


def pack_kernel(q_ref, k_ref, v_ref, out):
    for h in range(NX):
        cols = slice(h * HSIZE, (h + 1) * HSIZE)
        for i, src in enumerate((q_ref, k_ref, v_ref)):
            out[h, i] = src[:, cols]


def attend_kernel(pieces, kv0, kv1, kv2, kv3, o0, o1, o2, o3, acc, top):
    kv = (kv0, kv1, kv2, kv3)
    x = lax.axis_index("x")
    r = lax.axis_index("yl") * 2 + lax.axis_index("core")
    scale = LOG2E / math.sqrt(HSIZE)
    rows = pieces.shape[2]
    ones = jnp.ones((rows, HSIZE), BF16)
    for xq in range(NX):
        q = pieces[xq, 0]

        def group(xk):
            scores = [mm_nt(q, kv[i][xk, 0]) for i in range(4)]
            if xk == xq:
                at = lax.broadcasted_iota(jnp.int32, (rows, rows), 1)
                upto = lax.broadcasted_iota(jnp.int32, (rows, rows), 0)
                scores = [
                    jnp.where(at + jnp.bitwise_xor(r, i) * rows <= upto + r * rows, s, -1e30)
                    for i, s in enumerate(scores)
                ]
            best = jnp.maximum(
                jnp.maximum(scores[0], scores[1]), jnp.maximum(scores[2], scores[3])
            )
            new = jnp.max(best, axis=-1, keepdims=True)
            if xk > 0:
                old = top[...]
                new = jnp.maximum(old, new)
            out = None
            for i, s in enumerate(scores):
                weights = jnp.exp2((s - new) * scale).astype(BF16)
                term = mm(weights, jnp.concatenate([kv[i][xk, 1], ones], axis=1))
                out = term if out is None else out + term
            if xk > 0:
                out = acc[...] * jnp.exp2((old - new) * scale) + out
            acc[...] = out
            top[...] = new

        for xk in range(xq + 1):
            group(xk)
        total = acc[...]
        result = (total[:, :HSIZE] / total[:, HSIZE:]).astype(BF16)
        for d, out in enumerate((o0, o1, o2, o3)):

            @pl.when(lax.rem(xq + d, NX) == x)
            def _():
                out[...] = result


def mix_kernel(s0, s1, s2, s3, cross, out):
    x = lax.axis_index("x")
    for d, piece in enumerate((s0, s1, s2, s3)):
        cols = pl.ds(pl.multiple_of(lax.rem(x + d, NX) * HSIZE, HSIZE), HSIZE)
        out[:, cols] = (piece[...].astype(F32) + cross[:, cols]).astype(BF16)


def head_rows(rows):
    width = rows.shape[1]
    each = width // EHEADS
    at = lax.broadcasted_iota(jnp.int32, (1, width), 1)
    parts = []
    for h in range(EHEADS):
        keep = jnp.where((at >= h * each) & (at < (h + 1) * each), 1.0, 0.0).astype(BF16)
        parts.append(rows * keep)
    return jnp.concatenate(parts, axis=0)


def encode_kernel(
    ids, nb_h, ctx_h, wq_h, wk_h, wv_h, wo_h, enc, wt, ek_out, ev_out, *scratch
):
    nb, ctx, wq, wk, wv, wo, sems = scratch
    slots, rows, width = nb.shape
    each = width // EHEADS
    both = [(nb_h, nb)]
    for i in range(EHEADS):
        part = slice(i * each, (i + 1) * each)
        both.append((wq_h.at[part], wq.at[part]))
    both += [(ctx_h, ctx), (wk_h, wk), (wv_h, wv), (wo_h, wo)]
    copies = [pltpu.make_async_copy(a, b, sems.at[i]) for i, (a, b) in enumerate(both)]
    for c in copies:
        c.start()
    for c in copies[:5]:
        c.wait()
    x = nb[...].reshape(slots * rows, width)
    eq = mm(x, wq[...]).astype(BF16)
    copies[5].wait()
    contexts = []
    for t in range(slots):
        mine = (lax.axis_index("z") * 2 + lax.axis_index("yh")) * slots + t
        span = jnp.int32(0)
        for c in range(1, ids.shape[1]):
            span = jnp.where((ids[0, c] == mine) | (ids[1, c] == mine), c, span)
        contexts.append(ctx[pl.ds(pl.multiple_of(span * CL, CL), CL), :])
    m = jnp.concatenate(contexts, axis=0)
    copies[6].wait()
    ek = mm(m, wk[...]).astype(BF16)
    scores = [
        mm_nt(head_rows(ek[t * CL : (t + 1) * CL]), eq[t * rows : (t + 1) * rows])
        for t in range(slots)
    ]
    copies[7].wait()
    ev = mm(m, wv[...]).astype(BF16)
    copies[8].wait()
    probs = []
    for s in scores:
        s = (s * (1.0 / math.sqrt(each))).reshape(EHEADS, CL, rows)
        p = jnp.exp(s - jnp.max(s, axis=1, keepdims=True))
        probs.append((p * (1.0 / jnp.sum(p, axis=1, keepdims=True))).reshape(EHEADS * CL, rows))
    mixed = []
    for t, w in enumerate(probs):
        ev_t = ev[t * CL : (t + 1) * CL]
        mixed.append(mm_tn(w.astype(BF16), head_rows(ev_t)).astype(BF16))
        wt[t] = w
        ek_out[t] = ek[t * CL : (t + 1) * CL]
        ev_out[t] = ev_t
    out = x.astype(F32) + mm(jnp.concatenate(mixed, axis=0), wo[...])
    enc[...] = out.astype(BF16).reshape(slots, rows, width)


def pullback_kernel(d0, d1, d2, d3, wo, ev, wt, ek, wq, out):
    slots, rows, width = d0.shape
    each = width // EHEADS
    d = (d0[...].astype(F32) + d1[...].astype(F32)) + (d2[...].astype(F32) + d3[...].astype(F32))
    d = d.reshape(slots * rows, width)
    de = mm(d.astype(BF16), wo[...]).astype(BF16)
    turned = [
        mm_nt(head_rows(ev[t]), de[t * rows : (t + 1) * rows]) for t in range(slots)
    ]
    inner = []
    for t, dw in enumerate(turned):
        dw = dw.astype(BF16).astype(F32).reshape(EHEADS, CL, rows)
        w = wt[t].reshape(EHEADS, CL, rows)
        ds = w * (dw - jnp.sum(w * dw, axis=1, keepdims=True)) * (1.0 / math.sqrt(each))
        inner.append(ds.reshape(EHEADS * CL, rows).astype(BF16))
    back = [mm_tn(ds, head_rows(ek[t])).astype(BF16) for t, ds in enumerate(inner)]
    out[...] = (d + mm(jnp.concatenate(back, axis=0), wq[...])).reshape(slots, rows, width)


def turn_kernel(wq, wo, wq_t, wo_t):
    wq_t[...] = wq[...].T
    wo_t[...] = wo[...].T


def blocks_kernel(kw, vw, q, g, kvw, kv_t, qm_t, gm_t):
    width = kw.shape[1]
    kvw[:, :width] = kw[...]
    kvw[:, width:] = vw[...]
    kv_t[:width] = kw[...].T
    kv_t[width:] = vw[...].T
    for c in range(qm_t.shape[0]):
        qm_t[c] = head_blocks(q[c * CL : (c + 1) * CL]).T
        gm_t[c] = head_blocks(g[c * CL : (c + 1) * CL]).T


def head_blocks(rows):
    width = rows.shape[1]
    at = lax.broadcasted_iota(jnp.int32, (1, width), 1)
    parts = []
    for h in range(width // HSIZE):
        keep = jnp.where((at >= h * HSIZE) & (at < (h + 1) * HSIZE), 1.0, 0.0).astype(BF16)
        parts.append(rows * keep)
    return jnp.concatenate(parts, axis=0)


def cross_kernel(ids, e00, e01, e10, e11, e20, e21, e30, e31, *rest):
    blocks = (e00, e01, e10, e11, e20, e21, e30, e31)
    kvw, qm_t, gm_t, q, g, kv_t, cross = rest[:7]
    outs, (table, held, sent, ckv, dkv) = rest[7:15], rest[15:]
    width = q.shape[1]
    z, yh = lax.axis_index("z"), lax.axis_index("yh")
    n_named = held.shape[0]
    spans = n_named // 2
    scale = 1.0 / math.sqrt(HSIZE)

    for i in range(16):
        table[i] = jnp.int32(-1)
    for n in range(n_named):
        slot = ids[n % 2, n // 2]
        dz = lax.rem(slot // 4 - z + NX, NX)
        dy = jnp.bitwise_xor(lax.rem(slot // 2, 2), yh)
        table[dz * 4 + dy * 2 + lax.rem(slot, 2)] = jnp.int32(n)
    places = [(i, t) for i in range(8) for t in range(2)]
    for i, t in places:
        n = table[2 * i + t]

        @pl.when(n >= 0)
        def _():
            held[n] = blocks[i][t]

        @pl.when(n < 0)
        def _():
            outs[i][t] = jnp.zeros(outs[i].shape[1:], BF16)

    heads = width // HSIZE
    pair = 2 * NL

    def project(half):
        first = half * (n_named // 2)
        e = held[first : first + n_named // 2].reshape(n_named // 2 * NL, -1)
        ckv[first * NL : (first + n_named // 2) * NL] = mm(e, kvw[...]).astype(BF16)

    def scores(c):
        at = slice(c * pair, (c + 1) * pair)
        return mm(ckv[at, :width], qm_t[c]), mm(ckv[at, width:], gm_t[c])

    def soften(s, dp):
        p = jnp.exp2((s - jnp.max(s, axis=0, keepdims=True)) * (scale * LOG2E))
        p = p * (1.0 / jnp.sum(p, axis=0, keepdims=True))
        ds = p * ((dp - jnp.sum(p * dp, axis=0, keepdims=True)) * scale)
        return p.astype(BF16), ds.astype(BF16)

    def products(c, pb, ds):
        at = slice(c * pair, (c + 1) * pair)
        dkv[at, :width] = mm(ds, head_blocks(q[c * CL : (c + 1) * CL])).astype(BF16)
        dkv[at, width:] = mm(pb, head_blocks(g[c * CL : (c + 1) * CL])).astype(BF16)
        pt = pb.T
        for h in range(heads):
            cols = slice(h * HSIZE, (h + 1) * HSIZE)
            cross[c * CL : (c + 1) * CL, cols] = mm(
                pt[h * CL : (h + 1) * CL], ckv[at, width + h * HSIZE : width + (h + 1) * HSIZE]
            )

    def back(c):
        at = slice(c * pair, (c + 1) * pair)
        sent[2 * c : 2 * c + 2] = mm(dkv[at], kv_t[...]).astype(BF16).reshape(2, NL, -1)

    def send(low, high):
        for i, t in places:
            n = table[2 * i + t]

            @pl.when((n >= low) & (n < high))
            def _():
                outs[i][t] = sent[n]

    project(0)
    ahead = [scores(c) for c in range(spans // 2)]
    project(1)
    for c in range(spans):
        soft = soften(*ahead[c])
        if c + spans // 2 < spans:
            ahead.append(scores(c + spans // 2))
        if c >= 1:
            back(c - 1)
        products(c, *soft)
    send(0, n_named - 2)
    back(spans - 1)
    send(n_named - 2, n_named)


def shift(n, by):
    return [(i, (i + by) % n) for i in range(n)]


def local(
    self_q,
    self_k,
    self_v,
    cross_q,
    cross_k_weight,
    cross_v_weight,
    span_ctx,
    neighbours,
    neighbour_ids,
    enc_q,
    enc_k,
    enc_v,
    enc_o,
    mixed_grad,
):
    rows, width = self_q.shape
    slots, nl, ew = neighbours.shape
    spans, per_span = neighbour_ids.shape
    n_named = spans * per_span
    struct = jax.ShapeDtypeStruct
    after = lax.optimization_barrier

    ids = neighbour_ids.T

    e00, wt, ek, ev = call(
        encode_kernel,
        mib=56,
        out_shape=[
            struct((slots, nl, ew), BF16),
            struct((slots, EHEADS * CL, nl), F32),
            struct((slots, CL, ew), BF16),
            struct((slots, CL, ew), BF16),
        ],
        in_specs=[smem()] + [hbm()] * 6,
        out_specs=[vmem()] * 4,
        scratch_shapes=[pltpu.VMEM(neighbours.shape, BF16), pltpu.VMEM(span_ctx.shape, BF16)]
        + [pltpu.VMEM((ew, ew), BF16)] * 4
        + [pltpu.SemaphoreType.DMA((9,))],
    )(ids, neighbours, span_ctx, enc_q, enc_k, enc_v, enc_o)

    e01 = lax.ppermute(e00, "yh", shift(2, 1))
    e30 = lax.ppermute(e00, "z", shift(NX, 1))
    e10 = lax.ppermute(e00, "z", shift(NX, -1))

    self_q, self_k, self_v, _ = after((self_q, self_k, self_v, wt))
    packed = call(
        pack_kernel,
        out_shape=struct((NX, 3, rows, HSIZE), BF16),
        in_specs=[vmem()] * 3,
        out_specs=vmem(),
    )(self_q, self_k, self_v)
    pieces = lax.all_to_all(packed, "x", 0, 0)

    e01, e30, e10, packed = after((e01, e30, e10, packed))
    e11 = lax.ppermute(e01, "z", shift(NX, -1))
    e31 = lax.ppermute(e01, "z", shift(NX, 1))


    weights = after((enc_q, enc_o, e01))[:2]
    turned = call(
        turn_kernel,
        out_shape=[struct((ew, ew), BF16)] * 2,
        in_specs=[vmem()] * 2,
        out_specs=[vmem()] * 2,
    )(*weights)

    own_kv = pieces[:, 1:]
    e30, e11, e31, own_kv, *turned = after((e30, e11, e31, own_kv, *turned))
    swap = [(0, 3), (1, 2), (2, 1), (3, 0)]
    kvs = [
        own_kv,
        lax.ppermute(own_kv, "core", shift(2, 1)),
        lax.ppermute(own_kv, "yl", shift(2, 1)),
        lax.ppermute(own_kv, ("yl", "core"), swap),
    ]
    wq_t, wo_t = turned
    e20 = lax.ppermute(e30, "z", shift(NX, 1))
    e21 = lax.ppermute(e11, "z", shift(NX, -1))

    given = after((cross_k_weight, cross_v_weight, cross_q, mixed_grad, e11))[:4]
    kvw, kv_t, qm_t, gm_t = call(
        blocks_kernel,
        out_shape=[struct((ew, 2 * width), BF16), struct((2 * width, ew), BF16)]
        + [struct((spans, width, width // HSIZE * CL), BF16)] * 2,
        in_specs=[vmem()] * 4,
        out_specs=[vmem()] * 4,
    )(*given)

    cross, *p = call(
        cross_kernel,
        out_shape=[struct((rows, width), F32)] + [struct((slots, nl, ew), BF16)] * 8,
        in_specs=[smem()] + [vmem()] * 14,
        out_specs=[vmem()] * 9,
        scratch_shapes=[
            pltpu.SMEM((16,), jnp.int32),
            pltpu.VMEM((n_named, nl, ew), BF16),
            pltpu.VMEM((n_named, nl, ew), BF16),
            pltpu.VMEM((n_named * nl, 2 * width), BF16),
            pltpu.VMEM((n_named * nl, 2 * width), BF16),
        ],
    )(
        ids,
        e00,
        e01,
        e10,
        e11,
        e20,
        e21,
        e30,
        e31,
        kvw,
        qm_t,
        gm_t,
        cross_q,
        mixed_grad,
        kv_t,
    )
    p00, p01, p10, p11, p20, p21, p30, p31 = p

    def add(a, b):
        return (a.astype(F32) + b.astype(F32)).astype(BF16)

    far1 = lax.ppermute(p21, "z", shift(NX, -1))
    far0 = lax.ppermute(p20, "z", shift(NX, 1))
    *kvs, _ = after((*kvs, cross))
    outs = call(
        attend_kernel,
        out_shape=[struct((rows, HSIZE), BF16)] * NX,
        in_specs=[vmem()] * 5,
        out_specs=[vmem()] * NX,
        scratch_shapes=[
            pltpu.VMEM((rows, 2 * HSIZE), F32),
            pltpu.VMEM((rows, 1), F32),
        ],
    )(pieces, *kvs)
    far1, far0, p11, *outs = after((far1, far0, p11, *outs))
    selfs = [outs[0]] + [lax.ppermute(outs[d], "x", shift(NX, -d)) for d in range(1, NX)]
    down1 = lax.ppermute(add(p31, far1), "z", shift(NX, -1))
    up1 = lax.ppermute(p11, "z", shift(NX, 1))
    near0 = add(p10, far0)
    down1, up1, near0, p30, *selfs = after((down1, up1, near0, p30, *selfs))
    theirs = (p01.astype(F32) + up1.astype(F32) + down1.astype(F32)).astype(BF16)
    other = lax.ppermute(theirs, "yh", shift(2, 1))
    up0 = lax.ppermute(near0, "z", shift(NX, 1))
    down0 = lax.ppermute(p30, "z", shift(NX, -1))

    grad = call(
        pullback_kernel,
        out_shape=struct((slots, nl, ew), F32),
        in_specs=[vmem()] * 9,
        out_specs=vmem(),
    )(p00, up0, down0, other, wo_t, ev, wt, ek, wq_t)

    mixed = call(
        mix_kernel,
        out_shape=struct((rows, width), BF16),
        in_specs=[vmem()] * 5,
        out_specs=vmem(),
    )(*selfs, cross)
    return mixed, grad


def solution(mesh):
    fine = Mesh(mesh.devices.reshape(4, 2, 2, 4, 2), ("x", "yl", "core", "z", "yh"))
    ctx, enc = ("x", "yl", "core"), ("z", "yh")
    tokens = P(ctx, enc)
    return jax.shard_map(
        local,
        mesh=fine,
        in_specs=(
            tokens,
            tokens,
            tokens,
            tokens,
            P(None, enc),
            P(None, enc),
            P(ctx, None),
            P(ctx + enc, None, None),
            P(ctx, None),
            P(),
            P(),
            P(),
            P(),
            tokens,
        ),
        out_specs=(tokens, P(ctx + enc, None, None)),
        check_vma=False,
    )
```

```python
import math

import jax
import jax.numpy as jnp
from jax import lax
from jax.experimental import pallas as pl
from jax.experimental.pallas import tpu as pltpu
from jax.sharding import Mesh
from jax.sharding import PartitionSpec as P

HSIZE = 128
EHEADS = 4
CL = 64
NL = 128
NX = 4
LOG2E = math.log2(math.e)
BF16 = jnp.bfloat16
F32 = jnp.float32

NT = (((1,), (1,)), ((), ()))
TN = (((0,), (0,)), ((), ()))


def mm(a, b):
    return jnp.dot(a, b, preferred_element_type=F32)


def mm_nt(a, b):
    return lax.dot_general(a, b, NT, preferred_element_type=F32)


def mm_tn(a, b):
    return lax.dot_general(a, b, TN, preferred_element_type=F32)


def call(kernel, mib=24, **kw):
    return pl.pallas_call(
        kernel,
        compiler_params=pltpu.CompilerParams(vmem_limit_bytes=mib * 1024 * 1024),
        **kw,
    )


def smem():
    return pl.BlockSpec(memory_space=pltpu.SMEM)


def vmem():
    return pl.BlockSpec(memory_space=pltpu.VMEM)


def hbm():
    return pl.BlockSpec(memory_space=pltpu.HBM)


def pack_kernel(q_ref, k_ref, v_ref, out):
    for h in range(NX):
        cols = slice(h * HSIZE, (h + 1) * HSIZE)
        for i, src in enumerate((q_ref, k_ref, v_ref)):
            out[h, i] = src[:, cols]


def attend_kernel(pieces, kv0, kv1, kv2, kv3, o0, o1, o2, o3, acc, top):
    kv = (kv0, kv1, kv2, kv3)
    x = lax.axis_index("x")
    r = lax.axis_index("yl") * 2 + lax.axis_index("core")
    scale = LOG2E / math.sqrt(HSIZE)
    rows = pieces.shape[2]
    ones = jnp.ones((rows, HSIZE), BF16)
    for xq in range(NX):
        q = pieces[xq, 0]

        def group(xk):
            scores = [mm_nt(q, kv[i][xk, 0]) for i in range(4)]
            if xk == xq:
                at = lax.broadcasted_iota(jnp.int32, (rows, rows), 1)
                upto = lax.broadcasted_iota(jnp.int32, (rows, rows), 0)
                scores = [
                    jnp.where(at + jnp.bitwise_xor(r, i) * rows <= upto + r * rows, s, -1e30)
                    for i, s in enumerate(scores)
                ]
            best = jnp.maximum(
                jnp.maximum(scores[0], scores[1]), jnp.maximum(scores[2], scores[3])
            )
            new = jnp.max(best, axis=-1, keepdims=True)
            if xk > 0:
                old = top[...]
                new = jnp.maximum(old, new)
            out = None
            for i, s in enumerate(scores):
                weights = jnp.exp2((s - new) * scale).astype(BF16)
                term = mm(weights, jnp.concatenate([kv[i][xk, 1], ones], axis=1))
                out = term if out is None else out + term
            if xk > 0:
                out = acc[...] * jnp.exp2((old - new) * scale) + out
            acc[...] = out
            top[...] = new

        for xk in range(xq + 1):
            group(xk)
        total = acc[...]
        result = (total[:, :HSIZE] / total[:, HSIZE:]).astype(BF16)
        for d, out in enumerate((o0, o1, o2, o3)):

            @pl.when(lax.rem(xq + d, NX) == x)
            def _():
                out[...] = result


def mix_kernel(s0, s1, s2, s3, cross, out):
    x = lax.axis_index("x")
    for d, piece in enumerate((s0, s1, s2, s3)):
        cols = pl.ds(pl.multiple_of(lax.rem(x + d, NX) * HSIZE, HSIZE), HSIZE)
        out[:, cols] = (piece[...].astype(F32) + cross[:, cols]).astype(BF16)


def head_rows(rows):
    width = rows.shape[1]
    each = width // EHEADS
    at = lax.broadcasted_iota(jnp.int32, (1, width), 1)
    parts = []
    for h in range(EHEADS):
        keep = jnp.where((at >= h * each) & (at < (h + 1) * each), 1.0, 0.0).astype(BF16)
        parts.append(rows * keep)
    return jnp.concatenate(parts, axis=0)


def encode_kernel(
    ids, nb_h, ctx_h, wq_h, wk_h, wv_h, wo_h, enc, wt, ek_out, ev_out, *scratch
):
    nb, ctx, wq, wk, wv, wo, sems = scratch
    slots, rows, width = nb.shape
    each = width // EHEADS
    both = [(nb_h, nb)]
    for i in range(EHEADS):
        part = slice(i * each, (i + 1) * each)
        both.append((wq_h.at[part], wq.at[part]))
    both += [(ctx_h, ctx), (wk_h, wk), (wv_h, wv), (wo_h, wo)]
    copies = [pltpu.make_async_copy(a, b, sems.at[i]) for i, (a, b) in enumerate(both)]
    for c in copies:
        c.start()
    for c in copies[:5]:
        c.wait()
    x = nb[...].reshape(slots * rows, width)
    eq = mm(x, wq[...]).astype(BF16)
    copies[5].wait()
    contexts = []
    for t in range(slots):
        mine = (lax.axis_index("z") * 2 + lax.axis_index("yh")) * slots + t
        span = jnp.int32(0)
        for c in range(1, ids.shape[1]):
            span = jnp.where((ids[0, c] == mine) | (ids[1, c] == mine), c, span)
        contexts.append(ctx[pl.ds(pl.multiple_of(span * CL, CL), CL), :])
    m = jnp.concatenate(contexts, axis=0)
    copies[6].wait()
    ek = mm(m, wk[...]).astype(BF16)
    scores = [
        mm_nt(head_rows(ek[t * CL : (t + 1) * CL]), eq[t * rows : (t + 1) * rows])
        for t in range(slots)
    ]
    copies[7].wait()
    ev = mm(m, wv[...]).astype(BF16)
    copies[8].wait()
    probs = []
    for s in scores:
        s = (s * (1.0 / math.sqrt(each))).reshape(EHEADS, CL, rows)
        p = jnp.exp(s - jnp.max(s, axis=1, keepdims=True))
        probs.append((p * (1.0 / jnp.sum(p, axis=1, keepdims=True))).reshape(EHEADS * CL, rows))
    mixed = []
    for t, w in enumerate(probs):
        ev_t = ev[t * CL : (t + 1) * CL]
        mixed.append(mm_tn(w.astype(BF16), head_rows(ev_t)).astype(BF16))
        wt[t] = w
        ek_out[t] = ek[t * CL : (t + 1) * CL]
        ev_out[t] = ev_t
    out = x.astype(F32) + mm(jnp.concatenate(mixed, axis=0), wo[...])
    enc[...] = out.astype(BF16).reshape(slots, rows, width)


def pullback_kernel(d0, d1, d2, d3, wo, ev, wt, ek, wq, out):
    slots, rows, width = d0.shape
    each = width // EHEADS
    d = (d0[...].astype(F32) + d1[...].astype(F32)) + (d2[...].astype(F32) + d3[...].astype(F32))
    d = d.reshape(slots * rows, width)
    de = mm(d.astype(BF16), wo[...]).astype(BF16)
    turned = [
        mm_nt(head_rows(ev[t]), de[t * rows : (t + 1) * rows]) for t in range(slots)
    ]
    inner = []
    for t, dw in enumerate(turned):
        dw = dw.astype(BF16).astype(F32).reshape(EHEADS, CL, rows)
        w = wt[t].reshape(EHEADS, CL, rows)
        ds = w * (dw - jnp.sum(w * dw, axis=1, keepdims=True)) * (1.0 / math.sqrt(each))
        inner.append(ds.reshape(EHEADS * CL, rows).astype(BF16))
    back = [mm_tn(ds, head_rows(ek[t])).astype(BF16) for t, ds in enumerate(inner)]
    out[...] = (d + mm(jnp.concatenate(back, axis=0), wq[...])).reshape(slots, rows, width)


def turn_kernel(wq, wo, wq_t, wo_t):
    wq_t[...] = wq[...].T
    wo_t[...] = wo[...].T


def blocks_kernel(kw, vw, q, g, kvw, kv_t, qm_t, gm_t):
    width = kw.shape[1]
    kvw[:, :width] = kw[...]
    kvw[:, width:] = vw[...]
    kv_t[:width] = kw[...].T
    kv_t[width:] = vw[...].T
    for c in range(qm_t.shape[0]):
        qm_t[c] = head_blocks(q[c * CL : (c + 1) * CL]).T
        gm_t[c] = head_blocks(g[c * CL : (c + 1) * CL]).T


def head_blocks(rows):
    width = rows.shape[1]
    at = lax.broadcasted_iota(jnp.int32, (1, width), 1)
    parts = []
    for h in range(width // HSIZE):
        keep = jnp.where((at >= h * HSIZE) & (at < (h + 1) * HSIZE), 1.0, 0.0).astype(BF16)
        parts.append(rows * keep)
    return jnp.concatenate(parts, axis=0)


def cross_kernel(ids, e00, e01, e10, e11, e21, e30, up, *rest):
    slots = e00.shape[0]
    blocks = (e00, e01, e10, e11, up.at[slots:], e21, e30, up.at[:slots])
    kvw, qm_t, gm_t, q, g, kv_t, cross = rest[:7]
    p00, p01, p10, far, p21, p30, p31 = rest[7:14]
    outs = (p00, p01, p10, far.at[slots:], far.at[:slots], p21, p30, p31)
    table, held, sent, ckv, dkv = rest[14:]
    width = q.shape[1]
    z, yh = lax.axis_index("z"), lax.axis_index("yh")
    n_named = held.shape[0]
    spans = n_named // 2
    scale = 1.0 / math.sqrt(HSIZE)

    for i in range(16):
        table[i] = jnp.int32(-1)
    for n in range(n_named):
        slot = ids[n % 2, n // 2]
        dz = lax.rem(slot // 4 - z + NX, NX)
        dy = jnp.bitwise_xor(lax.rem(slot // 2, 2), yh)
        table[dz * 4 + dy * 2 + lax.rem(slot, 2)] = jnp.int32(n)
    places = [(i, t) for i in range(8) for t in range(2)]
    for i, t in places:
        n = table[2 * i + t]

        @pl.when(n >= 0)
        def _():
            held[n] = blocks[i][t]

        @pl.when(n < 0)
        def _():
            outs[i][t] = jnp.zeros((NL, e00.shape[2]), BF16)

    heads = width // HSIZE
    pair = 2 * NL

    def project(half):
        first = half * (n_named // 2)
        e = held[first : first + n_named // 2].reshape(n_named // 2 * NL, -1)
        ckv[first * NL : (first + n_named // 2) * NL] = mm(e, kvw[...]).astype(BF16)

    def scores(c):
        at = slice(c * pair, (c + 1) * pair)
        return mm(ckv[at, :width], qm_t[c]), mm(ckv[at, width:], gm_t[c])

    def soften(s, dp):
        p = jnp.exp2((s - jnp.max(s, axis=0, keepdims=True)) * (scale * LOG2E))
        p = p * (1.0 / jnp.sum(p, axis=0, keepdims=True))
        ds = p * ((dp - jnp.sum(p * dp, axis=0, keepdims=True)) * scale)
        return p.astype(BF16), ds.astype(BF16)

    def products(c, pb, ds):
        at = slice(c * pair, (c + 1) * pair)
        dkv[at, :width] = mm(ds, head_blocks(q[c * CL : (c + 1) * CL])).astype(BF16)
        dkv[at, width:] = mm(pb, head_blocks(g[c * CL : (c + 1) * CL])).astype(BF16)
        pt = pb.T
        for h in range(heads):
            cols = slice(h * HSIZE, (h + 1) * HSIZE)
            cross[c * CL : (c + 1) * CL, cols] = mm(
                pt[h * CL : (h + 1) * CL], ckv[at, width + h * HSIZE : width + (h + 1) * HSIZE]
            )

    def back(c):
        at = slice(c * pair, (c + 1) * pair)
        sent[2 * c : 2 * c + 2] = mm(dkv[at], kv_t[...]).astype(BF16).reshape(2, NL, -1)

    def send(low, high):
        for i, t in places:
            n = table[2 * i + t]

            @pl.when((n >= low) & (n < high))
            def _():
                outs[i][t] = sent[n]

    project(0)
    ahead = [scores(c) for c in range(spans // 2)]
    project(1)
    for c in range(spans):
        soft = soften(*ahead[c])
        if c + spans // 2 < spans:
            ahead.append(scores(c + spans // 2))
        if c >= 1:
            back(c - 1)
        products(c, *soft)
    send(0, n_named - 2)
    back(spans - 1)
    send(n_named - 2, n_named)


def shift(n, by):
    return [(i, (i + by) % n) for i in range(n)]


def local(
    self_q,
    self_k,
    self_v,
    cross_q,
    cross_k_weight,
    cross_v_weight,
    span_ctx,
    neighbours,
    neighbour_ids,
    enc_q,
    enc_k,
    enc_v,
    enc_o,
    mixed_grad,
):
    rows, width = self_q.shape
    slots, nl, ew = neighbours.shape
    spans, per_span = neighbour_ids.shape
    n_named = spans * per_span
    struct = jax.ShapeDtypeStruct
    after = lax.optimization_barrier

    ids = neighbour_ids.T

    e00, wt, ek, ev = call(
        encode_kernel,
        mib=56,
        out_shape=[
            struct((slots, nl, ew), BF16),
            struct((slots, EHEADS * CL, nl), F32),
            struct((slots, CL, ew), BF16),
            struct((slots, CL, ew), BF16),
        ],
        in_specs=[smem()] + [hbm()] * 6,
        out_specs=[vmem()] * 4,
        scratch_shapes=[pltpu.VMEM(neighbours.shape, BF16), pltpu.VMEM(span_ctx.shape, BF16)]
        + [pltpu.VMEM((ew, ew), BF16)] * 4
        + [pltpu.SemaphoreType.DMA((9,))],
    )(ids, neighbours, span_ctx, enc_q, enc_k, enc_v, enc_o)

    e01 = lax.ppermute(e00, "yh", shift(2, 1))
    e30 = lax.ppermute(e00, "z", shift(NX, 1))
    e10 = lax.ppermute(e00, "z", shift(NX, -1))

    self_q, self_k, self_v, _ = after((self_q, self_k, self_v, wt))
    packed = call(
        pack_kernel,
        out_shape=struct((NX, 3, rows, HSIZE), BF16),
        in_specs=[vmem()] * 3,
        out_specs=vmem(),
    )(self_q, self_k, self_v)
    pieces = lax.all_to_all(packed, "x", 0, 0)

    e01, e30, e10, packed = after((e01, e30, e10, packed))
    e11 = lax.ppermute(e01, "z", shift(NX, -1))
    up = lax.ppermute(jnp.concatenate([e01, e30]), "z", shift(NX, 1))


    weights = after((enc_q, enc_o, e01))[:2]
    turned = call(
        turn_kernel,
        out_shape=[struct((ew, ew), BF16)] * 2,
        in_specs=[vmem()] * 2,
        out_specs=[vmem()] * 2,
    )(*weights)

    own_kv = pieces[:, 1:]
    e11, own_kv, *turned = after((e11, own_kv, *turned))
    swap = [(0, 3), (1, 2), (2, 1), (3, 0)]
    kvs = [
        own_kv,
        lax.ppermute(own_kv, "core", shift(2, 1)),
        lax.ppermute(own_kv, "yl", shift(2, 1)),
        lax.ppermute(own_kv, ("yl", "core"), swap),
    ]
    wq_t, wo_t = turned
    e21 = lax.ppermute(e11, "z", shift(NX, -1))

    given = after((cross_k_weight, cross_v_weight, cross_q, mixed_grad, e11))[:4]
    kvw, kv_t, qm_t, gm_t = call(
        blocks_kernel,
        out_shape=[struct((ew, 2 * width), BF16), struct((2 * width, ew), BF16)]
        + [struct((spans, width, width // HSIZE * CL), BF16)] * 2,
        in_specs=[vmem()] * 4,
        out_specs=[vmem()] * 4,
    )(*given)

    cross, *p = call(
        cross_kernel,
        out_shape=[struct((rows, width), F32)]
        + [struct((k * slots, nl, ew), BF16) for k in (1, 1, 1, 2, 1, 1, 1)],
        in_specs=[smem()] + [vmem()] * 13,
        out_specs=[vmem()] * 8,
        scratch_shapes=[
            pltpu.SMEM((16,), jnp.int32),
            pltpu.VMEM((n_named, nl, ew), BF16),
            pltpu.VMEM((n_named, nl, ew), BF16),
            pltpu.VMEM((n_named * nl, 2 * width), BF16),
            pltpu.VMEM((n_named * nl, 2 * width), BF16),
        ],
    )(
        ids,
        e00,
        e01,
        e10,
        e11,
        e21,
        e30,
        up,
        kvw,
        qm_t,
        gm_t,
        cross_q,
        mixed_grad,
        kv_t,
    )
    p00, p01, p10, far, p21, p30, p31 = p

    def add(a, b):
        return (a.astype(F32) + b.astype(F32)).astype(BF16)

    far1 = lax.ppermute(p21, "z", shift(NX, -1))
    far = lax.ppermute(far, "z", shift(NX, 1))
    *kvs, _ = after((*kvs, cross))
    outs = call(
        attend_kernel,
        out_shape=[struct((rows, HSIZE), BF16)] * NX,
        in_specs=[vmem()] * 5,
        out_specs=[vmem()] * NX,
        scratch_shapes=[
            pltpu.VMEM((rows, 2 * HSIZE), F32),
            pltpu.VMEM((rows, 1), F32),
        ],
    )(pieces, *kvs)
    far1, *outs = after((far1, *outs))
    selfs = [outs[0]] + [lax.ppermute(outs[d], "x", shift(NX, -d)) for d in range(1, NX)]
    down1 = lax.ppermute(add(p31, far1), "z", shift(NX, -1))
    down1, far, p30, *selfs = after((down1, far, p30, *selfs))
    near0, up1 = add(p10, far[:slots]), far[slots:]
    theirs = (p01.astype(F32) + up1.astype(F32) + down1.astype(F32)).astype(BF16)
    other = lax.ppermute(theirs, "yh", shift(2, 1))
    up0 = lax.ppermute(near0, "z", shift(NX, 1))
    down0 = lax.ppermute(p30, "z", shift(NX, -1))

    grad = call(
        pullback_kernel,
        out_shape=struct((slots, nl, ew), F32),
        in_specs=[vmem()] * 9,
        out_specs=vmem(),
    )(p00, up0, down0, other, wo_t, ev, wt, ek, wq_t)

    mixed = call(
        mix_kernel,
        out_shape=struct((rows, width), BF16),
        in_specs=[vmem()] * 5,
        out_specs=vmem(),
    )(*selfs, cross)
    return mixed, grad


def solution(mesh):
    fine = Mesh(mesh.devices.reshape(4, 2, 2, 4, 2), ("x", "yl", "core", "z", "yh"))
    ctx, enc = ("x", "yl", "core"), ("z", "yh")
    tokens = P(ctx, enc)
    return jax.shard_map(
        local,
        mesh=fine,
        in_specs=(
            tokens,
            tokens,
            tokens,
            tokens,
            P(None, enc),
            P(None, enc),
            P(ctx, None),
            P(ctx + enc, None, None),
            P(ctx, None),
            P(),
            P(),
            P(),
            P(),
            tokens,
        ),
        out_specs=(tokens, P(ctx + enc, None, None)),
        check_vma=False,
    )
```

```python
import math

import jax
import jax.numpy as jnp
from jax import lax
from jax.experimental import pallas as pl
from jax.experimental.pallas import tpu as pltpu
from jax.sharding import Mesh
from jax.sharding import PartitionSpec as P

HSIZE = 128
EHEADS = 4
CL = 64
NL = 128
NX = 4
LOG2E = math.log2(math.e)
BF16 = jnp.bfloat16
F32 = jnp.float32

NT = (((1,), (1,)), ((), ()))
TN = (((0,), (0,)), ((), ()))


def mm(a, b):
    return jnp.dot(a, b, preferred_element_type=F32)


def mm_nt(a, b):
    return lax.dot_general(a, b, NT, preferred_element_type=F32)


def mm_tn(a, b):
    return lax.dot_general(a, b, TN, preferred_element_type=F32)


def call(kernel, mib=24, **kw):
    return pl.pallas_call(
        kernel,
        compiler_params=pltpu.CompilerParams(vmem_limit_bytes=mib * 1024 * 1024),
        **kw,
    )


def smem():
    return pl.BlockSpec(memory_space=pltpu.SMEM)


def vmem():
    return pl.BlockSpec(memory_space=pltpu.VMEM)


def hbm():
    return pl.BlockSpec(memory_space=pltpu.HBM)


def pack_kernel(q_ref, k_ref, v_ref, out):
    for h in range(NX):
        cols = slice(h * HSIZE, (h + 1) * HSIZE)
        for i, src in enumerate((q_ref, k_ref, v_ref)):
            out[h, i] = src[:, cols]


def attend_kernel(pieces, kv0, kv1, kv2, kv3, o0, o1, o2, o3, acc, top):
    kv = (kv0, kv1, kv2, kv3)
    x = lax.axis_index("x")
    r = lax.axis_index("yl") * 2 + lax.axis_index("core")
    scale = LOG2E / math.sqrt(HSIZE)
    rows = pieces.shape[2]
    ones = jnp.ones((rows, HSIZE), BF16)
    for xq in range(NX):
        q = pieces[xq, 0]

        def group(xk):
            scores = [mm_nt(q, kv[i][xk, 0]) for i in range(4)]
            if xk == xq:
                at = lax.broadcasted_iota(jnp.int32, (rows, rows), 1)
                upto = lax.broadcasted_iota(jnp.int32, (rows, rows), 0)
                scores = [
                    jnp.where(at + jnp.bitwise_xor(r, i) * rows <= upto + r * rows, s, -1e30)
                    for i, s in enumerate(scores)
                ]
            best = jnp.maximum(
                jnp.maximum(scores[0], scores[1]), jnp.maximum(scores[2], scores[3])
            )
            new = jnp.max(best, axis=-1, keepdims=True)
            if xk > 0:
                old = top[...]
                new = jnp.maximum(old, new)
            out = None
            for i, s in enumerate(scores):
                weights = jnp.exp2((s - new) * scale).astype(BF16)
                term = mm(weights, jnp.concatenate([kv[i][xk, 1], ones], axis=1))
                out = term if out is None else out + term
            if xk > 0:
                out = acc[...] * jnp.exp2((old - new) * scale) + out
            acc[...] = out
            top[...] = new

        for xk in range(xq + 1):
            group(xk)
        total = acc[...]
        result = (total[:, :HSIZE] / total[:, HSIZE:]).astype(BF16)
        for d, out in enumerate((o0, o1, o2, o3)):

            @pl.when(lax.rem(xq + d, NX) == x)
            def _():
                out[...] = result


def mix_kernel(s0, s1, s2, s3, cross, out):
    x = lax.axis_index("x")
    for d, piece in enumerate((s0, s1, s2, s3)):
        cols = pl.ds(pl.multiple_of(lax.rem(x + d, NX) * HSIZE, HSIZE), HSIZE)
        out[:, cols] = (piece[...].astype(F32) + cross[:, cols]).astype(BF16)


def head_rows(rows):
    width = rows.shape[1]
    each = width // EHEADS
    at = lax.broadcasted_iota(jnp.int32, (1, width), 1)
    parts = []
    for h in range(EHEADS):
        keep = jnp.where((at >= h * each) & (at < (h + 1) * each), 1.0, 0.0).astype(BF16)
        parts.append(rows * keep)
    return jnp.concatenate(parts, axis=0)


def encode_kernel(
    ids, nb_h, ctx_h, wq_h, wk_h, wv_h, wo_h, enc, wt, ek_out, ev_out, *scratch
):
    nb, ctx, wq, wk, wv, wo, sems = scratch
    slots, rows, width = nb.shape
    each = width // EHEADS
    both = [(nb_h, nb)]
    for i in range(EHEADS):
        part = slice(i * each, (i + 1) * each)
        both.append((wq_h.at[part], wq.at[part]))
    both += [(ctx_h, ctx), (wk_h, wk), (wv_h, wv), (wo_h, wo)]
    copies = [pltpu.make_async_copy(a, b, sems.at[i]) for i, (a, b) in enumerate(both)]
    for c in copies:
        c.start()
    for c in copies[:5]:
        c.wait()
    x = nb[...].reshape(slots * rows, width)
    eq = mm(x, wq[...]).astype(BF16)
    copies[5].wait()
    contexts = []
    for t in range(slots):
        mine = (lax.axis_index("z") * 2 + lax.axis_index("yh")) * slots + t
        span = jnp.int32(0)
        for c in range(1, ids.shape[1]):
            span = jnp.where((ids[0, c] == mine) | (ids[1, c] == mine), c, span)
        contexts.append(ctx[pl.ds(pl.multiple_of(span * CL, CL), CL), :])
    m = jnp.concatenate(contexts, axis=0)
    copies[6].wait()
    ek = mm(m, wk[...]).astype(BF16)
    scores = [
        mm_nt(head_rows(ek[t * CL : (t + 1) * CL]), eq[t * rows : (t + 1) * rows])
        for t in range(slots)
    ]
    copies[7].wait()
    ev = mm(m, wv[...]).astype(BF16)
    copies[8].wait()
    probs = []
    for s in scores:
        s = (s * (1.0 / math.sqrt(each))).reshape(EHEADS, CL, rows)
        p = jnp.exp(s - jnp.max(s, axis=1, keepdims=True))
        probs.append((p * (1.0 / jnp.sum(p, axis=1, keepdims=True))).reshape(EHEADS * CL, rows))
    mixed = []
    for t, w in enumerate(probs):
        ev_t = ev[t * CL : (t + 1) * CL]
        mixed.append(mm_tn(w.astype(BF16), head_rows(ev_t)).astype(BF16))
        wt[t] = w
        ek_out[t] = ek[t * CL : (t + 1) * CL]
        ev_out[t] = ev_t
    out = x.astype(F32) + mm(jnp.concatenate(mixed, axis=0), wo[...])
    enc[...] = out.astype(BF16).reshape(slots, rows, width)


def pullback_kernel(d0, d1, d2, d3, wo, ev, wt, ek, wq, out):
    slots, rows, width = d0.shape
    each = width // EHEADS
    d = (d0[...].astype(F32) + d1[...].astype(F32)) + (d2[...].astype(F32) + d3[...].astype(F32))
    d = d.reshape(slots * rows, width)
    de = mm(d.astype(BF16), wo[...]).astype(BF16)
    turned = [
        mm_nt(head_rows(ev[t]), de[t * rows : (t + 1) * rows]) for t in range(slots)
    ]
    inner = []
    for t, dw in enumerate(turned):
        dw = dw.astype(BF16).astype(F32).reshape(EHEADS, CL, rows)
        w = wt[t].reshape(EHEADS, CL, rows)
        ds = w * (dw - jnp.sum(w * dw, axis=1, keepdims=True)) * (1.0 / math.sqrt(each))
        inner.append(ds.reshape(EHEADS * CL, rows).astype(BF16))
    back = [mm_tn(ds, head_rows(ek[t])).astype(BF16) for t, ds in enumerate(inner)]
    out[...] = (d + mm(jnp.concatenate(back, axis=0), wq[...])).reshape(slots, rows, width)


def join_kernel(first, second, out):
    slots = first.shape[0]
    out[:slots] = first[...]
    out[slots:] = second[...]


def turn_kernel(wq, wo, wq_t, wo_t):
    wq_t[...] = wq[...].T
    wo_t[...] = wo[...].T


def blocks_kernel(kw, vw, q, g, kvw, kv_t, qm_t, gm_t):
    width = kw.shape[1]
    kvw[:, :width] = kw[...]
    kvw[:, width:] = vw[...]
    kv_t[:width] = kw[...].T
    kv_t[width:] = vw[...].T
    for c in range(qm_t.shape[0]):
        qm_t[c] = head_blocks(q[c * CL : (c + 1) * CL]).T
        gm_t[c] = head_blocks(g[c * CL : (c + 1) * CL]).T


def head_blocks(rows):
    width = rows.shape[1]
    at = lax.broadcasted_iota(jnp.int32, (1, width), 1)
    parts = []
    for h in range(width // HSIZE):
        keep = jnp.where((at >= h * HSIZE) & (at < (h + 1) * HSIZE), 1.0, 0.0).astype(BF16)
        parts.append(rows * keep)
    return jnp.concatenate(parts, axis=0)


def cross_kernel(ids, e00, e01, e10, e11, e21, e30, up, *rest):
    slots = e00.shape[0]
    blocks = (e00, e01, e10, e11, up.at[slots:], e21, e30, up.at[:slots])
    kvw, qm_t, gm_t, q, g, kv_t, cross = rest[:7]
    p00, p01, p10, far, p21, p30, p31 = rest[7:14]
    outs = (p00, p01, p10, far.at[slots:], far.at[:slots], p21, p30, p31)
    table, held, sent, ckv, dkv = rest[14:]
    width = q.shape[1]
    z, yh = lax.axis_index("z"), lax.axis_index("yh")
    n_named = held.shape[0]
    spans = n_named // 2
    scale = 1.0 / math.sqrt(HSIZE)

    for i in range(16):
        table[i] = jnp.int32(-1)
    for n in range(n_named):
        slot = ids[n % 2, n // 2]
        dz = lax.rem(slot // 4 - z + NX, NX)
        dy = jnp.bitwise_xor(lax.rem(slot // 2, 2), yh)
        table[dz * 4 + dy * 2 + lax.rem(slot, 2)] = jnp.int32(n)
    places = [(i, t) for i in range(8) for t in range(2)]
    for i, t in places:
        n = table[2 * i + t]

        @pl.when(n >= 0)
        def _():
            held[n] = blocks[i][t]

        @pl.when(n < 0)
        def _():
            outs[i][t] = jnp.zeros((NL, e00.shape[2]), BF16)

    heads = width // HSIZE
    pair = 2 * NL

    def project(half):
        first = half * (n_named // 2)
        e = held[first : first + n_named // 2].reshape(n_named // 2 * NL, -1)
        ckv[first * NL : (first + n_named // 2) * NL] = mm(e, kvw[...]).astype(BF16)

    def scores(c):
        at = slice(c * pair, (c + 1) * pair)
        return mm(ckv[at, :width], qm_t[c]), mm(ckv[at, width:], gm_t[c])

    def soften(s, dp):
        p = jnp.exp2((s - jnp.max(s, axis=0, keepdims=True)) * (scale * LOG2E))
        p = p * (1.0 / jnp.sum(p, axis=0, keepdims=True))
        ds = p * ((dp - jnp.sum(p * dp, axis=0, keepdims=True)) * scale)
        return p.astype(BF16), ds.astype(BF16)

    def products(c, pb, ds):
        at = slice(c * pair, (c + 1) * pair)
        dkv[at, :width] = mm(ds, head_blocks(q[c * CL : (c + 1) * CL])).astype(BF16)
        dkv[at, width:] = mm(pb, head_blocks(g[c * CL : (c + 1) * CL])).astype(BF16)
        pt = pb.T
        for h in range(heads):
            cols = slice(h * HSIZE, (h + 1) * HSIZE)
            cross[c * CL : (c + 1) * CL, cols] = mm(
                pt[h * CL : (h + 1) * CL], ckv[at, width + h * HSIZE : width + (h + 1) * HSIZE]
            )

    def back(c):
        at = slice(c * pair, (c + 1) * pair)
        sent[2 * c : 2 * c + 2] = mm(dkv[at], kv_t[...]).astype(BF16).reshape(2, NL, -1)

    def send(low, high):
        for i, t in places:
            n = table[2 * i + t]

            @pl.when((n >= low) & (n < high))
            def _():
                outs[i][t] = sent[n]

    project(0)
    ahead = [scores(c) for c in range(spans // 2)]
    project(1)
    for c in range(spans):
        soft = soften(*ahead[c])
        if c + spans // 2 < spans:
            ahead.append(scores(c + spans // 2))
        if c >= 1:
            back(c - 1)
        products(c, *soft)
    send(0, n_named - 2)
    back(spans - 1)
    send(n_named - 2, n_named)


def shift(n, by):
    return [(i, (i + by) % n) for i in range(n)]


def local(
    self_q,
    self_k,
    self_v,
    cross_q,
    cross_k_weight,
    cross_v_weight,
    span_ctx,
    neighbours,
    neighbour_ids,
    enc_q,
    enc_k,
    enc_v,
    enc_o,
    mixed_grad,
):
    rows, width = self_q.shape
    slots, nl, ew = neighbours.shape
    spans, per_span = neighbour_ids.shape
    n_named = spans * per_span
    struct = jax.ShapeDtypeStruct
    after = lax.optimization_barrier

    ids = neighbour_ids.T

    e00, wt, ek, ev = call(
        encode_kernel,
        mib=56,
        out_shape=[
            struct((slots, nl, ew), BF16),
            struct((slots, EHEADS * CL, nl), F32),
            struct((slots, CL, ew), BF16),
            struct((slots, CL, ew), BF16),
        ],
        in_specs=[smem()] + [hbm()] * 6,
        out_specs=[vmem()] * 4,
        scratch_shapes=[pltpu.VMEM(neighbours.shape, BF16), pltpu.VMEM(span_ctx.shape, BF16)]
        + [pltpu.VMEM((ew, ew), BF16)] * 4
        + [pltpu.SemaphoreType.DMA((9,))],
    )(ids, neighbours, span_ctx, enc_q, enc_k, enc_v, enc_o)

    e01 = lax.ppermute(e00, "yh", shift(2, 1))
    e30 = lax.ppermute(e00, "z", shift(NX, 1))
    e10 = lax.ppermute(e00, "z", shift(NX, -1))

    self_q, self_k, self_v, _ = after((self_q, self_k, self_v, wt))
    packed = call(
        pack_kernel,
        out_shape=struct((NX, 3, rows, HSIZE), BF16),
        in_specs=[vmem()] * 3,
        out_specs=vmem(),
    )(self_q, self_k, self_v)
    pieces = lax.all_to_all(packed, "x", 0, 0)

    e01, e30, e10, packed = after((e01, e30, e10, packed))
    e11 = lax.ppermute(e01, "z", shift(NX, -1))
    joined = call(
        join_kernel,
        out_shape=struct((2 * slots, nl, ew), BF16),
        in_specs=[vmem()] * 2,
        out_specs=vmem(),
    )(e01, e30)
    up = lax.ppermute(joined, "z", shift(NX, 1))


    weights = after((enc_q, enc_o, e01))[:2]
    turned = call(
        turn_kernel,
        out_shape=[struct((ew, ew), BF16)] * 2,
        in_specs=[vmem()] * 2,
        out_specs=[vmem()] * 2,
    )(*weights)

    own_kv = pieces[:, 1:]
    e11, own_kv, *turned = after((e11, own_kv, *turned))
    swap = [(0, 3), (1, 2), (2, 1), (3, 0)]
    kvs = [
        own_kv,
        lax.ppermute(own_kv, "core", shift(2, 1)),
        lax.ppermute(own_kv, "yl", shift(2, 1)),
        lax.ppermute(own_kv, ("yl", "core"), swap),
    ]
    wq_t, wo_t = turned
    e21 = lax.ppermute(e11, "z", shift(NX, -1))

    given = after((cross_k_weight, cross_v_weight, cross_q, mixed_grad, e11))[:4]
    kvw, kv_t, qm_t, gm_t = call(
        blocks_kernel,
        out_shape=[struct((ew, 2 * width), BF16), struct((2 * width, ew), BF16)]
        + [struct((spans, width, width // HSIZE * CL), BF16)] * 2,
        in_specs=[vmem()] * 4,
        out_specs=[vmem()] * 4,
    )(*given)

    cross, *p = call(
        cross_kernel,
        out_shape=[struct((rows, width), F32)]
        + [struct((k * slots, nl, ew), BF16) for k in (1, 1, 1, 2, 1, 1, 1)],
        in_specs=[smem()] + [vmem()] * 13,
        out_specs=[vmem()] * 8,
        scratch_shapes=[
            pltpu.SMEM((16,), jnp.int32),
            pltpu.VMEM((n_named, nl, ew), BF16),
            pltpu.VMEM((n_named, nl, ew), BF16),
            pltpu.VMEM((n_named * nl, 2 * width), BF16),
            pltpu.VMEM((n_named * nl, 2 * width), BF16),
        ],
    )(
        ids,
        e00,
        e01,
        e10,
        e11,
        e21,
        e30,
        up,
        kvw,
        qm_t,
        gm_t,
        cross_q,
        mixed_grad,
        kv_t,
    )
    p00, p01, p10, far, p21, p30, p31 = p

    def add(a, b):
        return (a.astype(F32) + b.astype(F32)).astype(BF16)

    far1 = lax.ppermute(p21, "z", shift(NX, -1))
    far = lax.ppermute(far, "z", shift(NX, 1))
    *kvs, _ = after((*kvs, cross))
    outs = call(
        attend_kernel,
        out_shape=[struct((rows, HSIZE), BF16)] * NX,
        in_specs=[vmem()] * 5,
        out_specs=[vmem()] * NX,
        scratch_shapes=[
            pltpu.VMEM((rows, 2 * HSIZE), F32),
            pltpu.VMEM((rows, 1), F32),
        ],
    )(pieces, *kvs)
    far1, *outs = after((far1, *outs))
    selfs = [outs[0]] + [lax.ppermute(outs[d], "x", shift(NX, -d)) for d in range(1, NX)]
    down1 = lax.ppermute(add(p31, far1), "z", shift(NX, -1))
    down1, far, p30, *selfs = after((down1, far, p30, *selfs))
    near0, up1 = add(p10, far[:slots]), far[slots:]
    theirs = (p01.astype(F32) + up1.astype(F32) + down1.astype(F32)).astype(BF16)
    other = lax.ppermute(theirs, "yh", shift(2, 1))
    up0 = lax.ppermute(near0, "z", shift(NX, 1))
    down0 = lax.ppermute(p30, "z", shift(NX, -1))

    grad = call(
        pullback_kernel,
        out_shape=struct((slots, nl, ew), F32),
        in_specs=[vmem()] * 9,
        out_specs=vmem(),
    )(p00, up0, down0, other, wo_t, ev, wt, ek, wq_t)

    mixed = call(
        mix_kernel,
        out_shape=struct((rows, width), BF16),
        in_specs=[vmem()] * 5,
        out_specs=vmem(),
    )(*selfs, cross)
    return mixed, grad


def solution(mesh):
    fine = Mesh(mesh.devices.reshape(4, 2, 2, 4, 2), ("x", "yl", "core", "z", "yh"))
    ctx, enc = ("x", "yl", "core"), ("z", "yh")
    tokens = P(ctx, enc)
    return jax.shard_map(
        local,
        mesh=fine,
        in_specs=(
            tokens,
            tokens,
            tokens,
            tokens,
            P(None, enc),
            P(None, enc),
            P(ctx, None),
            P(ctx + enc, None, None),
            P(ctx, None),
            P(),
            P(),
            P(),
            P(),
            tokens,
        ),
        out_specs=(tokens, P(ctx + enc, None, None)),
        check_vma=False,
    )
```
